128 devices in a mesh: tm: 8 (over y, z_hi), space: 16 (over x, z_lo, core).
Axes of the slice: x: 4, y: 4, z: 4 (z_hi: 2, z_lo: 2; z = z_hi * 2 + z_lo), core: 2. Of those that a mesh axis runs over, the one named last changes fastest.
Arguments:
- state_old: float32 [8, 128, 64, 1024], P('tm', 'space'), may hold values from -6 to 6
- velocity: float32 [3, 128, 64, 1024], P(None, 'space'), may hold values from -0.12 to 0.12
- diffusivity: float32 [128, 64, 1024], P('space'), may hold values from 0.01 to 0.08
Outputs:
- new_state: float32 [8, 128, 64, 1024], P('tm', 'space')
The draws below stay inside these ranges and needn't reach their ends.
All inputs are finite; a program needn't handle non-finite values.
Results may differ from the reference program's by a relative error of at most 0.00012.
Values sent between devices are 32-bit elements; how exact they have to be, the bound alone decides.
No kernel may reach another device: no remote copies, remote signals or barrier semaphores. Data moves between devices by JAX's collectives and lax.ppermute only.
A program may use at most 128 MiB of HBM per device.

```python
import math
import jax
import jax.numpy as jnp

NY = 64
NX = 1024
NZ = 128
GROUPS = 8


def block_levels(stream_key, extent, split, low, high):
    gain = 1.0
    for dim, blocks in split:
        heights = jax.random.uniform(jax.random.fold_in(jax.random.fold_in(stream_key, 6), dim), (blocks,), jnp.float32, low / len(split), high / len(split))
        gain = gain * jnp.repeat(jnp.exp(heights), extent[dim] // blocks).reshape((-1,) + (1,) * (len(extent) - 1 - dim))
    return gain


def scatter_about(rng, dims, scale, reach, cuts=(), kind=jnp.bfloat16):
    gain = block_levels(rng, dims, cuts, -0.22, 0.18) if cuts else 1.0
    entries = jax.random.normal(rng, dims, jnp.float32) * scale * gain
    return jnp.minimum(jnp.maximum(entries, -reach), reach).astype(kind)


def setup_inputs(seed: int = 0) -> dict:
    splits = jax.random.split(jax.random.key(seed), 4)
    return {
        "state_old": scatter_about(splits[0], (GROUPS, NZ, NY, NX), 1.0, 6.0, ((0, 8), (1, 16)), jnp.float32),
        "velocity": jnp.clip(jax.random.uniform(splits[1], (3, NZ, NY, NX), jnp.float32, -0.12, 0.12) * block_levels(splits[1], (3, NZ, NY, NX), ((1, 16),), -0.4, 0.0), -0.12, 0.12),
        "diffusivity": jnp.clip(jnp.exp(math.log(0.08) - 2.0794415 * jax.random.uniform(splits[2], (NZ, NY, NX), jnp.float32) ** block_levels(splits[2], (NZ, NY, NX), ((0, 16),), -0.2, 0.2)), 0.01, 0.08),
    }


def restrict(field_now):
    halved_x = field_now[..., 0::2] + field_now[..., 1::2]
    halved_y = halved_x[..., 0::2, :] + halved_x[..., 1::2, :]
    halved_z = halved_y[..., 0::2, :, :] + halved_y[..., 1::2, :, :]
    return halved_z * 0.125


def prolong(coarse_field):
    return jnp.repeat(jnp.repeat(jnp.repeat(coarse_field, 2, -1), 2, -2), 2, -3)


def upwind(velocity_part, centre, behind, forward):
    return jnp.maximum(velocity_part, 0.0) * (centre - behind) + jnp.minimum(velocity_part, 0.0) * (forward - centre)


def advance(padded, velocity, diffusivity, spacing, time_step):
    centre = padded[1:-1]
    layer_above = padded[2:]
    layer_below = padded[:-2]
    east_cell = jnp.roll(centre, -1, 2)
    west_cell = jnp.roll(centre, 1, 2)
    north_cell = jnp.roll(centre, -1, 1)
    south_cell = jnp.roll(centre, 1, 1)
    spread = (east_cell + west_cell + north_cell + south_cell + layer_above + layer_below - 6.0 * centre) / (spacing * spacing)
    drift = upwind(velocity[0], centre, west_cell, east_cell) + upwind(velocity[1], centre, south_cell, north_cell) + upwind(velocity[2], centre, layer_below, layer_above)
    return centre + time_step * (diffusivity * spread - drift / spacing)


def pad_layers(field_now):
    return jnp.pad(field_now, ((1, 1), (0, 0), (0, 0)))


def reference(state_old, velocity, diffusivity):
    coarse_velocity = restrict(velocity)
    coarse_diffusivity = restrict(diffusivity)

    def fine_solve(field_now):
        for sweep_index in range(2):
            field_now = advance(pad_layers(field_now), velocity, diffusivity, 1.0, 1.0)
        return field_now

    def coarse(coarse_field):
        return advance(pad_layers(coarse_field), coarse_velocity, coarse_diffusivity, 2.0, 2.0)

    carried = restrict(state_old[0])
    results = []
    for slice_index in range(GROUPS):
        field_now = state_old[slice_index]
        defect = fine_solve(field_now) - prolong(coarse(restrict(field_now)))
        moved = coarse(carried)
        results.append(prolong(moved) + defect)
        carried = moved + restrict(defect)
    return jnp.stack(results)
```

```python
import functools

import jax
import jax.numpy as jnp
from jax import lax
from jax.experimental import pallas as pl
from jax.experimental.pallas import tpu as pltpu
from jax.sharding import Mesh
from jax.sharding import PartitionSpec as P

F32 = jnp.float32
BF16 = jnp.bfloat16
NY, NX = 64, 1024
LZ = 8
CX, CL = 512, 128
GROUPS = 8
QUAD = 4
BLOCKS = GROUPS * QUAD
XB = CX // BLOCKS
WIN = XB + 16
TOP = 8
PADDED = NY + 16
SPACE = ("px", "pz", "core")
GROUP = ("tm", "pz", "core")


def params(mib):
    return pltpu.CompilerParams(vmem_limit_bytes=mib * 1024 * 1024)


def split3(x):
    hi = x.astype(BF16)
    rest = x - hi.astype(F32)
    mid = rest.astype(BF16)
    return hi, mid, (rest - mid.astype(F32)).astype(BF16)


def dot(a, b, ca, cb):
    return lax.dot_general(a, b, (((ca,), (cb,)), ((), ())), preferred_element_type=F32)


def table(shape, test):
    rows = lax.broadcasted_iota(jnp.int32, shape, 0)
    cols = lax.broadcasted_iota(jnp.int32, shape, 1)
    return test(rows, cols).astype(F32).astype(BF16)


def restrict_block(part, pairs):
    halve = table((128, 256), lambda r, c: r == c // 2)
    t1 = sum(dot(halve, p, 1, 1) for p in split3(part))
    return sum(dot(p, pairs, 1, 0) for p in split3(t1)) * 0.125


def advanced(c, w, e, s, n, b, t, ax, ay, az, k):
    lap = ((w + e) + (s + n)) + ((b + t) - 6.0 * c)
    dx = jnp.abs(ax) * (jnp.where(ax > 0, w, e) - c)
    dy = jnp.abs(ay) * (jnp.where(ay > 0, s, n) - c)
    dz = jnp.abs(az) * (jnp.where(az > 0, b, t) - c)
    return (c + k * lap) + ((dx + dy) + dz)


def wrap_rows(ref, z):
    ref[z, TOP - 1 : TOP, :] = ref[z, TOP + NY - 1 : TOP + NY, :]
    ref[z, TOP + NY : TOP + NY + 1, :] = ref[z, TOP : TOP + 1, :]


def plane(ref, z, r):
    c = ref[z, TOP + r : TOP + r + 8, :]
    s = ref[z, TOP + r - 1 : TOP + r + 7, :]
    n = ref[z, TOP + r + 1 : TOP + r + 9, :]
    return c, pltpu.roll(c, 1, 1), pltpu.roll(c, NX - 1, 1), s, n


def coarse_coefs(vx, vy, vz, k):
    half = 0.5 * k
    out = []
    for a in (vx, vy, vz):
        out += [half + jnp.maximum(a, 0.0), half - jnp.minimum(a, 0.0)]
    return out


def y_rolled(u, width, axis):
    y = lax.broadcasted_iota(jnp.int32, u.shape, axis) % 32
    s = jnp.where(y == 0, pltpu.roll(u, width - 31, axis), pltpu.roll(u, 1, axis))
    n = jnp.where(y == 31, pltpu.roll(u, 31, axis), pltpu.roll(u, width - 1, axis))
    return s, n


def edges_kernel(slo, shi, vlo, vhi, dlo, dhi, lo, hi, pad, zsum):
    pad[0, TOP : TOP + NY, :] = slo[0]
    pad[1, TOP : TOP + NY, :] = shi[1]
    for side, (out, st, v, d, inner) in enumerate(((lo, slo, vlo, dlo, 1), (hi, shi, vhi, dhi, 0))):
        wrap_rows(pad, side)
        for r in range(0, NY, 8):
            rows = slice(r, r + 8)
            c, w, e, s, n = plane(pad, side, r)
            inside = st[inner, rows, :]
            ax, ay, az = v[0, 0, rows, :], v[1, 0, rows, :], v[2, 0, rows, :]
            k = d[0, rows, :]
            none = jnp.zeros_like(c)
            if side == 0:
                a = advanced(c, w, e, s, n, none, inside, ax, ay, az, k)
                b = k + jnp.maximum(az, 0.0)
            else:
                a = advanced(c, w, e, s, n, inside, none, ax, ay, az, k)
                b = k - jnp.minimum(az, 0.0)
            out[r : r + 8, :] = c
            out[NY + r : NY + r + 8, :] = a
            out[2 * NY + r : 2 * NY + r + 8, :] = b
            zsum[side * NY + r : side * NY + r + 8, :] = c + inside
    pairs = table((128, 128), lambda r, c: r // 2 == c)
    lane = lax.broadcasted_iota(jnp.int32, (128, 128), 1)
    clo = jnp.zeros((128, 128), F32)
    chi = jnp.zeros((128, 128), F32)
    for b in range(4):
        t = restrict_block(zsum[:, 256 * b : 256 * b + 256], pairs)
        tl = jnp.where(lane < 32, t, 0.0)
        th = jnp.where((lane >= 32) & (lane < 64), t, 0.0)
        clo += pltpu.roll(tl, 32 * b, 1) if b else tl
        chi += pltpu.roll(th, (32 * b - 32) % 128, 1) if b != 1 else th
    for i in range(8):
        lo[3 * NY : 3 * NY + 16, 128 * i : 128 * i + 128] = clo[16 * i : 16 * i + 16, :]
        hi[3 * NY : 3 * NY + 16, 128 * i : 128 * i + 128] = chi[16 * i : 16 * i + 16, :]


MSG = 3 * NY + 16


def layer_specs():
    return [
        pl.BlockSpec((3, 1, NY, NX), lambda i: (0, 0, 0, 0)),
        pl.BlockSpec((3, 1, NY, NX), lambda i: (0, LZ - 1, 0, 0)),
        pl.BlockSpec((1, NY, NX), lambda i: (0, 0, 0)),
        pl.BlockSpec((1, NY, NX), lambda i: (LZ - 1, 0, 0)),
    ]


def whole():
    return pl.BlockSpec(memory_space=pltpu.VMEM)


def anywhere():
    return pl.BlockSpec(memory_space=pl.ANY)


def edges(state, velocity, diffusivity):
    msg = jax.ShapeDtypeStruct((MSG, NX), F32)
    return pl.pallas_call(
        edges_kernel,
        out_shape=[msg, msg],
        grid=(1,),
        in_specs=[
            pl.BlockSpec((2, NY, NX), lambda i: (0, 0, 0)),
            pl.BlockSpec((2, NY, NX), lambda i: (LZ // 2 - 1, 0, 0)),
        ]
        + layer_specs(),
        out_specs=[whole(), whole()],
        scratch_shapes=[pltpu.VMEM((2, PADDED, NX), F32), pltpu.VMEM((2 * NY, NX), F32)],
        compiler_params=params(24),
        name="edges",
    )(state, state, velocity, velocity, diffusivity, diffusivity)


def interior_kernel(st, vel, dif, mid, edge, ct, gcp, cb, rfm, u, u1, v, d, zs, ct0, usem, vsem, dsem):
    ucopy = pltpu.make_async_copy(st, u.at[:, TOP : TOP + NY, :], usem)
    ucopy.start()
    vcopies, dcopies = [], []
    for z in range(LZ):
        vcopies.append(pltpu.make_async_copy(vel.at[:, z], v.at[:, z], vsem.at[z]))
        dcopies.append(pltpu.make_async_copy(dif.at[z], d.at[z], dsem.at[z]))
        vcopies[z].start()
        dcopies[z].start()
    ucopy.wait()
    for z in range(LZ):
        wrap_rows(u, z)
        if z % 2 == 0:
            for r in range(0, NY, 8):
                zs[4, (z // 2) * NY + r : (z // 2) * NY + r + 8, :] = (
                    u[z, TOP + r : TOP + r + 8, :] + u[z + 1, TOP + r : TOP + r + 8, :]
                )

    for z in range(LZ):
        vcopies[z].wait()
        dcopies[z].wait()

    def first(z, _):
        for r in range(0, NY, 8):
            rows = slice(r, r + 8)
            here = slice(TOP + r, TOP + r + 8)
            c, w, e, s, n = plane(u, z, r)
            u1[z, here, :] = advanced(
                c, w, e, s, n, u[z - 1, here, :], u[z + 1, here, :],
                v[0, z, rows, :], v[1, z, rows, :], v[2, z, rows, :], d[z, rows, :],
            )
        wrap_rows(u1, z)
        return 0

    lax.fori_loop(1, LZ - 1, first, 0)
    u1[0, TOP : TOP + NY, :] = jnp.zeros((NY, NX), F32)
    u1[LZ - 1, TOP : TOP + NY, :] = jnp.zeros((NY, NX), F32)
    edge[0] = u1[1, TOP : TOP + NY, :]
    edge[1] = u1[LZ - 2, TOP : TOP + NY, :]

    def second(z, _):
        for r in range(0, NY, 8):
            rows = slice(r, r + 8)
            here = slice(TOP + r, TOP + r + 8)
            c, w, e, s, n = plane(u1, z, r)
            u[z, here, :] = advanced(
                c, w, e, s, n, u1[z - 1, here, :], u1[z + 1, here, :],
                v[0, z, rows, :], v[1, z, rows, :], v[2, z, rows, :], d[z, rows, :],
            )
        return 0

    lax.fori_loop(1, LZ - 1, second, 0)
    edge[2] = u[1, TOP : TOP + NY, :]
    edge[3] = u[LZ - 2, TOP : TOP + NY, :]
    edge[4] = d[1] + jnp.maximum(v[2, 1], 0.0)
    edge[5] = d[LZ - 2] - jnp.minimum(v[2, LZ - 2], 0.0)
    for z in range(2, LZ - 2):
        mid[z - 2] = u[z, TOP : TOP + NY, :]
    for zc in range(4):
        for r in range(0, NY, 8):
            rows = slice(r, r + 8)
            to = slice(zc * NY + r, zc * NY + r + 8)
            for comp in range(3):
                zs[comp, to, :] = v[comp, 2 * zc, rows, :] + v[comp, 2 * zc + 1, rows, :]
            zs[3, to, :] = d[2 * zc, rows, :] + d[2 * zc + 1, rows, :]
            if zc in (1, 2):
                here = slice(TOP + r, TOP + r + 8)
                zs[5, to, :] = u[2 * zc, here, :] + u[2 * zc + 1, here, :]
            else:
                zs[5, to, :] = jnp.zeros((8, NX), F32)

    pairs = table((256, 128), lambda r, c: r // 2 == c)
    for comp in range(6):
        for b in range(4):
            t = restrict_block(zs[comp, :, 256 * b : 256 * b + 256], pairs)
            if comp < 4:
                ct[comp, 8 + 128 * b : 136 + 128 * b, :] = t
            elif comp == 4:
                ct0[8 + 128 * b : 136 + 128 * b, :] = t
            else:
                rfm[128 * b : 128 * b + 128, :] = t
    for comp in range(4):
        ct[comp, 0:8, :] = ct[comp, CX : CX + 8, :]
        ct[comp, CX + 8 : CX + 32, :] = ct[comp, 8:32, :]
    ct0[0:8, :] = ct0[CX : CX + 8, :]
    ct0[CX + 8 : CX + 16, :] = ct0[8:16, :]
    lane = lax.broadcasted_iota(jnp.int32, (64, CL), 1)
    for r in range(0, CX, 64):
        c = ct0[8 + r : 72 + r, :]
        xl, xh, yl, yh, zl, zh = coarse_coefs(*(ct[i, 8 + r : 72 + r, :] for i in range(4)))
        s, n = y_rolled(c, CL, 1)
        b = jnp.where(lane < 32, 0.0, pltpu.roll(c, 32, 1))
        t = jnp.where(lane >= 96, 0.0, pltpu.roll(c, 96, 1))
        w = ct0[7 + r : 71 + r, :]
        e = ct0[9 + r : 73 + r, :]
        gcp[r : r + 64, :] = c + (
            (xl * (w - c) + xh * (e - c)) + (yl * (s - c) + yh * (n - c)) + (zl * (b - c) + zh * (t - c))
        )
        cb[r : r + 64, :] = jnp.where(lane < 32, zl, jnp.where(lane >= 96, zh, 0.0))


CROWS = CX + 32


def interior(state, velocity, diffusivity):
    small = jax.ShapeDtypeStruct((CX, CL), F32)
    return pl.pallas_call(
        interior_kernel,
        out_shape=[
            jax.ShapeDtypeStruct((4, NY, NX), F32),
            jax.ShapeDtypeStruct((6, NY, NX), F32),
            jax.ShapeDtypeStruct((4, CROWS, CL), F32),
            small,
            small,
            small,
        ],
        in_specs=[anywhere()] * 3,
        out_specs=[whole()] * 6,
        scratch_shapes=[
            pltpu.VMEM((LZ, PADDED, NX), F32),
            pltpu.VMEM((LZ, PADDED, NX), F32),
            pltpu.VMEM((3, LZ, NY, NX), F32),
            pltpu.VMEM((LZ, NY, NX), F32),
            pltpu.VMEM((6, 4 * NY, NX), F32),
            pltpu.VMEM((CX + 16, CL), F32),
            pltpu.SemaphoreType.DMA,
            pltpu.SemaphoreType.DMA((LZ,)),
            pltpu.SemaphoreType.DMA((LZ,)),
        ],
        compiler_params=params(40),
        cost_estimate=pl.CostEstimate(flops=60_000_000, bytes_accessed=20_000_000, transcendentals=0),
        name="interior",
    )(state, velocity, diffusivity)


def finish_kernel(rlo, rhi, olo, ohi, edge, vlo, vhi, dlo, dhi, gcp, cb, rfm, ct, ub, msg, gc, pad, zsum, jp):
    slice_index = lax.axis_index("tm")
    for side, (rec, own, v, d) in enumerate(((rlo, olo, vlo, dlo), (rhi, ohi, vhi, dhi))):
        for r in range(0, NY, 8):
            pad[side, TOP + r : TOP + r + 8, :] = (
                own[NY + r : NY + r + 8, :] + own[2 * NY + r : 2 * NY + r + 8, :] * rec[r : r + 8, :]
            )
        wrap_rows(pad, side)
        for r in range(0, NY, 8):
            rows = slice(r, r + 8)
            c, w, e, s, n = plane(pad, side, r)
            outside = rec[NY + r : NY + r + 8, :] + rec[2 * NY + r : 2 * NY + r + 8, :] * own[r : r + 8, :]
            inside = edge[side, rows, :]
            b, t = (outside, inside) if side == 0 else (inside, outside)
            last = advanced(c, w, e, s, n, b, t, v[0, 0, rows, :], v[1, 0, rows, :], v[2, 0, rows, :], d[0, rows, :])
            near = edge[2 + side, rows, :] + edge[4 + side, rows, :] * c
            ub[3 * side, rows, :] = last
            ub[1 + side, rows, :] = near
            zsum[side * NY + r : side * NY + r + 8, :] = last + near
    pairs = table(
        (128, 128), lambda r, c: ((r < 64) & (c == r // 2)) | ((r >= 64) & (c == 96 + (r - 64) // 2))
    )
    lane = lax.broadcasted_iota(jnp.int32, (128, 128), 1)
    halo_lo = jnp.concatenate([rlo[3 * NY : MSG, 128 * i : 128 * i + 128] for i in range(8)], axis=0)
    halo_hi = jnp.concatenate([rhi[3 * NY : MSG, 128 * i : 128 * i + 128] for i in range(8)], axis=0)
    for b in range(4):
        rows = slice(128 * b, 128 * b + 128)
        t = restrict_block(zsum[:, 256 * b : 256 * b + 256], pairs) + rfm[rows, :]
        hl = pltpu.roll(halo_lo, (128 - 32 * b) % 128, 1) if b else halo_lo
        hh = pltpu.roll(halo_hi, (96 - 32 * b) % 128, 1) if b != 3 else halo_hi
        halo = jnp.where(lane < 32, hl, hh)
        g = gcp[rows, :] + cb[rows, :] * halo
        g = jnp.where(slice_index == 0, 0.0, g)
        gc[rows, :] = g
        jp[8 + 128 * b : 136 + 128 * b, :] = t - g
    jp[0:8, :] = jp[CX : CX + 8, :]
    jp[CX + 8 : CX + 24, :] = jp[8:24, :]
    comp = slice_index // 2
    first = pl.multiple_of((slice_index % 2) * 16, 16)
    for i in range(BLOCKS):
        msg[i, 0:WIN, :] = jp[XB * i : XB * i + WIN, :]
        msg[i, WIN : WIN + 16, :] = ct[comp, pl.ds(first + XB * i, 16), :]


def finish(rlo, rhi, olo, ohi, edge, velocity, diffusivity, gcp, cb, rfm, ct):
    return pl.pallas_call(
        finish_kernel,
        out_shape=[
            jax.ShapeDtypeStruct((4, NY, NX), F32),
            jax.ShapeDtypeStruct((BLOCKS, WIN + 16, CL), F32),
            jax.ShapeDtypeStruct((CX, CL), F32),
        ],
        grid=(1,),
        in_specs=[whole()] * 5 + layer_specs() + [whole()] * 4,
        out_specs=[whole()] * 3,
        scratch_shapes=[
            pltpu.VMEM((2, PADDED, NX), F32),
            pltpu.VMEM((2 * NY, NX), F32),
            pltpu.VMEM((CX + 24, CL), F32),
        ],
        compiler_params=params(32),
        name="finish",
    )(rlo, rhi, olo, ohi, edge, velocity, velocity, diffusivity, diffusivity, gcp, cb, rfm, ct)


HALO = 18


def pick_kernel(got, up, down):
    for out, near, far in ((up, 3, 2), (down, 0, 1)):
        for j in range(7):
            out[j] = got[QUAD * j + near, 0:WIN, :]
        for j in range(3):
            out[7 + j] = got[QUAD * j + far, 0:WIN, :]
        for k in range(GROUPS):
            rows = slice(16 * (k % 2), 16 * (k % 2) + 16)
            out[10 + k // 2, rows, :] = got[QUAD * k + near, WIN : WIN + 16, :]
            out[14 + k // 2, rows, :] = got[QUAD * k + far, WIN : WIN + 16, :]


def pick(got):
    halo = jax.ShapeDtypeStruct((HALO, WIN, CL), F32)
    return pl.pallas_call(
        pick_kernel,
        out_shape=[halo, halo],
        in_specs=[whole()],
        out_specs=[whole(), whole()],
        compiler_params=params(16),
        name="pick",
    )(got)


LANES = 8 * CL


def chain_kernel(got, below, above, out, src, cf, e):
    for j in range(7):
        if j < 3:
            src[j, :, 0:CL] = below[7 + j]
            src[j, :, 7 * CL :] = above[7 + j]
        else:
            src[j, :, 0:CL] = jnp.zeros((WIN, CL), F32)
            src[j, :, 7 * CL :] = jnp.zeros((WIN, CL), F32)
        src[j, :, CL : 2 * CL] = below[j]
        src[j, :, 6 * CL : 7 * CL] = above[j]
        for q in range(QUAD):
            src[j, :, (2 + q) * CL : (3 + q) * CL] = got[QUAD * j + q, 0:WIN, :]
    for block in range(8):
        lanes = slice(block * CL, block * CL + CL)
        for half in range(2):
            rows = slice(16 * half, 16 * half + 16)
            if block == 0:
                parts = [below[14 + i, rows, :] for i in range(4)]
            elif block == 1:
                parts = [below[10 + i, rows, :] for i in range(4)]
            elif block == 6:
                parts = [above[10 + i, rows, :] for i in range(4)]
            elif block == 7:
                parts = [above[14 + i, rows, :] for i in range(4)]
            else:
                parts = [got[QUAD * (2 * i + half) + block - 2, WIN : WIN + 16, :] for i in range(4)]
            for i, value in enumerate(coarse_coefs(*parts)):
                cf[i, rows, lanes] = value
    for q in range(QUAD):
        out[q] = jnp.zeros((XB, CL), F32)
    e[...] = src[0]
    for k in range(1, GROUPS):
        c = e[...]
        s, n = y_rolled(c, LANES, 1)
        w, x = pltpu.roll(c, 1, 0), pltpu.roll(c, WIN - 1, 0)
        b, t = pltpu.roll(c, 32, 1), pltpu.roll(c, LANES - 32, 1)
        y = c + (
            (cf[0] * (w - c) + cf[1] * (x - c))
            + (cf[2] * (s - c) + cf[3] * (n - c))
            + (cf[4] * (b - c) + cf[5] * (t - c))
        )
        for q in range(QUAD):
            out[QUAD * k + q] = y[8 : 8 + XB, (2 + q) * CL : (3 + q) * CL]
        if k < GROUPS - 1:
            e[...] = y + src[k]


def chain(got, below, above):
    return pl.pallas_call(
        chain_kernel,
        out_shape=jax.ShapeDtypeStruct((BLOCKS, XB, CL), F32),
        in_specs=[whole()] * 3,
        out_specs=whole(),
        scratch_shapes=[
            pltpu.VMEM((7, WIN, LANES), F32),
            pltpu.VMEM((6, WIN, LANES), F32),
            pltpu.VMEM((WIN, LANES), F32),
        ],
        compiler_params=params(24),
        name="chain",
    )(got, below, above)


def result_kernel(y, gc, mid, ub, out):
    copy_y = table((256, CL), lambda r, c: r // 2 == c)
    copy_x = table((128, 256), lambda r, c: r == c // 2)
    for b in range(4):
        rows = slice(128 * b, 128 * b + 128)
        cols = slice(256 * b, 256 * b + 256)
        parts = split3(y[rows, :] - gc[rows, :])
        fine = sum(dot(dot(copy_y, p, 1, 1).astype(BF16), copy_x, 1, 0) for p in parts)
        for z in range(LZ):
            zc = z // 2
            base = mid[z - 2, :, cols] if 2 <= z < 6 else ub[z if z < 2 else z - 4, :, cols]
            out[z, :, cols] = base + fine[zc * NY : zc * NY + NY, :]


def result(y, gc, mid, ub):
    return pl.pallas_call(
        result_kernel,
        out_shape=jax.ShapeDtypeStruct((LZ, NY, NX), F32),
        in_specs=[whole()] * 4,
        out_specs=whole(),
        compiler_params=params(24),
        name="result",
    )(y, gc, mid, ub)


def shift(value, axes, by):
    count = lax.axis_size(axes)
    return lax.ppermute(value, axes, [(i, i + by) for i in range(count) if 0 <= i + by < count])


def shards(state_old, velocity, diffusivity):
    state = state_old[0]
    olo, ohi = edges(state, velocity, diffusivity)
    rlo = shift(ohi, SPACE, 1)
    rhi = shift(olo, SPACE, -1)
    mid, edge, ct, gcp, cb, rfm = interior(state, velocity, diffusivity)
    ub, msg, gc = finish(rlo, rhi, olo, ohi, edge, velocity, diffusivity, gcp, cb, rfm, ct)
    got = lax.all_to_all(msg, GROUP, 0, 0)
    up, down = pick(got)
    below = shift(up, "px", 1)
    above = shift(down, "px", -1)
    back = lax.all_to_all(chain(got, below, above), GROUP, 0, 0)
    return result(back.reshape(CX, CL), gc, mid, ub)[None]


def solution(mesh):
    fine_mesh = Mesh(mesh.devices.reshape(GROUPS, 4, 2, 2), ("tm",) + SPACE)
    return jax.shard_map(
        shards,
        mesh=fine_mesh,
        in_specs=(
            P("tm", SPACE, None, None),
            P(None, SPACE, None, None),
            P(SPACE, None, None),
        ),
        out_specs=P("tm", SPACE, None, None),
        check_vma=False,
    )
```

```python
import jax
import jax.numpy as jnp
from jax import lax
from jax.experimental import pallas as pl
from jax.experimental.pallas import tpu as pltpu
from jax.sharding import Mesh
from jax.sharding import PartitionSpec as P

F32 = jnp.float32
BF16 = jnp.bfloat16
NY, NX = 64, 1024
LZ = 8
CX, CL = 512, 128
GROUPS = 8
QUAD = 4
BLOCKS = GROUPS * QUAD
XB = CX // BLOCKS
WIN = XB + 16
TOP = 8
PADDED = NY + 16
SPACE = ("px", "pz", "core")
GROUP = ("tm", "pz", "core")


def params(mib):
    return pltpu.CompilerParams(vmem_limit_bytes=mib * 1024 * 1024)


def split3(x):
    hi = x.astype(BF16)
    rest = x - hi.astype(F32)
    mid = rest.astype(BF16)
    return hi, mid, (rest - mid.astype(F32)).astype(BF16)


def dot(a, b, ca, cb):
    return lax.dot_general(a, b, (((ca,), (cb,)), ((), ())), preferred_element_type=F32)


def table(shape, test):
    rows = lax.broadcasted_iota(jnp.int32, shape, 0)
    cols = lax.broadcasted_iota(jnp.int32, shape, 1)
    return test(rows, cols).astype(F32).astype(BF16)


def halved_x(part):
    halve = table((128, 256), lambda r, c: r == c // 2)
    return sum(dot(halve, p, 1, 1) for p in split3(part)) * 0.125


def put_columns(ref, at, value):
    for i in range(NX // 128):
        ref[i, at, :] = value[:, 128 * i : 128 * i + 128]


def paired(ref, column, first, rows):
    return ref[column, pl.ds(first, rows, 2), :] + ref[column, pl.ds(first + 1, rows, 2), :]


def advanced(c, w, e, s, n, b, t, ax, ay, az, k):
    lap = ((w + e) + (s + n)) + ((b + t) - 6.0 * c)
    dx = jnp.abs(ax) * (jnp.where(ax > 0, w, e) - c)
    dy = jnp.abs(ay) * (jnp.where(ay > 0, s, n) - c)
    dz = jnp.abs(az) * (jnp.where(az > 0, b, t) - c)
    return (c + k * lap) + ((dx + dy) + dz)


def wrap_rows(ref, z):
    ref[z, TOP - 1 : TOP, :] = ref[z, TOP + NY - 1 : TOP + NY, :]
    ref[z, TOP + NY : TOP + NY + 1, :] = ref[z, TOP : TOP + 1, :]


def plane(ref, z, r):
    c = ref[z, TOP + r : TOP + r + 8, :]
    s = ref[z, TOP + r - 1 : TOP + r + 7, :]
    n = ref[z, TOP + r + 1 : TOP + r + 9, :]
    return c, pltpu.roll(c, 1, 1), pltpu.roll(c, NX - 1, 1), s, n


def coarse_coefs(vx, vy, vz, k):
    half = 0.5 * k
    out = []
    for a in (vx, vy, vz):
        out += [half + jnp.maximum(a, 0.0), half - jnp.minimum(a, 0.0)]
    return out


def y_rolled(u, width, axis):
    y = lax.broadcasted_iota(jnp.int32, u.shape, axis) % 32
    s = jnp.where(y == 0, pltpu.roll(u, width - 31, axis), pltpu.roll(u, 1, axis))
    n = jnp.where(y == 31, pltpu.roll(u, 31, axis), pltpu.roll(u, width - 1, axis))
    return s, n


MSG = 3 * NY + 16
CROWS = CX + 32


def edges_kernel(st, vel, dif, lo, hi, pad, inner, v, d, zs, sems):
    copies = []
    for side, (z, near) in enumerate(((0, 1), (LZ - 1, LZ - 2))):
        pairs = (
            (st.at[z], pad.at[side, TOP : TOP + NY, :]),
            (vel.at[:, z], v.at[side]),
            (dif.at[z], d.at[side]),
            (st.at[near], inner.at[side]),
        )
        copies.append([pltpu.make_async_copy(a, b, sems.at[side, i]) for i, (a, b) in enumerate(pairs)])
    for group in copies:
        for copy in group:
            copy.start()
    for side, out in enumerate((lo, hi)):
        for copy in copies[side]:
            copy.wait()
        wrap_rows(pad, side)
        for r in range(0, NY, 8):
            rows = slice(r, r + 8)
            c, w, e, s, n = plane(pad, side, r)
            inside = inner[side, rows, :]
            ax, ay, az = v[side, 0, rows, :], v[side, 1, rows, :], v[side, 2, rows, :]
            k = d[side, rows, :]
            none = jnp.zeros_like(c)
            if side == 0:
                a = advanced(c, w, e, s, n, none, inside, ax, ay, az, k)
                b = k + jnp.maximum(az, 0.0)
            else:
                a = advanced(c, w, e, s, n, inside, none, ax, ay, az, k)
                b = k - jnp.minimum(az, 0.0)
            out[r : r + 8, :] = c
            out[NY + r : NY + r + 8, :] = a
            out[2 * NY + r : 2 * NY + r + 8, :] = b
            put_columns(zs, slice(side * NY + r, side * NY + r + 8), c + inside)
    lane = lax.broadcasted_iota(jnp.int32, (128, 128), 1)
    clo = jnp.zeros((128, 128), F32)
    chi = jnp.zeros((128, 128), F32)
    for b in range(4):
        part = jnp.concatenate([paired(zs, 2 * b + i, 0, 64) for i in range(2)], axis=1)
        t = halved_x(jnp.concatenate([part, jnp.zeros_like(part)], axis=0))
        tl = jnp.where(lane < 32, t, 0.0)
        th = jnp.where((lane >= 32) & (lane < 64), t, 0.0)
        clo += pltpu.roll(tl, 32 * b, 1) if b else tl
        chi += pltpu.roll(th, (32 * b - 32) % 128, 1) if b != 1 else th
    for i in range(8):
        lo[3 * NY : 3 * NY + 16, 128 * i : 128 * i + 128] = clo[16 * i : 16 * i + 16, :]
        hi[3 * NY : 3 * NY + 16, 128 * i : 128 * i + 128] = chi[16 * i : 16 * i + 16, :]


def whole():
    return pl.BlockSpec(memory_space=pltpu.VMEM)


def remains():
    return pl.BlockSpec(memory_space=pltpu.HBM)


def edges(state, velocity, diffusivity):
    msg = jax.ShapeDtypeStruct((MSG, NX), F32)
    return pl.pallas_call(
        edges_kernel,
        out_shape=[msg, msg],
        in_specs=[remains()] * 3,
        out_specs=[whole(), whole()],
        scratch_shapes=[
            pltpu.VMEM((2, PADDED, NX), F32),
            pltpu.VMEM((2, NY, NX), F32),
            pltpu.VMEM((2, 3, NY, NX), F32),
            pltpu.VMEM((2, NY, NX), F32),
            pltpu.VMEM((8, 2 * NY, 128), F32),
            pltpu.SemaphoreType.DMA((2, 4)),
        ],
        compiler_params=params(16),
        name="edges",
    )(state, velocity, diffusivity)


def interior_kernel(st, v, d, fin, edge, ct, gcp, cb, ymid, u, u1, zs, ct0, usem):
    copy = pltpu.make_async_copy(st, u.at[:, TOP : TOP + NY, :], usem)
    copy.start()
    for zc in range(4):
        for r in range(0, NY, 8):
            to, rows = slice(zc * NY + r, zc * NY + r + 8), slice(r, r + 8)
            for comp in range(3):
                put_columns(zs.at[comp], to, v[comp, 2 * zc, rows, :] + v[comp, 2 * zc + 1, rows, :])
            put_columns(zs.at[3], to, d[2 * zc, rows, :] + d[2 * zc + 1, rows, :])
    copy.wait()
    for z in range(LZ):
        wrap_rows(u, z)
    for zc in range(4):
        for r in range(0, NY, 8):
            here = slice(TOP + r, TOP + r + 8)
            put_columns(zs.at[4], slice(zc * NY + r, zc * NY + r + 8), u[2 * zc, here, :] + u[2 * zc + 1, here, :])

    def first(z, _):
        for r in range(0, NY, 8):
            rows = slice(r, r + 8)
            here = slice(TOP + r, TOP + r + 8)
            c, w, e, s, n = plane(u, z, r)
            u1[z, here, :] = advanced(
                c, w, e, s, n, u[z - 1, here, :], u[z + 1, here, :],
                v[0, z, rows, :], v[1, z, rows, :], v[2, z, rows, :], d[z, rows, :],
            )
        wrap_rows(u1, z)
        return 0

    lax.fori_loop(1, LZ - 1, first, 0)
    u1[0, TOP : TOP + NY, :] = jnp.zeros((NY, NX), F32)
    u1[LZ - 1, TOP : TOP + NY, :] = jnp.zeros((NY, NX), F32)
    edge[0] = u1[1, TOP : TOP + NY, :]
    edge[1] = u1[LZ - 2, TOP : TOP + NY, :]

    def second(z, _):
        for r in range(0, NY, 8):
            rows = slice(r, r + 8)
            here = slice(TOP + r, TOP + r + 8)
            c, w, e, s, n = plane(u1, z, r)
            fin[z - 1, rows, :] = advanced(
                c, w, e, s, n, u1[z - 1, here, :], u1[z + 1, here, :],
                v[0, z, rows, :], v[1, z, rows, :], v[2, z, rows, :], d[z, rows, :],
            )
        return 0

    lax.fori_loop(1, LZ - 1, second, 0)
    edge[2] = d[1] + jnp.maximum(v[2, 1], 0.0)
    edge[3] = d[LZ - 2] - jnp.minimum(v[2, LZ - 2], 0.0)
    for zc in (1, 2):
        for r in range(0, NY, 8):
            rows = slice(r, r + 8)
            put_columns(zs.at[5], slice((zc - 1) * NY + r, (zc - 1) * NY + r + 8), fin[2 * zc - 1, rows, :] + fin[2 * zc, rows, :])
    for i in range(8):
        ymid[i] = paired(zs.at[5], i, 0, 64)

    for comp in range(5):
        for b in range(4):
            t = halved_x(jnp.concatenate([paired(zs.at[comp], 2 * b + i, 0, 128) for i in range(2)], axis=1))
            if comp < 4:
                ct[comp, 8 + 128 * b : 136 + 128 * b, :] = t
            else:
                ct0[8 + 128 * b : 136 + 128 * b, :] = t
    for comp in range(4):
        ct[comp, 0:8, :] = ct[comp, CX : CX + 8, :]
        ct[comp, CX + 8 : CX + 32, :] = ct[comp, 8:32, :]
    ct0[0:8, :] = ct0[CX : CX + 8, :]
    ct0[CX + 8 : CX + 16, :] = ct0[8:16, :]
    lane = lax.broadcasted_iota(jnp.int32, (64, CL), 1)
    for r in range(0, CX, 64):
        c = ct0[8 + r : 72 + r, :]
        xl, xh, yl, yh, zl, zh = coarse_coefs(*(ct[i, 8 + r : 72 + r, :] for i in range(4)))
        s, n = y_rolled(c, CL, 1)
        b = jnp.where(lane < 32, 0.0, pltpu.roll(c, 32, 1))
        t = jnp.where(lane >= 96, 0.0, pltpu.roll(c, 96, 1))
        w = ct0[7 + r : 71 + r, :]
        e = ct0[9 + r : 73 + r, :]
        gcp[r : r + 64, :] = c + (
            (xl * (w - c) + xh * (e - c)) + (yl * (s - c) + yh * (n - c)) + (zl * (b - c) + zh * (t - c))
        )
        cb[r : r + 64, :] = jnp.where(lane < 32, zl, jnp.where(lane >= 96, zh, 0.0))


def interior(state, velocity, diffusivity):
    small = jax.ShapeDtypeStruct((CX, CL), F32)
    return pl.pallas_call(
        interior_kernel,
        out_shape=[
            jax.ShapeDtypeStruct((LZ - 2, NY, NX), F32),
            jax.ShapeDtypeStruct((4, NY, NX), F32),
            jax.ShapeDtypeStruct((4, CROWS, CL), F32),
            small,
            small,
            jax.ShapeDtypeStruct((8, 64, 128), F32),
        ],
        in_specs=[remains(), whole(), whole()],
        out_specs=[whole()] * 6,
        scratch_shapes=[
            pltpu.VMEM((LZ, PADDED, NX), F32),
            pltpu.VMEM((LZ, PADDED, NX), F32),
            pltpu.VMEM((6, 8, 4 * NY, 128), F32),
            pltpu.VMEM((CX + 16, CL), F32),
            pltpu.SemaphoreType.DMA,
        ],
        compiler_params=params(32),
        cost_estimate=pl.CostEstimate(flops=60_000_000, bytes_accessed=20_000_000, transcendentals=0),
        name="interior",
    )(state, velocity, diffusivity)


def finish_kernel(rlo, rhi, olo, ohi, fin, edge, vel, dif, gcp, cb, ymid, ct, ub, msg, gc, pad, v, d, zs, jp, sems):
    copies = []
    for side, z in enumerate((0, LZ - 1)):
        copies.append(pltpu.make_async_copy(vel.at[:, z], v.at[side], sems.at[side, 0]))
        copies.append(pltpu.make_async_copy(dif.at[z], d.at[side], sems.at[side, 1]))
    for copy in copies:
        copy.start()
    slice_index = lax.axis_index("tm")
    for side, (rec, own) in enumerate(((rlo, olo), (rhi, ohi))):
        for r in range(0, NY, 8):
            pad[side, TOP + r : TOP + r + 8, :] = (
                own[NY + r : NY + r + 8, :] + own[2 * NY + r : 2 * NY + r + 8, :] * rec[r : r + 8, :]
            )
        wrap_rows(pad, side)
        copies[2 * side].wait()
        copies[2 * side + 1].wait()
        for r in range(0, NY, 8):
            rows = slice(r, r + 8)
            c, w, e, s, n = plane(pad, side, r)
            outside = rec[NY + r : NY + r + 8, :] + rec[2 * NY + r : 2 * NY + r + 8, :] * own[r : r + 8, :]
            inside = edge[side, rows, :]
            b, t = (outside, inside) if side == 0 else (inside, outside)
            last = advanced(
                c, w, e, s, n, b, t,
                v[side, 0, rows, :], v[side, 1, rows, :], v[side, 2, rows, :], d[side, rows, :],
            )
            near = fin[5 * side, rows, :] + edge[2 + side, rows, :] * c
            ub[3 * side, rows, :] = last
            ub[1 + side, rows, :] = near
            put_columns(zs, slice(side * NY + r, side * NY + r + 8), last + near)
    lane = lax.broadcasted_iota(jnp.int32, (128, 128), 1)
    halo_lo = jnp.concatenate([rlo[3 * NY : MSG, 128 * i : 128 * i + 128] for i in range(8)], axis=0)
    halo_hi = jnp.concatenate([rhi[3 * NY : MSG, 128 * i : 128 * i + 128] for i in range(8)], axis=0)
    for b in range(4):
        rows = slice(128 * b, 128 * b + 128)
        t = halved_x(
            jnp.concatenate(
                [
                    jnp.concatenate([paired(zs, i, 0, 32), ymid[i], paired(zs, i, NY, 32)], axis=0)
                    for i in (2 * b, 2 * b + 1)
                ],
                axis=1,
            )
        )
        hl = pltpu.roll(halo_lo, (128 - 32 * b) % 128, 1) if b else halo_lo
        hh = pltpu.roll(halo_hi, (96 - 32 * b) % 128, 1) if b != 3 else halo_hi
        halo = jnp.where(lane < 32, hl, hh)
        g = gcp[rows, :] + cb[rows, :] * halo
        g = jnp.where(slice_index == 0, 0.0, g)
        gc[rows, :] = g
        jp[8 + 128 * b : 136 + 128 * b, :] = t - g
    jp[0:8, :] = jp[CX : CX + 8, :]
    jp[CX + 8 : CX + 24, :] = jp[8:24, :]
    comp = slice_index // 2
    first = pl.multiple_of((slice_index % 2) * 16, 16)
    for i in range(BLOCKS):
        msg[i, 0:WIN, :] = jp[XB * i : XB * i + WIN, :]
        msg[i, WIN : WIN + 16, :] = ct[comp, pl.ds(first + XB * i, 16), :]


def finish(rlo, rhi, olo, ohi, fin, edge, velocity, diffusivity, gcp, cb, ymid, ct):
    return pl.pallas_call(
        finish_kernel,
        out_shape=[
            jax.ShapeDtypeStruct((4, NY, NX), F32),
            jax.ShapeDtypeStruct((BLOCKS, WIN + 16, CL), F32),
            jax.ShapeDtypeStruct((CX, CL), F32),
        ],
        in_specs=[whole()] * 6 + [remains()] * 2 + [whole()] * 4,
        out_specs=[whole()] * 3,
        scratch_shapes=[
            pltpu.VMEM((2, PADDED, NX), F32),
            pltpu.VMEM((2, 3, NY, NX), F32),
            pltpu.VMEM((2, NY, NX), F32),
            pltpu.VMEM((8, 2 * NY, 128), F32),
            pltpu.VMEM((CX + 24, CL), F32),
            pltpu.SemaphoreType.DMA((2, 2)),
        ],
        compiler_params=params(24),
        name="finish",
    )(rlo, rhi, olo, ohi, fin, edge, velocity, diffusivity, gcp, cb, ymid, ct)


HALO = 13
SHARED = ((0, 6, 96), (1, 5, 64), (2, 4, 32))


def pick_kernel(got, up, down):
    lane = lax.broadcasted_iota(jnp.int32, (WIN, CL), 1)

    def coef(i, slab):
        return jnp.concatenate([got[QUAD * (2 * i + h) + slab, WIN : WIN + 16, :] for h in range(2)], axis=0)

    for out, near, far in ((up, 3, 2), (down, 0, 1)):
        for j in range(4):
            out[j] = got[QUAD * j + near, 0:WIN, :]
            out[7 + j] = coef(j, near)
        for j, other, width in SHARED:
            mine = lane >= CL - width if near == 3 else lane < width
            turn = CL - width if near == 3 else width
            out[4 + j] = jnp.where(
                mine, got[QUAD * j + far, 0:WIN, :], pltpu.roll(got[QUAD * other + near, 0:WIN, :], turn, 1)
            )
        for j in range(2):
            mine = lane >= 64 if near == 3 else lane < 64
            out[11 + j] = jnp.where(mine, coef(2 * j, far), pltpu.roll(coef(2 * j + 1, far), 64, 1))


def pick(got):
    halo = jax.ShapeDtypeStruct((HALO, WIN, CL), F32)
    return pl.pallas_call(
        pick_kernel,
        out_shape=[halo, halo],
        in_specs=[whole()],
        out_specs=[whole(), whole()],
        compiler_params=params(16),
        name="pick",
    )(got)


LANES = 8 * CL


def chain_kernel(got, below, above, out, src, cf, e):
    for j in range(7):
        for q in range(QUAD):
            src[j, :, (2 + q) * CL : (3 + q) * CL] = got[QUAD * j + q, 0:WIN, :]
        for halo, near, far in ((below, 1, 0), (above, 6, 7)):
            if j < 4:
                src[j, :, near * CL : near * CL + CL] = halo[j]
            if j >= 3:
                src[j, :, far * CL : far * CL + CL] = jnp.zeros((WIN, CL), F32)
    for halo, near, far in ((below, 1, 0), (above, 6, 7)):
        for j, other, width in SHARED:
            turn = width if near == 1 else CL - width
            src[j, :, far * CL : far * CL + CL] = halo[4 + j]
            src[other, :, near * CL : near * CL + CL] = pltpu.roll(halo[4 + j], turn, 1)
    for block in range(8):
        lanes = slice(block * CL, block * CL + CL)
        halo = below if block < 2 else above
        for half in range(2):
            rows = slice(16 * half, 16 * half + 16)
            if block in (1, 6):
                parts = [halo[7 + i, rows, :] for i in range(4)]
            elif block in (0, 7):
                parts = [
                    pltpu.roll(halo[11 + i // 2, rows, :], 64, 1) if i % 2 else halo[11 + i // 2, rows, :]
                    for i in range(4)
                ]
            else:
                parts = [got[QUAD * (2 * i + half) + block - 2, WIN : WIN + 16, :] for i in range(4)]
            for i, value in enumerate(coarse_coefs(*parts)):
                cf[i, rows, lanes] = value
    for q in range(QUAD):
        out[q] = jnp.zeros((XB, CL), F32)
    e[...] = src[0]
    for k in range(1, GROUPS):
        c = e[...]
        s, n = y_rolled(c, LANES, 1)
        w, x = pltpu.roll(c, 1, 0), pltpu.roll(c, WIN - 1, 0)
        b, t = pltpu.roll(c, 32, 1), pltpu.roll(c, LANES - 32, 1)
        y = c + (
            (cf[0] * (w - c) + cf[1] * (x - c))
            + (cf[2] * (s - c) + cf[3] * (n - c))
            + (cf[4] * (b - c) + cf[5] * (t - c))
        )
        for q in range(QUAD):
            out[QUAD * k + q] = y[8 : 8 + XB, (2 + q) * CL : (3 + q) * CL]
        if k < GROUPS - 1:
            e[...] = y + src[k]


def chain(got, below, above):
    return pl.pallas_call(
        chain_kernel,
        out_shape=jax.ShapeDtypeStruct((BLOCKS, XB, CL), F32),
        in_specs=[whole()] * 3,
        out_specs=whole(),
        scratch_shapes=[
            pltpu.VMEM((7, WIN, LANES), F32),
            pltpu.VMEM((6, WIN, LANES), F32),
            pltpu.VMEM((WIN, LANES), F32),
        ],
        compiler_params=params(24),
        name="chain",
    )(got, below, above)


def result_kernel(y, gc, fin, ub, out, buf, sems):
    copy_y = table((256, CL), lambda r, c: r // 2 == c)
    copy_x = table((128, 256), lambda r, c: r == c // 2)
    copies = []
    for b in range(4):
        rows = slice(128 * b, 128 * b + 128)
        cols = slice(256 * b, 256 * b + 256)
        parts = split3(y[rows, :] - gc[rows, :])
        fine = sum(dot(dot(copy_y, p, 1, 1).astype(BF16), copy_x, 1, 0) for p in parts)
        for z in range(LZ):
            base = fin[z - 1, :, cols] if 2 <= z < 6 else ub[z if z < 2 else z - 4, :, cols]
            buf[z, :, cols] = base + fine[z // 2 * NY : z // 2 * NY + NY, :]
        copies.append(pltpu.make_async_copy(buf.at[:, :, cols], out.at[:, :, cols], sems.at[b]))
        copies[b].start()
    for copy in copies:
        copy.wait()


def result(y, gc, fin, ub):
    return pl.pallas_call(
        result_kernel,
        out_shape=jax.ShapeDtypeStruct((LZ, NY, NX), F32),
        in_specs=[whole()] * 4,
        out_specs=remains(),
        scratch_shapes=[pltpu.VMEM((LZ, NY, NX), F32), pltpu.SemaphoreType.DMA((4,))],
        compiler_params=params(16),
        name="result",
    )(y, gc, fin, ub)


def shift(value, axes, by):
    count = lax.axis_size(axes)
    return lax.ppermute(value, axes, [(i, i + by) for i in range(count) if 0 <= i + by < count])


def shards(state_old, velocity, diffusivity):
    state = state_old[0]
    olo, ohi = edges(state, velocity, diffusivity)
    rlo = shift(ohi, SPACE, 1)
    rhi = shift(olo, SPACE, -1)
    fin, edge, ct, gcp, cb, ymid = interior(state, velocity, diffusivity)
    ub, msg, gc = finish(rlo, rhi, olo, ohi, fin, edge, velocity, diffusivity, gcp, cb, ymid, ct)
    got = lax.all_to_all(msg, GROUP, 0, 0)
    up, down = pick(got)
    below = shift(up, "px", 1)
    above = shift(down, "px", -1)
    back = lax.all_to_all(chain(got, below, above), GROUP, 0, 0)
    return result(back.reshape(CX, CL), gc, fin, ub)[None]


def solution(mesh):
    fine_mesh = Mesh(mesh.devices.reshape(GROUPS, 4, 2, 2), ("tm",) + SPACE)
    return jax.shard_map(
        shards,
        mesh=fine_mesh,
        in_specs=(
            P("tm", SPACE, None, None),
            P(None, SPACE, None, None),
            P(SPACE, None, None),
        ),
        out_specs=P("tm", SPACE, None, None),
        check_vma=False,
    )
```

```python
import jax
import jax.numpy as jnp
from jax import lax
from jax.experimental import pallas as pl
from jax.experimental.pallas import tpu as pltpu
from jax.sharding import Mesh
from jax.sharding import PartitionSpec as P

F32 = jnp.float32
BF16 = jnp.bfloat16
NY, NX = 64, 1024
LZ = 8
CX, CL = 512, 128
GROUPS = 8
QUAD = 4
BLOCKS = GROUPS * QUAD
XB = CX // BLOCKS
WIN = XB + 16
TOP = 8
PADDED = NY + 16
SPACE = ("px", "pz", "core")
GROUP = ("tm", "pz", "core")


def params(mib):
    return pltpu.CompilerParams(vmem_limit_bytes=mib * 1024 * 1024)


def split3(x):
    hi = x.astype(BF16)
    rest = x - hi.astype(F32)
    mid = rest.astype(BF16)
    return hi, mid, (rest - mid.astype(F32)).astype(BF16)


def dot(a, b, ca, cb):
    return lax.dot_general(a, b, (((ca,), (cb,)), ((), ())), preferred_element_type=F32)


def table(shape, test):
    rows = lax.broadcasted_iota(jnp.int32, shape, 0)
    cols = lax.broadcasted_iota(jnp.int32, shape, 1)
    return test(rows, cols).astype(F32).astype(BF16)


def halved_x(part):
    halve = table((128, 256), lambda r, c: r == c // 2)
    return sum(dot(halve, p, 1, 1) for p in split3(part)) * 0.125


def put_columns(ref, at, value):
    for i in range(NX // 128):
        ref[i, at, :] = value[:, 128 * i : 128 * i + 128]


def paired(ref, column, first, rows):
    return ref[column, pl.ds(first, rows, 2), :] + ref[column, pl.ds(first + 1, rows, 2), :]


def advanced(c, w, e, s, n, b, t, ax, ay, az, k):
    lap = ((w + e) + (s + n)) + ((b + t) - 6.0 * c)
    dx = jnp.abs(ax) * (jnp.where(ax > 0, w, e) - c)
    dy = jnp.abs(ay) * (jnp.where(ay > 0, s, n) - c)
    dz = jnp.abs(az) * (jnp.where(az > 0, b, t) - c)
    return (c + k * lap) + ((dx + dy) + dz)


def wrap_rows(ref, z):
    ref[z, TOP - 1 : TOP, :] = ref[z, TOP + NY - 1 : TOP + NY, :]
    ref[z, TOP + NY : TOP + NY + 1, :] = ref[z, TOP : TOP + 1, :]


def plane(ref, z, r):
    c = ref[z, TOP + r : TOP + r + 8, :]
    s = ref[z, TOP + r - 1 : TOP + r + 7, :]
    n = ref[z, TOP + r + 1 : TOP + r + 9, :]
    return c, pltpu.roll(c, 1, 1), pltpu.roll(c, NX - 1, 1), s, n


def coarse_coefs(vx, vy, vz, k):
    half = 0.5 * k
    out = []
    for a in (vx, vy, vz):
        out += [half + jnp.maximum(a, 0.0), half - jnp.minimum(a, 0.0)]
    return out


def y_rolled(u, width, axis):
    y = lax.broadcasted_iota(jnp.int32, u.shape, axis) % 32
    s = jnp.where(y == 0, pltpu.roll(u, width - 31, axis), pltpu.roll(u, 1, axis))
    n = jnp.where(y == 31, pltpu.roll(u, 31, axis), pltpu.roll(u, width - 1, axis))
    return s, n


MSG = 2 * NY + 16
CROWS = CX + 32


def edges_kernel(st, vel, dif, lo, hi, blo, bhi, pad, inner, v, d, zs, sems):
    copies = []
    for side, (z, near) in enumerate(((0, 1), (LZ - 1, LZ - 2))):
        pairs = (
            (st.at[z], pad.at[side, TOP : TOP + NY, :]),
            (vel.at[:, z], v.at[side]),
            (dif.at[z], d.at[side]),
            (st.at[near], inner.at[side]),
        )
        copies.append([pltpu.make_async_copy(a, b, sems.at[side, i]) for i, (a, b) in enumerate(pairs)])
    for group in copies:
        for copy in group:
            copy.start()
    for side, (out, factor) in enumerate(((lo, blo), (hi, bhi))):
        for copy in copies[side]:
            copy.wait()
        wrap_rows(pad, side)
        for r in range(0, NY, 8):
            rows = slice(r, r + 8)
            c, w, e, s, n = plane(pad, side, r)
            inside = inner[side, rows, :]
            ax, ay, az = v[side, 0, rows, :], v[side, 1, rows, :], v[side, 2, rows, :]
            k = d[side, rows, :]
            none = jnp.zeros_like(c)
            if side == 0:
                a = advanced(c, w, e, s, n, none, inside, ax, ay, az, k)
                b = k + jnp.maximum(az, 0.0)
            else:
                a = advanced(c, w, e, s, n, inside, none, ax, ay, az, k)
                b = k - jnp.minimum(az, 0.0)
            out[r : r + 8, :] = c
            out[NY + r : NY + r + 8, :] = a
            factor[rows, :] = b
            put_columns(zs, slice(side * NY + r, side * NY + r + 8), c + inside)
    lane = lax.broadcasted_iota(jnp.int32, (128, 128), 1)
    clo = jnp.zeros((128, 128), F32)
    chi = jnp.zeros((128, 128), F32)
    for b in range(4):
        part = jnp.concatenate([paired(zs, 2 * b + i, 0, 64) for i in range(2)], axis=1)
        t = halved_x(jnp.concatenate([part, jnp.zeros_like(part)], axis=0))
        tl = jnp.where(lane < 32, t, 0.0)
        th = jnp.where((lane >= 32) & (lane < 64), t, 0.0)
        clo += pltpu.roll(tl, 32 * b, 1) if b else tl
        chi += pltpu.roll(th, (32 * b - 32) % 128, 1) if b != 1 else th
    for i in range(8):
        lo[2 * NY : MSG, 128 * i : 128 * i + 128] = clo[16 * i : 16 * i + 16, :]
        hi[2 * NY : MSG, 128 * i : 128 * i + 128] = chi[16 * i : 16 * i + 16, :]


def whole():
    return pl.BlockSpec(memory_space=pltpu.VMEM)


def remains():
    return pl.BlockSpec(memory_space=pltpu.HBM)


def edges(state, velocity, diffusivity):
    msg = jax.ShapeDtypeStruct((MSG, NX), F32)
    factor = jax.ShapeDtypeStruct((NY, NX), F32)
    return pl.pallas_call(
        edges_kernel,
        out_shape=[msg, msg, factor, factor],
        in_specs=[remains()] * 3,
        out_specs=[whole()] * 4,
        scratch_shapes=[
            pltpu.VMEM((2, PADDED, NX), F32),
            pltpu.VMEM((2, NY, NX), F32),
            pltpu.VMEM((2, 3, NY, NX), F32),
            pltpu.VMEM((2, NY, NX), F32),
            pltpu.VMEM((8, 2 * NY, 128), F32),
            pltpu.SemaphoreType.DMA((2, 4)),
        ],
        compiler_params=params(58),
        name="edges",
    )(state, velocity, diffusivity)


def interior_kernel(st, vel, dif, fin, edge, ct, gcp, cb, ymid, u, u1, v, d, zs, ct0, usem, sems):
    def layer(z):
        return (
            pltpu.make_async_copy(vel.at[:, z], v.at[:, z], sems.at[z, 0]),
            pltpu.make_async_copy(dif.at[z], d.at[z], sems.at[z, 1]),
        )

    copy = pltpu.make_async_copy(st, u.at[:, TOP : TOP + NY, :], usem)
    copy.start()
    for z in (1, 2, 3, 4, 5, 6, 0, 7):
        for part in layer(z):
            part.start()
    copy.wait()
    for z in range(LZ):
        wrap_rows(u, z)
    for zc in range(4):
        for r in range(0, NY, 8):
            here = slice(TOP + r, TOP + r + 8)
            put_columns(zs.at[4], slice(zc * NY + r, zc * NY + r + 8), u[2 * zc, here, :] + u[2 * zc + 1, here, :])

    def first(z, _):
        for part in layer(z):
            part.wait()
        for r in range(0, NY, 8):
            rows = slice(r, r + 8)
            here = slice(TOP + r, TOP + r + 8)
            c, w, e, s, n = plane(u, z, r)
            u1[z, here, :] = advanced(
                c, w, e, s, n, u[z - 1, here, :], u[z + 1, here, :],
                v[0, z, rows, :], v[1, z, rows, :], v[2, z, rows, :], d[z, rows, :],
            )
        wrap_rows(u1, z)
        return 0

    lax.fori_loop(1, LZ - 1, first, 0)
    u1[0, TOP : TOP + NY, :] = jnp.zeros((NY, NX), F32)
    u1[LZ - 1, TOP : TOP + NY, :] = jnp.zeros((NY, NX), F32)
    edge[0] = u1[1, TOP : TOP + NY, :]
    edge[1] = u1[LZ - 2, TOP : TOP + NY, :]

    def second(z, _):
        for r in range(0, NY, 8):
            rows = slice(r, r + 8)
            here = slice(TOP + r, TOP + r + 8)
            c, w, e, s, n = plane(u1, z, r)
            fin[z - 1, rows, :] = advanced(
                c, w, e, s, n, u1[z - 1, here, :], u1[z + 1, here, :],
                v[0, z, rows, :], v[1, z, rows, :], v[2, z, rows, :], d[z, rows, :],
            )
        return 0

    lax.fori_loop(1, LZ - 1, second, 0)
    edge[2] = d[1] + jnp.maximum(v[2, 1], 0.0)
    edge[3] = d[LZ - 2] - jnp.minimum(v[2, LZ - 2], 0.0)
    for zc in (1, 2):
        for r in range(0, NY, 8):
            rows = slice(r, r + 8)
            put_columns(zs.at[5], slice((zc - 1) * NY + r, (zc - 1) * NY + r + 8), fin[2 * zc - 1, rows, :] + fin[2 * zc, rows, :])
    for i in range(8):
        ymid[i] = paired(zs.at[5], i, 0, 64)

    for z in (0, LZ - 1):
        for part in layer(z):
            part.wait()
    for zc in range(4):
        for r in range(0, NY, 8):
            to, rows = slice(zc * NY + r, zc * NY + r + 8), slice(r, r + 8)
            for comp in range(3):
                put_columns(zs.at[comp], to, v[comp, 2 * zc, rows, :] + v[comp, 2 * zc + 1, rows, :])
            put_columns(zs.at[3], to, d[2 * zc, rows, :] + d[2 * zc + 1, rows, :])
    for comp in range(5):
        for b in range(4):
            t = halved_x(jnp.concatenate([paired(zs.at[comp], 2 * b + i, 0, 128) for i in range(2)], axis=1))
            if comp < 4:
                ct[comp, 8 + 128 * b : 136 + 128 * b, :] = t
            else:
                ct0[8 + 128 * b : 136 + 128 * b, :] = t
    for comp in range(4):
        ct[comp, 0:8, :] = ct[comp, CX : CX + 8, :]
        ct[comp, CX + 8 : CX + 32, :] = ct[comp, 8:32, :]
    ct0[0:8, :] = ct0[CX : CX + 8, :]
    ct0[CX + 8 : CX + 16, :] = ct0[8:16, :]
    lane = lax.broadcasted_iota(jnp.int32, (64, CL), 1)
    for r in range(0, CX, 64):
        c = ct0[8 + r : 72 + r, :]
        xl, xh, yl, yh, zl, zh = coarse_coefs(*(ct[i, 8 + r : 72 + r, :] for i in range(4)))
        s, n = y_rolled(c, CL, 1)
        b = jnp.where(lane < 32, 0.0, pltpu.roll(c, 32, 1))
        t = jnp.where(lane >= 96, 0.0, pltpu.roll(c, 96, 1))
        w = ct0[7 + r : 71 + r, :]
        e = ct0[9 + r : 73 + r, :]
        gcp[r : r + 64, :] = c + (
            (xl * (w - c) + xh * (e - c)) + (yl * (s - c) + yh * (n - c)) + (zl * (b - c) + zh * (t - c))
        )
        cb[r : r + 64, :] = jnp.where(lane < 32, zl, jnp.where(lane >= 96, zh, 0.0))


def interior(state, velocity, diffusivity):
    small = jax.ShapeDtypeStruct((CX, CL), F32)
    return pl.pallas_call(
        interior_kernel,
        out_shape=[
            jax.ShapeDtypeStruct((LZ - 2, NY, NX), F32),
            jax.ShapeDtypeStruct((4, NY, NX), F32),
            jax.ShapeDtypeStruct((4, CROWS, CL), F32),
            small,
            small,
            jax.ShapeDtypeStruct((8, 64, 128), F32),
        ],
        in_specs=[remains()] * 3,
        out_specs=[whole()] * 6,
        scratch_shapes=[
            pltpu.VMEM((LZ, PADDED, NX), F32),
            pltpu.VMEM((LZ, PADDED, NX), F32),
            pltpu.VMEM((3, LZ, NY, NX), F32),
            pltpu.VMEM((LZ, NY, NX), F32),
            pltpu.VMEM((6, 8, 4 * NY, 128), F32),
            pltpu.VMEM((CX + 16, CL), F32),
            pltpu.SemaphoreType.DMA,
            pltpu.SemaphoreType.DMA((LZ, 2)),
        ],
        compiler_params=params(48),
        cost_estimate=pl.CostEstimate(flops=60_000_000, bytes_accessed=20_000_000, transcendentals=0),
        name="interior",
    )(state, velocity, diffusivity)


def finish_kernel(rlo, rhi, rblo, rbhi, olo, ohi, oblo, obhi, fin, edge, vel, dif, gcp, cb, ymid, ct, ub, msg, gc, pad, v, d, zs, jp, sems):
    copies = []
    for side, z in enumerate((0, LZ - 1)):
        copies.append(pltpu.make_async_copy(vel.at[:, z], v.at[side], sems.at[side, 0]))
        copies.append(pltpu.make_async_copy(dif.at[z], d.at[side], sems.at[side, 1]))
    for copy in copies:
        copy.start()
    slice_index = lax.axis_index("tm")
    for side, (rec, recb, own, ownb) in enumerate(((rlo, rblo, olo, oblo), (rhi, rbhi, ohi, obhi))):
        for r in range(0, NY, 8):
            pad[side, TOP + r : TOP + r + 8, :] = (
                own[NY + r : NY + r + 8, :] + ownb[r : r + 8, :] * rec[r : r + 8, :]
            )
        wrap_rows(pad, side)
        copies[2 * side].wait()
        copies[2 * side + 1].wait()
        for r in range(0, NY, 8):
            rows = slice(r, r + 8)
            c, w, e, s, n = plane(pad, side, r)
            outside = rec[NY + r : NY + r + 8, :] + recb[r : r + 8, :] * own[r : r + 8, :]
            inside = edge[side, rows, :]
            b, t = (outside, inside) if side == 0 else (inside, outside)
            last = advanced(
                c, w, e, s, n, b, t,
                v[side, 0, rows, :], v[side, 1, rows, :], v[side, 2, rows, :], d[side, rows, :],
            )
            near = fin[5 * side, rows, :] + edge[2 + side, rows, :] * c
            ub[3 * side, rows, :] = last
            ub[1 + side, rows, :] = near
            put_columns(zs, slice(side * NY + r, side * NY + r + 8), last + near)
    lane = lax.broadcasted_iota(jnp.int32, (128, 128), 1)
    halo_lo = jnp.concatenate([rlo[2 * NY : MSG, 128 * i : 128 * i + 128] for i in range(8)], axis=0)
    halo_hi = jnp.concatenate([rhi[2 * NY : MSG, 128 * i : 128 * i + 128] for i in range(8)], axis=0)
    for b in range(4):
        rows = slice(128 * b, 128 * b + 128)
        t = halved_x(
            jnp.concatenate(
                [
                    jnp.concatenate([paired(zs, i, 0, 32), ymid[i], paired(zs, i, NY, 32)], axis=0)
                    for i in (2 * b, 2 * b + 1)
                ],
                axis=1,
            )
        )
        hl = pltpu.roll(halo_lo, (128 - 32 * b) % 128, 1) if b else halo_lo
        hh = pltpu.roll(halo_hi, (96 - 32 * b) % 128, 1) if b != 3 else halo_hi
        halo = jnp.where(lane < 32, hl, hh)
        g = gcp[rows, :] + cb[rows, :] * halo
        g = jnp.where(slice_index == 0, 0.0, g)
        gc[rows, :] = g
        jp[8 + 128 * b : 136 + 128 * b, :] = t - g
    jp[0:8, :] = jp[CX : CX + 8, :]
    jp[CX + 8 : CX + 24, :] = jp[8:24, :]
    comp = slice_index // 2
    first = pl.multiple_of((slice_index % 2) * 16, 16)
    for i in range(BLOCKS):
        msg[i, 0:WIN, :] = jp[XB * i : XB * i + WIN, :]
        msg[i, WIN : WIN + 16, :] = ct[comp, pl.ds(first + XB * i, 16), :]


def finish(messages, fin, edge, velocity, diffusivity, gcp, cb, ymid, ct):
    return pl.pallas_call(
        finish_kernel,
        out_shape=[
            jax.ShapeDtypeStruct((4, NY, NX), F32),
            jax.ShapeDtypeStruct((BLOCKS, WIN + 16, CL), F32),
            jax.ShapeDtypeStruct((CX, CL), F32),
        ],
        in_specs=[whole()] * 10 + [remains()] * 2 + [whole()] * 4,
        out_specs=[whole()] * 3,
        scratch_shapes=[
            pltpu.VMEM((2, PADDED, NX), F32),
            pltpu.VMEM((2, 3, NY, NX), F32),
            pltpu.VMEM((2, NY, NX), F32),
            pltpu.VMEM((8, 2 * NY, 128), F32),
            pltpu.VMEM((CX + 24, CL), F32),
            pltpu.SemaphoreType.DMA((2, 2)),
        ],
        compiler_params=params(24),
        name="finish",
    )(*messages, fin, edge, velocity, diffusivity, gcp, cb, ymid, ct)


HALO = 13
SHARED = ((0, 6, 96), (1, 5, 64), (2, 4, 32))


def pick_kernel(got, up, down):
    lane = lax.broadcasted_iota(jnp.int32, (WIN, CL), 1)

    def coef(i, slab):
        return jnp.concatenate([got[QUAD * (2 * i + h) + slab, WIN : WIN + 16, :] for h in range(2)], axis=0)

    for out, near, far in ((up, 3, 2), (down, 0, 1)):
        for j in range(4):
            out[j] = got[QUAD * j + near, 0:WIN, :]
            out[7 + j] = coef(j, near)
        for j, other, width in SHARED:
            mine = lane >= CL - width if near == 3 else lane < width
            turn = CL - width if near == 3 else width
            out[4 + j] = jnp.where(
                mine, got[QUAD * j + far, 0:WIN, :], pltpu.roll(got[QUAD * other + near, 0:WIN, :], turn, 1)
            )
        for j in range(2):
            mine = lane >= 64 if near == 3 else lane < 64
            out[11 + j] = jnp.where(mine, coef(2 * j, far), pltpu.roll(coef(2 * j + 1, far), 64, 1))


def pick(got):
    halo = jax.ShapeDtypeStruct((HALO, WIN, CL), F32)
    return pl.pallas_call(
        pick_kernel,
        out_shape=[halo, halo],
        in_specs=[whole()],
        out_specs=[whole(), whole()],
        compiler_params=params(16),
        name="pick",
    )(got)


LANES = 8 * CL


def chain_kernel(got, below, above, out, src, cf, e):
    for j in range(7):
        for q in range(QUAD):
            src[j, :, (2 + q) * CL : (3 + q) * CL] = got[QUAD * j + q, 0:WIN, :]
        for halo, near, far in ((below, 1, 0), (above, 6, 7)):
            if j < 4:
                src[j, :, near * CL : near * CL + CL] = halo[j]
            if j >= 3:
                src[j, :, far * CL : far * CL + CL] = jnp.zeros((WIN, CL), F32)
    for halo, near, far in ((below, 1, 0), (above, 6, 7)):
        for j, other, width in SHARED:
            turn = width if near == 1 else CL - width
            src[j, :, far * CL : far * CL + CL] = halo[4 + j]
            src[other, :, near * CL : near * CL + CL] = pltpu.roll(halo[4 + j], turn, 1)
    for block in range(8):
        lanes = slice(block * CL, block * CL + CL)
        halo = below if block < 2 else above
        for half in range(2):
            rows = slice(16 * half, 16 * half + 16)
            if block in (1, 6):
                parts = [halo[7 + i, rows, :] for i in range(4)]
            elif block in (0, 7):
                parts = [
                    pltpu.roll(halo[11 + i // 2, rows, :], 64, 1) if i % 2 else halo[11 + i // 2, rows, :]
                    for i in range(4)
                ]
            else:
                parts = [got[QUAD * (2 * i + half) + block - 2, WIN : WIN + 16, :] for i in range(4)]
            for i, value in enumerate(coarse_coefs(*parts)):
                cf[i, rows, lanes] = value
    for q in range(QUAD):
        out[q] = jnp.zeros((XB, CL), F32)
    e[...] = src[0]
    for k in range(1, GROUPS):
        c = e[...]
        s, n = y_rolled(c, LANES, 1)
        w, x = pltpu.roll(c, 1, 0), pltpu.roll(c, WIN - 1, 0)
        b, t = pltpu.roll(c, 32, 1), pltpu.roll(c, LANES - 32, 1)
        y = c + (
            (cf[0] * (w - c) + cf[1] * (x - c))
            + (cf[2] * (s - c) + cf[3] * (n - c))
            + (cf[4] * (b - c) + cf[5] * (t - c))
        )
        for q in range(QUAD):
            out[QUAD * k + q] = y[8 : 8 + XB, (2 + q) * CL : (3 + q) * CL]
        if k < GROUPS - 1:
            e[...] = y + src[k]


def chain(got, below, above):
    return pl.pallas_call(
        chain_kernel,
        out_shape=jax.ShapeDtypeStruct((BLOCKS, XB, CL), F32),
        in_specs=[whole()] * 3,
        out_specs=whole(),
        scratch_shapes=[
            pltpu.VMEM((7, WIN, LANES), F32),
            pltpu.VMEM((6, WIN, LANES), F32),
            pltpu.VMEM((WIN, LANES), F32),
        ],
        compiler_params=params(24),
        name="chain",
    )(got, below, above)


def result_kernel(y, gc, fin, ub, out, buf, sems):
    copy_y = table((256, CL), lambda r, c: r // 2 == c)
    copy_x = table((128, 256), lambda r, c: r == c // 2)
    copies = []
    for b in range(4):
        rows = slice(128 * b, 128 * b + 128)
        cols = slice(256 * b, 256 * b + 256)
        parts = split3(y[rows, :] - gc[rows, :])
        fine = sum(dot(dot(copy_y, p, 1, 1).astype(BF16), copy_x, 1, 0) for p in parts)
        for z in range(LZ):
            base = fin[z - 1, :, cols] if 2 <= z < 6 else ub[z if z < 2 else z - 4, :, cols]
            buf[z, :, cols] = base + fine[z // 2 * NY : z // 2 * NY + NY, :]
        copies.append(pltpu.make_async_copy(buf.at[:, :, cols], out.at[:, :, cols], sems.at[b]))
        copies[b].start()
    for copy in copies:
        copy.wait()


def result(y, gc, fin, ub):
    return pl.pallas_call(
        result_kernel,
        out_shape=jax.ShapeDtypeStruct((LZ, NY, NX), F32),
        in_specs=[whole()] * 4,
        out_specs=remains(),
        scratch_shapes=[pltpu.VMEM((LZ, NY, NX), F32), pltpu.SemaphoreType.DMA((4,))],
        compiler_params=params(16),
        name="result",
    )(y, gc, fin, ub)


def shift(value, axes, by):
    count = lax.axis_size(axes)
    return lax.ppermute(value, axes, [(i, i + by) for i in range(count) if 0 <= i + by < count])


def shift_copy(value, by):
    slabs = 16
    pairs = []
    for t in range(GROUPS):
        for i in range(slabs):
            if 0 <= i + by < slabs:
                t_from = t if i // 2 == (i + by) // 2 else t ^ 1
                pairs.append((t_from * slabs + i, t * slabs + i + by))
    return lax.ppermute(value, ("tm",) + SPACE, pairs)


def shards(state_old, velocity, diffusivity):
    state = state_old[0]
    olo, ohi, oblo, obhi = edges(state, velocity, diffusivity)
    rlo = shift(ohi, SPACE, 1)
    rhi = shift(olo, SPACE, -1)
    rblo = shift_copy(obhi, 1)
    rbhi = shift_copy(oblo, -1)
    fin, edge, ct, gcp, cb, ymid = interior(state, velocity, diffusivity)
    messages = (rlo, rhi, rblo, rbhi, olo, ohi, oblo, obhi)
    ub, msg, gc = finish(messages, fin, edge, velocity, diffusivity, gcp, cb, ymid, ct)
    got = lax.all_to_all(msg, GROUP, 0, 0)
    up, down = pick(got)
    below = shift(up, "px", 1)
    above = shift(down, "px", -1)
    back = lax.all_to_all(chain(got, below, above), GROUP, 0, 0)
    return result(back.reshape(CX, CL), gc, fin, ub)[None]


def solution(mesh):
    fine_mesh = Mesh(mesh.devices.reshape(GROUPS, 4, 2, 2), ("tm",) + SPACE)
    return jax.shard_map(
        shards,
        mesh=fine_mesh,
        in_specs=(
            P("tm", SPACE, None, None),
            P(None, SPACE, None, None),
            P(SPACE, None, None),
        ),
        out_specs=P("tm", SPACE, None, None),
        check_vma=False,
    )
```

```python
import jax
import jax.numpy as jnp
from jax import lax
from jax.experimental import pallas as pl
from jax.experimental.pallas import tpu as pltpu
from jax.sharding import Mesh
from jax.sharding import PartitionSpec as P

F32 = jnp.float32
BF16 = jnp.bfloat16
NY, NX = 64, 1024
LZ = 8
CX, CL = 512, 128
GROUPS = 8
QUAD = 4
BLOCKS = GROUPS * QUAD
XB = CX // BLOCKS
WIN = XB + 16
TOP = 8
PADDED = NY + 16
SPACE = ("px", "pz", "core")
GROUP = ("tm", "pz", "core")


def params(mib):
    return pltpu.CompilerParams(vmem_limit_bytes=mib * 1024 * 1024)


def split3(x):
    hi = x.astype(BF16)
    rest = x - hi.astype(F32)
    mid = rest.astype(BF16)
    return hi, mid, (rest - mid.astype(F32)).astype(BF16)


def dot(a, b, ca, cb):
    return lax.dot_general(a, b, (((ca,), (cb,)), ((), ())), preferred_element_type=F32)


def table(shape, test):
    rows = lax.broadcasted_iota(jnp.int32, shape, 0)
    cols = lax.broadcasted_iota(jnp.int32, shape, 1)
    return test(rows, cols).astype(F32).astype(BF16)


def halved_x(part):
    halve = table((128, 256), lambda r, c: r == c // 2)
    return sum(dot(halve, p, 1, 1) for p in split3(part)) * 0.125


def put_columns(ref, at, value):
    for i in range(NX // 128):
        ref[i, at, :] = value[:, 128 * i : 128 * i + 128]


def paired(ref, column, first, rows):
    return ref[column, pl.ds(first, rows, 2), :] + ref[column, pl.ds(first + 1, rows, 2), :]


def advanced(c, w, e, s, n, b, t, ax, ay, az, k):
    lap = ((w + e) + (s + n)) + ((b + t) - 6.0 * c)
    dx = jnp.abs(ax) * (jnp.where(ax > 0, w, e) - c)
    dy = jnp.abs(ay) * (jnp.where(ay > 0, s, n) - c)
    dz = jnp.abs(az) * (jnp.where(az > 0, b, t) - c)
    return (c + k * lap) + ((dx + dy) + dz)


def wrap_rows(ref, z):
    ref[z, TOP - 1 : TOP, :] = ref[z, TOP + NY - 1 : TOP + NY, :]
    ref[z, TOP + NY : TOP + NY + 1, :] = ref[z, TOP : TOP + 1, :]


def plane(ref, z, r):
    c = ref[z, TOP + r : TOP + r + 8, :]
    s = ref[z, TOP + r - 1 : TOP + r + 7, :]
    n = ref[z, TOP + r + 1 : TOP + r + 9, :]
    return c, pltpu.roll(c, 1, 1), pltpu.roll(c, NX - 1, 1), s, n


def coarse_coefs(vx, vy, vz, k):
    half = 0.5 * k
    out = []
    for a in (vx, vy, vz):
        out += [half + jnp.maximum(a, 0.0), half - jnp.minimum(a, 0.0)]
    return out


def y_rolled(u, width, axis):
    y = lax.broadcasted_iota(jnp.int32, u.shape, axis) % 32
    s = jnp.where(y == 0, pltpu.roll(u, width - 31, axis), pltpu.roll(u, 1, axis))
    n = jnp.where(y == 31, pltpu.roll(u, 31, axis), pltpu.roll(u, width - 1, axis))
    return s, n


FAR = 2 * NY + 16
NEAR = FAR + NY
CROWS = CX + 32


def edge_is_top(kind):
    return lax.axis_index("core") == kind


def edges_kernel(st, vel, dif, near, far, factor, pad, inner, v, d, zs, sems):
    copies = []
    tops = [edge_is_top(kind) for kind in range(2)]
    for kind, top in enumerate(tops):
        z, beside = jnp.where(top, LZ - 1, 0), jnp.where(top, LZ - 2, 1)
        pairs = (
            (st.at[z], pad.at[kind, TOP : TOP + NY, :]),
            (vel.at[:, z], v.at[kind]),
            (dif.at[z], d.at[kind]),
            (st.at[beside], inner.at[kind]),
        )
        copies.append([pltpu.make_async_copy(a, b, sems.at[kind, i]) for i, (a, b) in enumerate(pairs)])
    for group in copies:
        for copy in group:
            copy.start()
    for kind, top in enumerate(tops):
        out = (near, far)[kind]
        for copy in copies[kind]:
            copy.wait()
        wrap_rows(pad, kind)
        for r in range(0, NY, 8):
            rows = slice(r, r + 8)
            c, w, e, s, n = plane(pad, kind, r)
            inside = inner[kind, rows, :]
            ax, ay, k = v[kind, 0, rows, :], v[kind, 1, rows, :], d[kind, rows, :]
            up = jnp.where(top, v[kind, 2, rows, :], -v[kind, 2, rows, :])
            out[r : r + 8, :] = c
            out[NY + r : NY + r + 8, :] = advanced(c, w, e, s, n, inside, jnp.zeros_like(c), ax, ay, up, k)
            b = k - jnp.minimum(up, 0.0)
            if kind == 0:
                near[FAR + r : FAR + r + 8, :] = b
            else:
                factor[rows, :] = b
            put_columns(zs, slice(kind * NY + r, kind * NY + r + 8), c + inside)
    lane = lax.broadcasted_iota(jnp.int32, (128, 128), 1)
    cnear = jnp.zeros((128, 128), F32)
    cfar = jnp.zeros((128, 128), F32)
    for b in range(4):
        part = jnp.concatenate([paired(zs, 2 * b + i, 0, 64) for i in range(2)], axis=1)
        t = halved_x(jnp.concatenate([part, jnp.zeros_like(part)], axis=0))
        tn = jnp.where(lane < 32, t, 0.0)
        tf = jnp.where((lane >= 32) & (lane < 64), t, 0.0)
        cnear += pltpu.roll(tn, 32 * b, 1) if b else tn
        cfar += pltpu.roll(tf, (32 * b - 32) % 128, 1) if b != 1 else tf
    for i in range(8):
        near[2 * NY : FAR, 128 * i : 128 * i + 128] = cnear[16 * i : 16 * i + 16, :]
        far[2 * NY : FAR, 128 * i : 128 * i + 128] = cfar[16 * i : 16 * i + 16, :]


def whole():
    return pl.BlockSpec(memory_space=pltpu.VMEM)


def remains():
    return pl.BlockSpec(memory_space=pltpu.HBM)


def edges(state, velocity, diffusivity):
    return pl.pallas_call(
        edges_kernel,
        out_shape=[
            jax.ShapeDtypeStruct((NEAR, NX), F32),
            jax.ShapeDtypeStruct((FAR, NX), F32),
            jax.ShapeDtypeStruct((NY, NX), F32),
        ],
        in_specs=[remains()] * 3,
        out_specs=[whole()] * 3,
        scratch_shapes=[
            pltpu.VMEM((2, PADDED, NX), F32),
            pltpu.VMEM((2, NY, NX), F32),
            pltpu.VMEM((2, 3, NY, NX), F32),
            pltpu.VMEM((2, NY, NX), F32),
            pltpu.VMEM((8, 2 * NY, 128), F32),
            pltpu.SemaphoreType.DMA((2, 4)),
        ],
        compiler_params=params(58),
        name="edges",
    )(state, velocity, diffusivity)


def quad_rank():
    return lax.axis_index("pz") * 2 + lax.axis_index("core")


def interior_kernel(st, vel, dif, fin, edge, bound, w0, w1, w2, w3, gcp, cb, ymid, u, u1, ct, v, d, zs, ct0, usem, sems):
    def layer(z):
        return (
            pltpu.make_async_copy(vel.at[:, z], v.at[:, z], sems.at[z, 0]),
            pltpu.make_async_copy(dif.at[z], d.at[z], sems.at[z, 1]),
        )

    copy = pltpu.make_async_copy(st, u.at[:, TOP : TOP + NY, :], usem)
    copy.start()
    for z in (1, 2, 3, 4, 5, 6, 0, 7):
        for part in layer(z):
            part.start()
    copy.wait()
    for z in range(LZ):
        wrap_rows(u, z)
    for zc in range(4):
        for r in range(0, NY, 8):
            here = slice(TOP + r, TOP + r + 8)
            put_columns(zs.at[4], slice(zc * NY + r, zc * NY + r + 8), u[2 * zc, here, :] + u[2 * zc + 1, here, :])

    def first(z, _):
        for part in layer(z):
            part.wait()
        for r in range(0, NY, 8):
            rows = slice(r, r + 8)
            here = slice(TOP + r, TOP + r + 8)
            c, w, e, s, n = plane(u, z, r)
            u1[z, here, :] = advanced(
                c, w, e, s, n, u[z - 1, here, :], u[z + 1, here, :],
                v[0, z, rows, :], v[1, z, rows, :], v[2, z, rows, :], d[z, rows, :],
            )
        wrap_rows(u1, z)
        return 0

    lax.fori_loop(1, LZ - 1, first, 0)
    u1[0, TOP : TOP + NY, :] = jnp.zeros((NY, NX), F32)
    u1[LZ - 1, TOP : TOP + NY, :] = jnp.zeros((NY, NX), F32)
    edge[0] = u1[1, TOP : TOP + NY, :]
    edge[1] = u1[LZ - 2, TOP : TOP + NY, :]

    def second(z, _):
        for r in range(0, NY, 8):
            rows = slice(r, r + 8)
            here = slice(TOP + r, TOP + r + 8)
            c, w, e, s, n = plane(u1, z, r)
            fin[z - 1, rows, :] = advanced(
                c, w, e, s, n, u1[z - 1, here, :], u1[z + 1, here, :],
                v[0, z, rows, :], v[1, z, rows, :], v[2, z, rows, :], d[z, rows, :],
            )
        return 0

    lax.fori_loop(1, LZ - 1, second, 0)
    edge[2] = d[1] + jnp.maximum(v[2, 1], 0.0)
    edge[3] = d[LZ - 2] - jnp.minimum(v[2, LZ - 2], 0.0)
    for zc in (1, 2):
        for r in range(0, NY, 8):
            rows = slice(r, r + 8)
            put_columns(zs.at[5], slice((zc - 1) * NY + r, (zc - 1) * NY + r + 8), fin[2 * zc - 1, rows, :] + fin[2 * zc, rows, :])
    for i in range(8):
        ymid[i] = paired(zs.at[5], i, 0, 64)

    for side, z in enumerate((0, LZ - 1)):
        for part in layer(z):
            part.wait()
        for comp in range(3):
            bound[side, comp] = v[comp, z]
        bound[side, 3] = d[z]
    for zc in range(4):
        for r in range(0, NY, 8):
            to, rows = slice(zc * NY + r, zc * NY + r + 8), slice(r, r + 8)
            for comp in range(3):
                put_columns(zs.at[comp], to, v[comp, 2 * zc, rows, :] + v[comp, 2 * zc + 1, rows, :])
            put_columns(zs.at[3], to, d[2 * zc, rows, :] + d[2 * zc + 1, rows, :])
    for comp in range(5):
        for b in range(4):
            t = halved_x(jnp.concatenate([paired(zs.at[comp], 2 * b + i, 0, 128) for i in range(2)], axis=1))
            if comp < 4:
                ct[comp, 8 + 128 * b : 136 + 128 * b, :] = t
            else:
                ct0[8 + 128 * b : 136 + 128 * b, :] = t
    for comp in range(4):
        ct[comp, 0:8, :] = ct[comp, CX : CX + 8, :]
        ct[comp, CX + 8 : CX + 32, :] = ct[comp, 8:32, :]
    mine = quad_rank()
    for i, out in enumerate((w0, w1, w2, w3)):
        block = lax.axis_index("tm") * QUAD + (mine ^ i)
        for comp in range(4):
            out[comp] = ct[comp, pl.ds(pl.multiple_of(block * XB, XB), WIN), :]
    ct0[0:8, :] = ct0[CX : CX + 8, :]
    ct0[CX + 8 : CX + 16, :] = ct0[8:16, :]
    lane = lax.broadcasted_iota(jnp.int32, (64, CL), 1)
    for r in range(0, CX, 64):
        c = ct0[8 + r : 72 + r, :]
        xl, xh, yl, yh, zl, zh = coarse_coefs(*(ct[i, 8 + r : 72 + r, :] for i in range(4)))
        s, n = y_rolled(c, CL, 1)
        b = jnp.where(lane < 32, 0.0, pltpu.roll(c, 32, 1))
        t = jnp.where(lane >= 96, 0.0, pltpu.roll(c, 96, 1))
        w = ct0[7 + r : 71 + r, :]
        e = ct0[9 + r : 73 + r, :]
        gcp[r : r + 64, :] = c + (
            (xl * (w - c) + xh * (e - c)) + (yl * (s - c) + yh * (n - c)) + (zl * (b - c) + zh * (t - c))
        )
        cb[r : r + 64, :] = jnp.where(lane < 32, zl, jnp.where(lane >= 96, zh, 0.0))


def interior(state, velocity, diffusivity):
    small = jax.ShapeDtypeStruct((CX, CL), F32)
    window = jax.ShapeDtypeStruct((4, WIN, CL), F32)
    return pl.pallas_call(
        interior_kernel,
        out_shape=[
            jax.ShapeDtypeStruct((LZ - 2, NY, NX), F32),
            jax.ShapeDtypeStruct((4, NY, NX), F32),
            jax.ShapeDtypeStruct((2, 4, NY, NX), F32),
            window,
            window,
            window,
            window,
            small,
            small,
            jax.ShapeDtypeStruct((8, 64, 128), F32),
        ],
        in_specs=[remains()] * 3,
        out_specs=[whole()] * 10,
        scratch_shapes=[
            pltpu.VMEM((LZ, PADDED, NX), F32),
            pltpu.VMEM((LZ, PADDED, NX), F32),
            pltpu.VMEM((4, CROWS, CL), F32),
            pltpu.VMEM((3, LZ, NY, NX), F32),
            pltpu.VMEM((LZ, NY, NX), F32),
            pltpu.VMEM((6, 8, 4 * NY, 128), F32),
            pltpu.VMEM((CX + 16, CL), F32),
            pltpu.SemaphoreType.DMA,
            pltpu.SemaphoreType.DMA((LZ, 2)),
        ],
        compiler_params=params(48),
        cost_estimate=pl.CostEstimate(flops=60_000_000, bytes_accessed=20_000_000, transcendentals=0),
        name="interior",
    )(state, velocity, diffusivity)


def finish_kernel(rnear, rfar, rfac, onear, ofar, ofac, fin, edge, bound, gcp, cb, ymid, ub, msg, gc, pad, zs, jp):
    for kind, (rec, own, recb, ownb, at) in enumerate(
        ((rnear, onear, rnear, onear, FAR), (rfar, ofar, rfac, ofac, 0))
    ):
        top = edge_is_top(kind)
        side = jnp.where(top, 1, 0)
        for r in range(0, NY, 8):
            pad[kind, TOP + r : TOP + r + 8, :] = (
                own[NY + r : NY + r + 8, :] + ownb[at + r : at + r + 8, :] * rec[r : r + 8, :]
            )
        wrap_rows(pad, kind)
        for r in range(0, NY, 8):
            rows = slice(r, r + 8)
            c, w, e, s, n = plane(pad, kind, r)
            outside = rec[NY + r : NY + r + 8, :] + recb[at + r : at + r + 8, :] * own[r : r + 8, :]
            inside = edge[side, rows, :]
            ax, ay, az, k = (bound[side, i, rows, :] for i in range(4))
            last = advanced(c, w, e, s, n, inside, outside, ax, ay, jnp.where(top, az, -az), k)
            near = fin[5 * side, rows, :] + edge[2 + side, rows, :] * c
            ub[3 * side, rows, :] = last
            ub[1 + side, rows, :] = near
            put_columns(zs.at[side], rows, last + near)
    lane = lax.broadcasted_iota(jnp.int32, (128, 128), 1)
    hnear = jnp.concatenate([rnear[2 * NY : FAR, 128 * i : 128 * i + 128] for i in range(8)], axis=0)
    hfar = jnp.concatenate([rfar[2 * NY : FAR, 128 * i : 128 * i + 128] for i in range(8)], axis=0)
    first_core = lax.axis_index("core") == 0
    halo_lo, halo_hi = jnp.where(first_core, hfar, hnear), jnp.where(first_core, hnear, hfar)
    for b in range(4):
        rows = slice(128 * b, 128 * b + 128)
        t = halved_x(
            jnp.concatenate(
                [
                    jnp.concatenate([paired(zs.at[0], i, 0, 32), ymid[i], paired(zs.at[1], i, 0, 32)], axis=0)
                    for i in (2 * b, 2 * b + 1)
                ],
                axis=1,
            )
        )
        hl = pltpu.roll(halo_lo, (128 - 32 * b) % 128, 1) if b else halo_lo
        hh = pltpu.roll(halo_hi, (96 - 32 * b) % 128, 1) if b != 3 else halo_hi
        halo = jnp.where(lane < 32, hl, hh)
        g = gcp[rows, :] + cb[rows, :] * halo
        g = jnp.where(lax.axis_index("tm") == 0, 0.0, g)
        gc[rows, :] = g
        jp[8 + 128 * b : 136 + 128 * b, :] = t - g
    jp[0:8, :] = jp[CX : CX + 8, :]
    jp[CX + 8 : CX + 24, :] = jp[8:24, :]
    for i in range(BLOCKS):
        msg[i] = jp[XB * i : XB * i + WIN, :]


def finish(messages, fin, edge, bound, gcp, cb, ymid):
    return pl.pallas_call(
        finish_kernel,
        out_shape=[
            jax.ShapeDtypeStruct((4, NY, NX), F32),
            jax.ShapeDtypeStruct((BLOCKS, WIN, CL), F32),
            jax.ShapeDtypeStruct((CX, CL), F32),
        ],
        in_specs=[whole()] * 12,
        out_specs=[whole()] * 3,
        scratch_shapes=[
            pltpu.VMEM((2, PADDED, NX), F32),
            pltpu.VMEM((2, 8, NY, 128), F32),
            pltpu.VMEM((CX + 24, CL), F32),
        ],
        compiler_params=params(24),
        name="finish",
    )(*messages, fin, edge, bound, gcp, cb, ymid)


HALO = 13
SHARED = ((0, 6, 96), (1, 5, 64), (2, 4, 32))


def pick_kernel(got, w0, w1, w2, w3, even, odd, coefs):
    lane = lax.broadcasted_iota(jnp.int32, (WIN, CL), 1)
    mine = quad_rank()
    for i, window in enumerate((w0, w1, w2, w3)):
        coefs[mine ^ i] = window[...]
    for parity, out in enumerate((even, odd)):
        up = lax.rem(lax.axis_index("px"), 2) == parity
        near, far = jnp.where(up, 3, 0), jnp.where(up, 2, 1)

        def shared(main, other, width):
            return jnp.where(
                up,
                jnp.where(lane >= CL - width, main, pltpu.roll(other, CL - width, 1)),
                jnp.where(lane < width, main, pltpu.roll(other, width, 1)),
            )

        for j in range(4):
            out[j] = got[QUAD * j + near]
            out[7 + j] = coefs[near, j]
        for j, other, width in SHARED:
            out[4 + j] = shared(got[QUAD * j + far], got[QUAD * other + near], width)
        for j in range(2):
            out[11 + j] = shared(coefs[far, 2 * j], coefs[far, 2 * j + 1], 64)


def pick(got, windows):
    halo = jax.ShapeDtypeStruct((HALO, WIN, CL), F32)
    return pl.pallas_call(
        pick_kernel,
        out_shape=[halo, halo],
        in_specs=[whole()] * 5,
        out_specs=[whole(), whole()],
        scratch_shapes=[pltpu.VMEM((QUAD, 4, WIN, CL), F32)],
        compiler_params=params(16),
        name="pick",
    )(got, *windows)


LANES = 8 * CL


def chain_kernel(got, w0, w1, w2, w3, even, odd, out, src, cf, e):
    first = lax.rem(lax.axis_index("px"), 2) == 0

    def below(i):
        return jnp.where(first, odd[i], even[i])

    def above(i):
        return jnp.where(first, even[i], odd[i])

    def put_coefs(values, lanes):
        for i, value in enumerate(coarse_coefs(*values)):
            cf[i, :, lanes] = value

    for j in range(7):
        for q in range(QUAD):
            src[j, :, (2 + q) * CL : (3 + q) * CL] = got[QUAD * j + q]
        for halo, near, far in ((below, 1, 0), (above, 6, 7)):
            if j < 4:
                src[j, :, near * CL : near * CL + CL] = halo(j)
            if j >= 3:
                src[j, :, far * CL : far * CL + CL] = jnp.zeros((WIN, CL), F32)
    for halo, near, far in ((below, 1, 0), (above, 6, 7)):
        for j, other, width in SHARED:
            turn = width if near == 1 else CL - width
            block = halo(4 + j)
            src[j, :, far * CL : far * CL + CL] = block
            src[other, :, near * CL : near * CL + CL] = pltpu.roll(block, turn, 1)
        put_coefs([halo(7 + i) for i in range(4)], slice(near * CL, near * CL + CL))
        pairs = [halo(11), halo(12)]
        put_coefs(
            [pairs[0], pltpu.roll(pairs[0], 64, 1), pairs[1], pltpu.roll(pairs[1], 64, 1)],
            slice(far * CL, far * CL + CL),
        )
    mine = quad_rank()
    for i, window in enumerate((w0, w1, w2, w3)):
        lanes = pl.ds(pl.multiple_of((2 + (mine ^ i)) * CL, CL), CL)
        put_coefs([window[comp] for comp in range(4)], lanes)
    for q in range(QUAD):
        out[q] = jnp.zeros((XB, CL), F32)
    e[...] = src[0]
    for k in range(1, GROUPS):
        c = e[...]
        s, n = y_rolled(c, LANES, 1)
        w, x = pltpu.roll(c, 1, 0), pltpu.roll(c, WIN - 1, 0)
        b, t = pltpu.roll(c, 32, 1), pltpu.roll(c, LANES - 32, 1)
        y = c + (
            (cf[0] * (w - c) + cf[1] * (x - c))
            + (cf[2] * (s - c) + cf[3] * (n - c))
            + (cf[4] * (b - c) + cf[5] * (t - c))
        )
        for q in range(QUAD):
            out[QUAD * k + q] = y[8 : 8 + XB, (2 + q) * CL : (3 + q) * CL]
        if k < GROUPS - 1:
            e[...] = y + src[k]


def chain(got, windows, even, odd):
    return pl.pallas_call(
        chain_kernel,
        out_shape=jax.ShapeDtypeStruct((BLOCKS, XB, CL), F32),
        in_specs=[whole()] * 7,
        out_specs=whole(),
        scratch_shapes=[
            pltpu.VMEM((7, WIN, LANES), F32),
            pltpu.VMEM((6, WIN, LANES), F32),
            pltpu.VMEM((WIN, LANES), F32),
        ],
        compiler_params=params(24),
        name="chain",
    )(got, *windows, even, odd)


def result_kernel(y, gc, fin, ub, out, buf, sems):
    copy_y = table((256, CL), lambda r, c: r // 2 == c)
    copy_x = table((128, 256), lambda r, c: r == c // 2)
    copies = []
    for b in range(4):
        rows = slice(128 * b, 128 * b + 128)
        cols = slice(256 * b, 256 * b + 256)
        parts = split3(y[rows, :] - gc[rows, :])
        fine = sum(dot(dot(copy_y, p, 1, 1).astype(BF16), copy_x, 1, 0) for p in parts)
        for z in range(LZ):
            base = fin[z - 1, :, cols] if 2 <= z < 6 else ub[z if z < 2 else z - 4, :, cols]
            buf[z, :, cols] = base + fine[z // 2 * NY : z // 2 * NY + NY, :]
        copies.append(pltpu.make_async_copy(buf.at[:, :, cols], out.at[:, :, cols], sems.at[b]))
        copies[b].start()
    for copy in copies:
        copy.wait()


def result(y, gc, fin, ub):
    return pl.pallas_call(
        result_kernel,
        out_shape=jax.ShapeDtypeStruct((LZ, NY, NX), F32),
        in_specs=[whole()] * 4,
        out_specs=remains(),
        scratch_shapes=[pltpu.VMEM((LZ, NY, NX), F32), pltpu.SemaphoreType.DMA((4,))],
        compiler_params=params(16),
        name="result",
    )(y, gc, fin, ub)


def swap(value, axes, partner):
    pairs = [(i, partner(i)) for i in range(lax.axis_size(axes))]
    return lax.ppermute(value, axes, [(i, j) for i, j in pairs if j is not None])


def off_chip(i):
    j = i + 1 if i % 2 else i - 1
    return j if 0 <= j < 16 else None


def off_chip_copy(i):
    j = off_chip(i % 16)
    return None if j is None else (i // 16 ^ 1) * 16 + j


def quad_beside(i):
    j = i + 1 if i % 2 else i - 1
    return j if 0 <= j < 4 else None


def shards(state_old, velocity, diffusivity):
    state = state_old[0]
    onear, ofar, ofac = edges(state, velocity, diffusivity)
    rnear = swap(onear, SPACE, lambda i: i ^ 1)
    rfar = swap(ofar, SPACE, off_chip)
    rfac = swap(ofac, ("tm",) + SPACE, off_chip_copy)
    fin, edge, bound, w0, w1, w2, w3, gcp, cb, ymid = interior(state, velocity, diffusivity)
    windows = (
        w0,
        swap(w1, SPACE, lambda i: i ^ 1),
        swap(w2, SPACE, lambda i: i ^ 2),
        swap(w3, SPACE, lambda i: i ^ 3),
    )
    messages = (rnear, rfar, rfac, onear, ofar, ofac)
    ub, msg, gc = finish(messages, fin, edge, bound, gcp, cb, ymid)
    got = lax.all_to_all(msg, GROUP, 0, 0)
    even, odd = pick(got, windows)
    even = swap(even, "px", lambda i: i ^ 1)
    odd = swap(odd, "px", quad_beside)
    back = lax.all_to_all(chain(got, windows, even, odd), GROUP, 0, 0)
    return result(back.reshape(CX, CL), gc, fin, ub)[None]


def solution(mesh):
    fine_mesh = Mesh(mesh.devices.reshape(GROUPS, 4, 2, 2), ("tm",) + SPACE)
    return jax.shard_map(
        shards,
        mesh=fine_mesh,
        in_specs=(
            P("tm", SPACE, None, None),
            P(None, SPACE, None, None),
            P(SPACE, None, None),
        ),
        out_specs=P("tm", SPACE, None, None),
        check_vma=False,
    )
```

```python
import jax
import jax.numpy as jnp
from jax import lax
from jax.experimental import pallas as pl
from jax.experimental.pallas import tpu as pltpu
from jax.sharding import Mesh
from jax.sharding import PartitionSpec as P

F32 = jnp.float32
BF16 = jnp.bfloat16
NY, NX = 64, 1024
LZ = 8
CX, CL = 512, 128
GROUPS = 8
QUAD = 4
BLOCKS = GROUPS * QUAD
XB = CX // BLOCKS
WIN = XB + 16
TOP = 8
PADDED = NY + 16
SPACE = ("px", "pz", "core")
GROUP = ("tm", "pz", "core")


def params(mib):
    return pltpu.CompilerParams(vmem_limit_bytes=mib * 1024 * 1024)


def split3(x):
    hi = x.astype(BF16)
    rest = x - hi.astype(F32)
    mid = rest.astype(BF16)
    return hi, mid, (rest - mid.astype(F32)).astype(BF16)


def dot(a, b, ca, cb):
    return lax.dot_general(a, b, (((ca,), (cb,)), ((), ())), preferred_element_type=F32)


def table(shape, test):
    rows = lax.broadcasted_iota(jnp.int32, shape, 0)
    cols = lax.broadcasted_iota(jnp.int32, shape, 1)
    return test(rows, cols).astype(F32).astype(BF16)


def halved_x(part):
    halve = table((128, 256), lambda r, c: r == c // 2)
    return sum(dot(halve, p, 1, 1) for p in split3(part)) * 0.125


def put_columns(ref, at, value):
    for i in range(NX // 128):
        ref[i, at, :] = value[:, 128 * i : 128 * i + 128]


def paired(ref, column, first, rows):
    return ref[column, pl.ds(first, rows, 2), :] + ref[column, pl.ds(first + 1, rows, 2), :]


def advanced(c, w, e, s, n, b, t, ax, ay, az, k):
    lap = ((w + e) + (s + n)) + ((b + t) - 6.0 * c)
    dx = jnp.abs(ax) * (jnp.where(ax > 0, w, e) - c)
    dy = jnp.abs(ay) * (jnp.where(ay > 0, s, n) - c)
    dz = jnp.abs(az) * (jnp.where(az > 0, b, t) - c)
    return (c + k * lap) + ((dx + dy) + dz)


def wrap_rows(ref, z):
    ref[z, TOP - 1 : TOP, :] = ref[z, TOP + NY - 1 : TOP + NY, :]
    ref[z, TOP + NY : TOP + NY + 1, :] = ref[z, TOP : TOP + 1, :]


def plane(ref, z, r):
    c = ref[z, TOP + r : TOP + r + 8, :]
    s = ref[z, TOP + r - 1 : TOP + r + 7, :]
    n = ref[z, TOP + r + 1 : TOP + r + 9, :]
    return c, pltpu.roll(c, 1, 1), pltpu.roll(c, NX - 1, 1), s, n


def coarse_coefs(vx, vy, vz, k):
    half = 0.5 * k
    out = []
    for a in (vx, vy, vz):
        out += [half + jnp.maximum(a, 0.0), half - jnp.minimum(a, 0.0)]
    return out


def y_rolled(u, width, axis):
    y = lax.broadcasted_iota(jnp.int32, u.shape, axis) % 32
    s = jnp.where(y == 0, pltpu.roll(u, width - 31, axis), pltpu.roll(u, 1, axis))
    n = jnp.where(y == 31, pltpu.roll(u, 31, axis), pltpu.roll(u, width - 1, axis))
    return s, n


FAR = 2 * NY + 16
NEAR = FAR + NY
CROWS = CX + 32


def edge_is_top(kind):
    return lax.axis_index("core") == kind


def edges_kernel(st, vel, dif, near, far, factor, pad, inner, v, d, zs, sems):
    copies = []
    tops = [edge_is_top(kind) for kind in range(2)]
    for kind, top in enumerate(tops):
        z, beside = jnp.where(top, LZ - 1, 0), jnp.where(top, LZ - 2, 1)
        pairs = (
            (st.at[z], pad.at[kind, TOP : TOP + NY, :]),
            (vel.at[:, z], v.at[kind]),
            (dif.at[z], d.at[kind]),
            (st.at[beside], inner.at[kind]),
        )
        copies.append([pltpu.make_async_copy(a, b, sems.at[kind, i]) for i, (a, b) in enumerate(pairs)])
    for group in copies:
        for copy in group:
            copy.start()
    for kind, top in enumerate(tops):
        out = (near, far)[kind]
        for copy in copies[kind]:
            copy.wait()
        wrap_rows(pad, kind)
        for r in range(0, NY, 8):
            rows = slice(r, r + 8)
            c, w, e, s, n = plane(pad, kind, r)
            inside = inner[kind, rows, :]
            ax, ay, k = v[kind, 0, rows, :], v[kind, 1, rows, :], d[kind, rows, :]
            up = jnp.where(top, v[kind, 2, rows, :], -v[kind, 2, rows, :])
            out[r : r + 8, :] = c
            out[NY + r : NY + r + 8, :] = advanced(c, w, e, s, n, inside, jnp.zeros_like(c), ax, ay, up, k)
            b = k - jnp.minimum(up, 0.0)
            if kind == 0:
                near[FAR + r : FAR + r + 8, :] = b
            else:
                factor[rows, :] = b
            put_columns(zs, slice(kind * NY + r, kind * NY + r + 8), c + inside)
    lane = lax.broadcasted_iota(jnp.int32, (128, 128), 1)
    cnear = jnp.zeros((128, 128), F32)
    cfar = jnp.zeros((128, 128), F32)
    for b in range(4):
        part = jnp.concatenate([paired(zs, 2 * b + i, 0, 64) for i in range(2)], axis=1)
        t = halved_x(jnp.concatenate([part, jnp.zeros_like(part)], axis=0))
        tn = jnp.where(lane < 32, t, 0.0)
        tf = jnp.where((lane >= 32) & (lane < 64), t, 0.0)
        cnear += pltpu.roll(tn, 32 * b, 1) if b else tn
        cfar += pltpu.roll(tf, (32 * b - 32) % 128, 1) if b != 1 else tf
    for i in range(8):
        near[2 * NY : FAR, 128 * i : 128 * i + 128] = cnear[16 * i : 16 * i + 16, :]
        far[2 * NY : FAR, 128 * i : 128 * i + 128] = cfar[16 * i : 16 * i + 16, :]


def whole():
    return pl.BlockSpec(memory_space=pltpu.VMEM)


def remains():
    return pl.BlockSpec(memory_space=pltpu.HBM)


def edges(state, velocity, diffusivity):
    return pl.pallas_call(
        edges_kernel,
        out_shape=[
            jax.ShapeDtypeStruct((NEAR, NX), F32),
            jax.ShapeDtypeStruct((FAR, NX), F32),
            jax.ShapeDtypeStruct((NY, NX), F32),
        ],
        in_specs=[remains()] * 3,
        out_specs=[whole()] * 3,
        scratch_shapes=[
            pltpu.VMEM((2, PADDED, NX), F32),
            pltpu.VMEM((2, NY, NX), F32),
            pltpu.VMEM((2, 3, NY, NX), F32),
            pltpu.VMEM((2, NY, NX), F32),
            pltpu.VMEM((8, 2 * NY, 128), F32),
            pltpu.SemaphoreType.DMA((2, 4)),
        ],
        compiler_params=params(52),
        name="edges",
    )(state, velocity, diffusivity)


def quad_rank():
    return lax.axis_index("pz") * 2 + lax.axis_index("core")


def coefs_kernel(vel, dif, ct, w0, w1, w2, w3, v, zs, sems):
    def part(comp, zc):
        layers = slice(2 * zc, 2 * zc + 2)
        source = dif.at[layers] if comp == 3 else vel.at[comp, layers]
        return pltpu.make_async_copy(source, v.at[comp, layers], sems.at[comp, zc])

    for comp in range(4):
        for zc in range(4):
            part(comp, zc).start()
    for comp in range(4):
        for zc in range(4):
            part(comp, zc).wait()
            for r in range(0, NY, 8):
                rows = slice(r, r + 8)
                put_columns(
                    zs.at[comp], slice(zc * NY + r, zc * NY + r + 8), v[comp, 2 * zc, rows, :] + v[comp, 2 * zc + 1, rows, :]
                )
        for b in range(4):
            ct[comp, 8 + 128 * b : 136 + 128 * b, :] = halved_x(
                jnp.concatenate([paired(zs.at[comp], 2 * b + i, 0, 128) for i in range(2)], axis=1)
            )
        ct[comp, 0:8, :] = ct[comp, CX : CX + 8, :]
        ct[comp, CX + 8 : CX + 32, :] = ct[comp, 8:32, :]
    mine = quad_rank()
    for i, out in enumerate((w0, w1, w2, w3)):
        block = lax.axis_index("tm") * QUAD + (mine ^ i)
        for comp in range(4):
            out[comp] = ct[comp, pl.ds(pl.multiple_of(block * XB, XB), WIN), :]


def coefs(velocity, diffusivity):
    window = jax.ShapeDtypeStruct((4, WIN, CL), F32)
    return pl.pallas_call(
        coefs_kernel,
        out_shape=[jax.ShapeDtypeStruct((4, CROWS, CL), F32), window, window, window, window],
        in_specs=[remains()] * 2,
        out_specs=[whole()] * 5,
        scratch_shapes=[
            pltpu.VMEM((4, LZ, NY, NX), F32),
            pltpu.VMEM((4, 8, 4 * NY, 128), F32),
            pltpu.SemaphoreType.DMA((4, 4)),
        ],
        compiler_params=params(50),
        cost_estimate=pl.CostEstimate(flops=20_000_000, bytes_accessed=9_000_000, transcendentals=0),
        name="coefs",
    )(velocity, diffusivity)


def interior_kernel(st, vel, dif, ct, fin, edge, bound, gcp, cb, ymid, u, u1, v, d, zs, zf, ct0, usem, sems):
    def layer(z):
        return (
            pltpu.make_async_copy(vel.at[:, z], v.at[:, z], sems.at[z, 0]),
            pltpu.make_async_copy(dif.at[z], d.at[z], sems.at[z, 1]),
        )

    def state(z):
        return pltpu.make_async_copy(st.at[z], u.at[z, TOP : TOP + NY, :], usem.at[z])

    for z in range(3):
        state(z).start()
    for part in layer(1):
        part.start()
    for z in range(3, LZ):
        state(z).start()
        for part in layer(z - 1):
            part.start()
    bounds = []
    for side, z in enumerate((0, LZ - 1)):
        bounds.append(pltpu.make_async_copy(vel.at[:, z], bound.at[side, 0:3], sems.at[z, 0]))
        bounds.append(pltpu.make_async_copy(dif.at[z], bound.at[side, 3], sems.at[z, 1]))
    for copy in bounds:
        copy.start()
    for z in range(2):
        state(z).wait()
        wrap_rows(u, z)
    def first(z, _):
        state(z + 1).wait()
        wrap_rows(u, z + 1)
        for part in layer(z):
            part.wait()
        for r in range(0, NY, 8):
            rows = slice(r, r + 8)
            here = slice(TOP + r, TOP + r + 8)
            c, w, e, s, n = plane(u, z, r)
            u1[z, here, :] = advanced(
                c, w, e, s, n, u[z - 1, here, :], u[z + 1, here, :],
                v[0, z, rows, :], v[1, z, rows, :], v[2, z, rows, :], d[z, rows, :],
            )
        wrap_rows(u1, z)
        return 0

    lax.fori_loop(1, LZ - 1, first, 0)
    u1[0, TOP : TOP + NY, :] = jnp.zeros((NY, NX), F32)
    u1[LZ - 1, TOP : TOP + NY, :] = jnp.zeros((NY, NX), F32)
    edge[0] = u1[1, TOP : TOP + NY, :]
    edge[1] = u1[LZ - 2, TOP : TOP + NY, :]

    def second(z, _):
        for r in range(0, NY, 8):
            rows = slice(r, r + 8)
            here = slice(TOP + r, TOP + r + 8)
            c, w, e, s, n = plane(u1, z, r)
            fin[z - 1, rows, :] = advanced(
                c, w, e, s, n, u1[z - 1, here, :], u1[z + 1, here, :],
                v[0, z, rows, :], v[1, z, rows, :], v[2, z, rows, :], d[z, rows, :],
            )
        return 0

    lax.fori_loop(1, LZ - 1, second, 0)
    for copy in bounds:
        copy.wait()
    edge[2] = d[1] + jnp.maximum(v[2, 1], 0.0)
    edge[3] = d[LZ - 2] - jnp.minimum(v[2, LZ - 2], 0.0)
    for zc in (1, 2):
        for r in range(0, NY, 8):
            rows = slice(r, r + 8)
            put_columns(zf, slice((zc - 1) * NY + r, (zc - 1) * NY + r + 8), fin[2 * zc - 1, rows, :] + fin[2 * zc, rows, :])
    for i in range(8):
        ymid[i] = paired(zf, i, 0, 64)

    for zc in range(4):
        for r in range(0, NY, 8):
            here = slice(TOP + r, TOP + r + 8)
            put_columns(zs, slice(zc * NY + r, zc * NY + r + 8), u[2 * zc, here, :] + u[2 * zc + 1, here, :])
    for b in range(4):
        ct0[8 + 128 * b : 136 + 128 * b, :] = halved_x(
            jnp.concatenate([paired(zs, 2 * b + i, 0, 128) for i in range(2)], axis=1)
        )
    ct0[0:8, :] = ct0[CX : CX + 8, :]
    ct0[CX + 8 : CX + 16, :] = ct0[8:16, :]
    lane = lax.broadcasted_iota(jnp.int32, (64, CL), 1)
    for r in range(0, CX, 64):
        c = ct0[8 + r : 72 + r, :]
        xl, xh, yl, yh, zl, zh = coarse_coefs(*(ct[i, 8 + r : 72 + r, :] for i in range(4)))
        s, n = y_rolled(c, CL, 1)
        b = jnp.where(lane < 32, 0.0, pltpu.roll(c, 32, 1))
        t = jnp.where(lane >= 96, 0.0, pltpu.roll(c, 96, 1))
        w = ct0[7 + r : 71 + r, :]
        e = ct0[9 + r : 73 + r, :]
        gcp[r : r + 64, :] = c + (
            (xl * (w - c) + xh * (e - c)) + (yl * (s - c) + yh * (n - c)) + (zl * (b - c) + zh * (t - c))
        )
        cb[r : r + 64, :] = jnp.where(lane < 32, zl, jnp.where(lane >= 96, zh, 0.0))


def interior(state, velocity, diffusivity, ct):
    small = jax.ShapeDtypeStruct((CX, CL), F32)
    return pl.pallas_call(
        interior_kernel,
        out_shape=[
            jax.ShapeDtypeStruct((LZ - 2, NY, NX), F32),
            jax.ShapeDtypeStruct((4, NY, NX), F32),
            jax.ShapeDtypeStruct((2, 4, NY, NX), F32),
            small,
            small,
            jax.ShapeDtypeStruct((8, 64, 128), F32),
        ],
        in_specs=[remains()] * 3 + [whole()],
        out_specs=[whole()] * 6,
        scratch_shapes=[
            pltpu.VMEM((LZ, PADDED, NX), F32),
            pltpu.VMEM((LZ, PADDED, NX), F32),
            pltpu.VMEM((3, LZ, NY, NX), F32),
            pltpu.VMEM((LZ, NY, NX), F32),
            pltpu.VMEM((8, 4 * NY, 128), F32),
            pltpu.VMEM((8, 2 * NY, 128), F32),
            pltpu.VMEM((CX + 16, CL), F32),
            pltpu.SemaphoreType.DMA((LZ,)),
            pltpu.SemaphoreType.DMA((LZ, 2)),
        ],
        compiler_params=params(44),
        cost_estimate=pl.CostEstimate(flops=60_000_000, bytes_accessed=20_000_000, transcendentals=0),
        name="interior",
    )(state, velocity, diffusivity, ct)


def finish_kernel(
    rnear, rfar, rfac, onear, ofar, ofac, w0, w1, w2, w3, fin, edge, bound, gcp, cb, ymid, ub, msg, gc, quad, pad, zs, jp
):
    mine = quad_rank()
    for i, window in enumerate((w0, w1, w2, w3)):
        quad[mine ^ i] = window[...]
    for kind, (rec, own, recb, ownb, at) in enumerate(
        ((rnear, onear, rnear, onear, FAR), (rfar, ofar, rfac, ofac, 0))
    ):
        top = edge_is_top(kind)
        side = jnp.where(top, 1, 0)
        for r in range(0, NY, 8):
            pad[kind, TOP + r : TOP + r + 8, :] = (
                own[NY + r : NY + r + 8, :] + ownb[at + r : at + r + 8, :] * rec[r : r + 8, :]
            )
        wrap_rows(pad, kind)
        for r in range(0, NY, 8):
            rows = slice(r, r + 8)
            c, w, e, s, n = plane(pad, kind, r)
            outside = rec[NY + r : NY + r + 8, :] + recb[at + r : at + r + 8, :] * own[r : r + 8, :]
            inside = edge[side, rows, :]
            ax, ay, az, k = (bound[side, i, rows, :] for i in range(4))
            last = advanced(c, w, e, s, n, inside, outside, ax, ay, jnp.where(top, az, -az), k)
            near = fin[5 * side, rows, :] + edge[2 + side, rows, :] * c
            ub[3 * side, rows, :] = last
            ub[1 + side, rows, :] = near
            put_columns(zs.at[side], rows, last + near)
    lane = lax.broadcasted_iota(jnp.int32, (128, 128), 1)
    hnear = jnp.concatenate([rnear[2 * NY : FAR, 128 * i : 128 * i + 128] for i in range(8)], axis=0)
    hfar = jnp.concatenate([rfar[2 * NY : FAR, 128 * i : 128 * i + 128] for i in range(8)], axis=0)
    first_core = lax.axis_index("core") == 0
    halo_lo, halo_hi = jnp.where(first_core, hfar, hnear), jnp.where(first_core, hnear, hfar)
    for b in range(4):
        rows = slice(128 * b, 128 * b + 128)
        t = halved_x(
            jnp.concatenate(
                [
                    jnp.concatenate([paired(zs.at[0], i, 0, 32), ymid[i], paired(zs.at[1], i, 0, 32)], axis=0)
                    for i in (2 * b, 2 * b + 1)
                ],
                axis=1,
            )
        )
        hl = pltpu.roll(halo_lo, (128 - 32 * b) % 128, 1) if b else halo_lo
        hh = pltpu.roll(halo_hi, (96 - 32 * b) % 128, 1) if b != 3 else halo_hi
        halo = jnp.where(lane < 32, hl, hh)
        g = gcp[rows, :] + cb[rows, :] * halo
        g = jnp.where(lax.axis_index("tm") == 0, 0.0, g)
        gc[rows, :] = g
        jp[8 + 128 * b : 136 + 128 * b, :] = t - g
    jp[0:8, :] = jp[CX : CX + 8, :]
    jp[CX + 8 : CX + 24, :] = jp[8:24, :]
    for i in range(BLOCKS):
        msg[i] = jp[XB * i : XB * i + WIN, :]


def finish(messages, windows, fin, edge, bound, gcp, cb, ymid):
    return pl.pallas_call(
        finish_kernel,
        out_shape=[
            jax.ShapeDtypeStruct((4, NY, NX), F32),
            jax.ShapeDtypeStruct((BLOCKS, WIN, CL), F32),
            jax.ShapeDtypeStruct((CX, CL), F32),
            jax.ShapeDtypeStruct((QUAD, 4, WIN, CL), F32),
        ],
        in_specs=[whole()] * 16,
        out_specs=[whole()] * 4,
        scratch_shapes=[
            pltpu.VMEM((2, PADDED, NX), F32),
            pltpu.VMEM((2, 8, NY, 128), F32),
            pltpu.VMEM((CX + 24, CL), F32),
        ],
        compiler_params=params(24),
        name="finish",
    )(*messages, *windows, fin, edge, bound, gcp, cb, ymid)


HALO = 13
SHARED = ((0, 6, 96), (1, 5, 64), (2, 4, 32))


def pick_kernel(got, quad, even, odd):
    lane = lax.broadcasted_iota(jnp.int32, (WIN, CL), 1)
    for parity, out in enumerate((even, odd)):
        up = lax.rem(lax.axis_index("px"), 2) == parity
        near, far = jnp.where(up, 3, 0), jnp.where(up, 2, 1)

        def shared(main, other, width):
            return jnp.where(
                up,
                jnp.where(lane >= CL - width, main, pltpu.roll(other, CL - width, 1)),
                jnp.where(lane < width, main, pltpu.roll(other, width, 1)),
            )

        for j in range(4):
            out[j] = got[QUAD * j + near]
            out[7 + j] = quad[near, j]
        for j, other, width in SHARED:
            out[4 + j] = shared(got[QUAD * j + far], got[QUAD * other + near], width)
        for j in range(2):
            out[11 + j] = shared(quad[far, 2 * j], quad[far, 2 * j + 1], 64)


def pick(got, quad):
    halo = jax.ShapeDtypeStruct((HALO, WIN, CL), F32)
    return pl.pallas_call(
        pick_kernel,
        out_shape=[halo, halo],
        in_specs=[whole()] * 2,
        out_specs=[whole(), whole()],
        compiler_params=params(16),
        name="pick",
    )(got, quad)


LANES = 8 * CL


def chain_kernel(got, quad, even, odd, out, src, cf, e):
    first = lax.rem(lax.axis_index("px"), 2) == 0

    def below(i):
        return jnp.where(first, odd[i], even[i])

    def above(i):
        return jnp.where(first, even[i], odd[i])

    def put_coefs(values, lanes):
        for i, value in enumerate(coarse_coefs(*values)):
            cf[i, :, lanes] = value

    for j in range(7):
        for q in range(QUAD):
            src[j, :, (2 + q) * CL : (3 + q) * CL] = got[QUAD * j + q]
        for halo, near, far in ((below, 1, 0), (above, 6, 7)):
            if j < 4:
                src[j, :, near * CL : near * CL + CL] = halo(j)
            if j >= 3:
                src[j, :, far * CL : far * CL + CL] = jnp.zeros((WIN, CL), F32)
    for halo, near, far in ((below, 1, 0), (above, 6, 7)):
        for j, other, width in SHARED:
            turn = width if near == 1 else CL - width
            block = halo(4 + j)
            src[j, :, far * CL : far * CL + CL] = block
            src[other, :, near * CL : near * CL + CL] = pltpu.roll(block, turn, 1)
        put_coefs([halo(7 + i) for i in range(4)], slice(near * CL, near * CL + CL))
        pairs = [halo(11), halo(12)]
        put_coefs(
            [pairs[0], pltpu.roll(pairs[0], 64, 1), pairs[1], pltpu.roll(pairs[1], 64, 1)],
            slice(far * CL, far * CL + CL),
        )
    for q in range(QUAD):
        put_coefs([quad[q, comp] for comp in range(4)], slice((2 + q) * CL, (3 + q) * CL))
    for q in range(QUAD):
        out[q] = jnp.zeros((XB, CL), F32)
    e[...] = src[0]
    for k in range(1, GROUPS):
        c = e[...]
        s, n = y_rolled(c, LANES, 1)
        w, x = pltpu.roll(c, 1, 0), pltpu.roll(c, WIN - 1, 0)
        b, t = pltpu.roll(c, 32, 1), pltpu.roll(c, LANES - 32, 1)
        y = c + (
            (cf[0] * (w - c) + cf[1] * (x - c))
            + (cf[2] * (s - c) + cf[3] * (n - c))
            + (cf[4] * (b - c) + cf[5] * (t - c))
        )
        for q in range(QUAD):
            out[QUAD * k + q] = y[8 : 8 + XB, (2 + q) * CL : (3 + q) * CL]
        if k < GROUPS - 1:
            e[...] = y + src[k]


def chain(got, quad, even, odd):
    return pl.pallas_call(
        chain_kernel,
        out_shape=jax.ShapeDtypeStruct((BLOCKS, XB, CL), F32),
        in_specs=[whole()] * 4,
        out_specs=whole(),
        scratch_shapes=[
            pltpu.VMEM((7, WIN, LANES), F32),
            pltpu.VMEM((6, WIN, LANES), F32),
            pltpu.VMEM((WIN, LANES), F32),
        ],
        compiler_params=params(24),
        name="chain",
    )(got, quad, even, odd)


def result_kernel(y, gc, fin, ub, out, buf, sems):
    copy_y = table((256, CL), lambda r, c: r // 2 == c)
    copy_x = table((128, 256), lambda r, c: r == c // 2)
    copies = []
    for b in range(4):
        rows = slice(128 * b, 128 * b + 128)
        cols = slice(256 * b, 256 * b + 256)
        parts = split3(y[rows, :] - gc[rows, :])
        fine = sum(dot(dot(copy_y, p, 1, 1).astype(BF16), copy_x, 1, 0) for p in parts)
        for z in range(LZ):
            base = fin[z - 1, :, cols] if 2 <= z < 6 else ub[z if z < 2 else z - 4, :, cols]
            buf[z, :, cols] = base + fine[z // 2 * NY : z // 2 * NY + NY, :]
        copies.append(pltpu.make_async_copy(buf.at[:, :, cols], out.at[:, :, cols], sems.at[b]))
        copies[b].start()
    for copy in copies:
        copy.wait()


def result(y, gc, fin, ub):
    return pl.pallas_call(
        result_kernel,
        out_shape=jax.ShapeDtypeStruct((LZ, NY, NX), F32),
        in_specs=[whole()] * 4,
        out_specs=remains(),
        scratch_shapes=[pltpu.VMEM((LZ, NY, NX), F32), pltpu.SemaphoreType.DMA((4,))],
        compiler_params=params(16),
        name="result",
    )(y, gc, fin, ub)


def swap(value, axes, partner):
    pairs = [(i, partner(i)) for i in range(lax.axis_size(axes))]
    return lax.ppermute(value, axes, [(i, j) for i, j in pairs if j is not None])


def off_chip(i):
    j = i + 1 if i % 2 else i - 1
    return j if 0 <= j < 16 else None


def off_chip_copy(i):
    j = off_chip(i % 16)
    return None if j is None else (i // 16 ^ 1) * 16 + j


def quad_beside(i):
    j = i + 1 if i % 2 else i - 1
    return j if 0 <= j < 4 else None


def shards(state_old, velocity, diffusivity):
    state = state_old[0]
    onear, ofar, ofac = edges(state, velocity, diffusivity)
    rnear = swap(onear, SPACE, lambda i: i ^ 1)
    rfar = swap(ofar, SPACE, off_chip)
    rfac = swap(ofac, ("tm",) + SPACE, off_chip_copy)
    ct, w0, w1, w2, w3 = coefs(velocity, diffusivity)
    windows = (
        w0,
        swap(w1, SPACE, lambda i: i ^ 1),
        swap(w2, SPACE, lambda i: i ^ 2),
        swap(w3, SPACE, lambda i: i ^ 3),
    )
    fin, edge, bound, gcp, cb, ymid = interior(state, velocity, diffusivity, ct)
    messages = (rnear, rfar, rfac, onear, ofar, ofac)
    ub, msg, gc, quad = finish(messages, windows, fin, edge, bound, gcp, cb, ymid)
    got = lax.all_to_all(msg, GROUP, 0, 0)
    even, odd = pick(got, quad)
    even = swap(even, "px", lambda i: i ^ 1)
    odd = swap(odd, "px", quad_beside)
    back = lax.all_to_all(chain(got, quad, even, odd), GROUP, 0, 0)
    return result(back.reshape(CX, CL), gc, fin, ub)[None]


def solution(mesh):
    fine_mesh = Mesh(mesh.devices.reshape(GROUPS, 4, 2, 2), ("tm",) + SPACE)
    return jax.shard_map(
        shards,
        mesh=fine_mesh,
        in_specs=(
            P("tm", SPACE, None, None),
            P(None, SPACE, None, None),
            P(SPACE, None, None),
        ),
        out_specs=P("tm", SPACE, None, None),
        check_vma=False,
    )
```

```python
import jax
import jax.numpy as jnp
from jax import lax
from jax.experimental import pallas as pl
from jax.experimental.pallas import tpu as pltpu
from jax.sharding import Mesh
from jax.sharding import PartitionSpec as P

F32 = jnp.float32
BF16 = jnp.bfloat16
NY, NX = 64, 1024
LZ = 8
CX, CL = 512, 128
GROUPS = 8
QUAD = 4
BLOCKS = GROUPS * QUAD
XB = CX // BLOCKS
WIN = XB + 16
SPACE = ("px", "pz", "core")
GROUP = ("tm", "pz", "core")


def params(mib):
    return pltpu.CompilerParams(vmem_limit_bytes=mib * 1024 * 1024)


def split3(x):
    hi = x.astype(BF16)
    rest = x - hi.astype(F32)
    mid = rest.astype(BF16)
    return hi, mid, (rest - mid.astype(F32)).astype(BF16)


def dot(a, b, ca, cb):
    return lax.dot_general(a, b, (((ca,), (cb,)), ((), ())), preferred_element_type=F32)


def table(shape, test):
    rows = lax.broadcasted_iota(jnp.int32, shape, 0)
    cols = lax.broadcasted_iota(jnp.int32, shape, 1)
    return test(rows, cols).astype(F32).astype(BF16)


def halved_x(part):
    halve = table((128, 256), lambda r, c: r == c // 2)
    return sum(dot(halve, p, 1, 1) for p in split3(part)) * 0.125


def put_columns(ref, at, value):
    for i in range(NX // 128):
        ref[i, at, :] = value[:, 128 * i : 128 * i + 128]


def paired(ref, column, first, rows):
    return ref[column, pl.ds(first, rows, 2), :] + ref[column, pl.ds(first + 1, rows, 2), :]


def advanced(c, w, e, s, n, b, t, ax, ay, az, k):
    lap = ((w + e) + (s + n)) + ((b + t) - 6.0 * c)
    dx = jnp.abs(ax) * (jnp.where(ax > 0, w, e) - c)
    dy = jnp.abs(ay) * (jnp.where(ay > 0, s, n) - c)
    dz = jnp.abs(az) * (jnp.where(az > 0, b, t) - c)
    return (c + k * lap) + ((dx + dy) + dz)


def planes(ref, z):
    row = lax.broadcasted_iota(jnp.int32, (8, NX), 0)
    c = ref[z, 0:8, :]
    before = pltpu.roll(ref[z, NY - 8 : NY, :], 1, 0)
    for r in range(0, NY, 8):
        after = ref[z, (r + 8) % NY : (r + 8) % NY + 8, :]
        down = pltpu.roll(c, 1, 0)
        s = jnp.where(row == 0, before, down)
        n = jnp.where(row == 7, pltpu.roll(after, 7, 0), pltpu.roll(c, 7, 0))
        yield r, slice(r, r + 8), (c, pltpu.roll(c, 1, 1), pltpu.roll(c, NX - 1, 1), s, n)
        c, before = after, down


def coarse_coefs(vx, vy, vz, k):
    half = 0.5 * k
    out = []
    for a in (vx, vy, vz):
        out += [half + jnp.maximum(a, 0.0), half - jnp.minimum(a, 0.0)]
    return out


def y_rolled(u, width, axis):
    y = lax.broadcasted_iota(jnp.int32, u.shape, axis) % 32
    s = jnp.where(y == 0, pltpu.roll(u, width - 31, axis), pltpu.roll(u, 1, axis))
    n = jnp.where(y == 31, pltpu.roll(u, 31, axis), pltpu.roll(u, width - 1, axis))
    return s, n


FAR = 2 * NY + 16
NEAR = FAR + NY
CROWS = CX + 32


def edge_is_top(kind):
    return lax.axis_index("core") == kind


def edges_kernel(st, vel, dif, near, far, factor, u, vx, vy, vz, d, zs, sems):
    tops = [edge_is_top(kind) for kind in range(2)]

    def layer(z, which=(0, 1, 2, 3, 4)):
        pairs = (
            (st.at[z], u.at[z]),
            (vel.at[0, z], vx.at[z]),
            (vel.at[1, z], vy.at[z]),
            (vel.at[2, z], vz.at[z]),
            (dif.at[z], d.at[z]),
        )
        return [pltpu.make_async_copy(*pairs[i], sems.at[z, i]) for i in which]

    order = []
    for top in tops:
        order += [jnp.where(top, LZ - 1, 0), jnp.where(top, LZ - 2, 1)]
    middle = list(range(2, LZ - 2))
    early, late = (0,), (1, 2, 3, 4)
    for kind in range(2):
        for copy in layer(order[2 * kind]) + layer(order[2 * kind + 1], early):
            copy.start()
    for z in (1, LZ - 2):
        for copy in layer(z, late):
            copy.start()
    for z in middle:
        for copy in layer(z):
            copy.start()
    for kind, top in enumerate(tops):
        out = (near, far)[kind]
        z, beside = order[2 * kind], order[2 * kind + 1]
        for copy in layer(z) + layer(beside, early):
            copy.wait()
        for r, rows, (c, w, e, s, n) in planes(u, z):
            inside = u[beside, rows, :]
            ax, ay, k = vx[z, rows, :], vy[z, rows, :], d[z, rows, :]
            up = jnp.where(top, vz[z, rows, :], -vz[z, rows, :])
            out[r : r + 8, :] = c
            out[NY + r : NY + r + 8, :] = advanced(c, w, e, s, n, inside, jnp.zeros_like(c), ax, ay, up, k)
            b = k - jnp.minimum(up, 0.0)
            if kind == 0:
                near[FAR + r : FAR + r + 8, :] = b
            else:
                factor[rows, :] = b
            put_columns(zs, slice(kind * NY + r, kind * NY + r + 8), c + inside)
    lane = lax.broadcasted_iota(jnp.int32, (128, 128), 1)
    cnear = jnp.zeros((128, 128), F32)
    cfar = jnp.zeros((128, 128), F32)
    for b in range(4):
        part = jnp.concatenate([paired(zs, 2 * b + i, 0, 64) for i in range(2)], axis=1)
        t = halved_x(jnp.concatenate([part, jnp.zeros_like(part)], axis=0))
        tn = jnp.where(lane < 32, t, 0.0)
        tf = jnp.where((lane >= 32) & (lane < 64), t, 0.0)
        cnear += pltpu.roll(tn, 32 * b, 1) if b else tn
        cfar += pltpu.roll(tf, (32 * b - 32) % 128, 1) if b != 1 else tf
    for i in range(8):
        near[2 * NY : FAR, 128 * i : 128 * i + 128] = cnear[16 * i : 16 * i + 16, :]
        far[2 * NY : FAR, 128 * i : 128 * i + 128] = cfar[16 * i : 16 * i + 16, :]
    for z in (1, LZ - 2):
        for copy in layer(z, late):
            copy.wait()
    for z in middle:
        for copy in layer(z):
            copy.wait()


def whole():
    return pl.BlockSpec(memory_space=pltpu.VMEM)


def remains():
    return pl.BlockSpec(memory_space=pltpu.HBM)


def edges(state, velocity, diffusivity):
    slab = jax.ShapeDtypeStruct((LZ, NY, NX), F32)
    return pl.pallas_call(
        edges_kernel,
        out_shape=[
            jax.ShapeDtypeStruct((NEAR, NX), F32),
            jax.ShapeDtypeStruct((FAR, NX), F32),
            jax.ShapeDtypeStruct((NY, NX), F32),
        ]
        + [slab] * 5,
        in_specs=[remains()] * 3,
        out_specs=[whole()] * 8,
        scratch_shapes=[
            pltpu.VMEM((8, 2 * NY, 128), F32),
            pltpu.SemaphoreType.DMA((LZ, 5)),
        ],
        compiler_params=params(42),
        name="edges",
    )(state, velocity, diffusivity)


def quad_rank():
    return lax.axis_index("pz") * 2 + lax.axis_index("core")


def coefs_kernel(vx, vy, vz, d, ct, w0, w1, w2, w3, zs):
    for comp, ref in enumerate((vx, vy, vz, d)):
        for zc in range(4):
            for r in range(0, NY, 8):
                rows = slice(r, r + 8)
                put_columns(
                    zs.at[comp], slice(zc * NY + r, zc * NY + r + 8), ref[2 * zc, rows, :] + ref[2 * zc + 1, rows, :]
                )
        for b in range(4):
            ct[comp, 8 + 128 * b : 136 + 128 * b, :] = halved_x(
                jnp.concatenate([paired(zs.at[comp], 2 * b + i, 0, 128) for i in range(2)], axis=1)
            )
        ct[comp, 0:8, :] = ct[comp, CX : CX + 8, :]
        ct[comp, CX + 8 : CX + 32, :] = ct[comp, 8:32, :]
    mine = quad_rank()
    for i, out in enumerate((w0, w1, w2, w3)):
        block = lax.axis_index("tm") * QUAD + (mine ^ i)
        for comp in range(4):
            out[comp] = ct[comp, pl.ds(pl.multiple_of(block * XB, XB), WIN), :]


def coefs(fields):
    window = jax.ShapeDtypeStruct((4, WIN, CL), F32)
    return pl.pallas_call(
        coefs_kernel,
        out_shape=[jax.ShapeDtypeStruct((4, CROWS, CL), F32), window, window, window, window],
        in_specs=[whole()] * 4,
        out_specs=[whole()] * 5,
        scratch_shapes=[pltpu.VMEM((4, 8, 4 * NY, 128), F32)],
        compiler_params=params(12),
        cost_estimate=pl.CostEstimate(flops=20_000_000, bytes_accessed=9_000_000, transcendentals=0),
        name="coefs",
    )(*fields)


def interior_kernel(u, vx, vy, vz, d, ct, fin, edge, gcp, cb, ymid, u1, zs, zf, ct0):
    def first(z, _):
        for _, rows, (c, w, e, s, n) in planes(u, z):
            u1[z, rows, :] = advanced(
                c, w, e, s, n, u[z - 1, rows, :], u[z + 1, rows, :],
                vx[z, rows, :], vy[z, rows, :], vz[z, rows, :], d[z, rows, :],
            )
        return 0

    lax.fori_loop(1, LZ - 1, first, 0)
    u1[0] = jnp.zeros((NY, NX), F32)
    u1[LZ - 1] = jnp.zeros((NY, NX), F32)
    edge[0] = u1[1]
    edge[1] = u1[LZ - 2]

    def second(z, _):
        for _, rows, (c, w, e, s, n) in planes(u1, z):
            fin[z - 1, rows, :] = advanced(
                c, w, e, s, n, u1[z - 1, rows, :], u1[z + 1, rows, :],
                vx[z, rows, :], vy[z, rows, :], vz[z, rows, :], d[z, rows, :],
            )
        return 0

    lax.fori_loop(1, LZ - 1, second, 0)
    edge[2] = d[1] + jnp.maximum(vz[1], 0.0)
    edge[3] = d[LZ - 2] - jnp.minimum(vz[LZ - 2], 0.0)
    for zc in (1, 2):
        for r in range(0, NY, 8):
            rows = slice(r, r + 8)
            put_columns(zf, slice((zc - 1) * NY + r, (zc - 1) * NY + r + 8), fin[2 * zc - 1, rows, :] + fin[2 * zc, rows, :])
    for i in range(8):
        ymid[i] = paired(zf, i, 0, 64)

    for zc in range(4):
        for r in range(0, NY, 8):
            rows = slice(r, r + 8)
            put_columns(zs, slice(zc * NY + r, zc * NY + r + 8), u[2 * zc, rows, :] + u[2 * zc + 1, rows, :])
    for b in range(4):
        ct0[8 + 128 * b : 136 + 128 * b, :] = halved_x(
            jnp.concatenate([paired(zs, 2 * b + i, 0, 128) for i in range(2)], axis=1)
        )
    ct0[0:8, :] = ct0[CX : CX + 8, :]
    ct0[CX + 8 : CX + 16, :] = ct0[8:16, :]
    lane = lax.broadcasted_iota(jnp.int32, (64, CL), 1)
    for r in range(0, CX, 64):
        c = ct0[8 + r : 72 + r, :]
        xl, xh, yl, yh, zl, zh = coarse_coefs(*(ct[i, 8 + r : 72 + r, :] for i in range(4)))
        s, n = y_rolled(c, CL, 1)
        b = jnp.where(lane < 32, 0.0, pltpu.roll(c, 32, 1))
        t = jnp.where(lane >= 96, 0.0, pltpu.roll(c, 96, 1))
        w = ct0[7 + r : 71 + r, :]
        e = ct0[9 + r : 73 + r, :]
        gcp[r : r + 64, :] = c + (
            (xl * (w - c) + xh * (e - c)) + (yl * (s - c) + yh * (n - c)) + (zl * (b - c) + zh * (t - c))
        )
        cb[r : r + 64, :] = jnp.where(lane < 32, zl, jnp.where(lane >= 96, zh, 0.0))


def interior(state, fields, ct):
    small = jax.ShapeDtypeStruct((CX, CL), F32)
    return pl.pallas_call(
        interior_kernel,
        out_shape=[
            jax.ShapeDtypeStruct((LZ - 2, NY, NX), F32),
            jax.ShapeDtypeStruct((4, NY, NX), F32),
            small,
            small,
            jax.ShapeDtypeStruct((8, 64, 128), F32),
        ],
        in_specs=[whole()] * 6,
        out_specs=[whole()] * 5,
        scratch_shapes=[
            pltpu.VMEM((LZ, NY, NX), F32),
            pltpu.VMEM((8, 4 * NY, 128), F32),
            pltpu.VMEM((8, 2 * NY, 128), F32),
            pltpu.VMEM((CX + 16, CL), F32),
        ],
        compiler_params=params(16),
        cost_estimate=pl.CostEstimate(flops=60_000_000, bytes_accessed=20_000_000, transcendentals=0),
        name="interior",
    )(state, *fields, ct)


def finish_kernel(
    rnear, rfar, rfac, onear, ofar, ofac, w0, w1, w2, w3, fin, edge, vx, vy, vz, d, gcp, cb, ymid, ub, msg, gc, quad, u1, zs, jp
):
    mine = quad_rank()
    for i, window in enumerate((w0, w1, w2, w3)):
        quad[mine ^ i] = window[...]
    for kind, (rec, own, recb, ownb, at) in enumerate(
        ((rnear, onear, rnear, onear, FAR), (rfar, ofar, rfac, ofac, 0))
    ):
        top = edge_is_top(kind)
        side = jnp.where(top, 1, 0)
        for r in range(0, NY, 8):
            u1[kind, r : r + 8, :] = (
                own[NY + r : NY + r + 8, :] + ownb[at + r : at + r + 8, :] * rec[r : r + 8, :]
            )
        z = side * (LZ - 1)
        for r, rows, (c, w, e, s, n) in planes(u1, kind):
            outside = rec[NY + r : NY + r + 8, :] + recb[at + r : at + r + 8, :] * own[r : r + 8, :]
            inside = edge[side, rows, :]
            ax, ay, az, k = vx[z, rows, :], vy[z, rows, :], vz[z, rows, :], d[z, rows, :]
            last = advanced(c, w, e, s, n, inside, outside, ax, ay, jnp.where(top, az, -az), k)
            near = fin[5 * side, rows, :] + edge[2 + side, rows, :] * c
            ub[3 * side, rows, :] = last
            ub[1 + side, rows, :] = near
            put_columns(zs.at[side], rows, last + near)
    lane = lax.broadcasted_iota(jnp.int32, (128, 128), 1)
    hnear = jnp.concatenate([rnear[2 * NY : FAR, 128 * i : 128 * i + 128] for i in range(8)], axis=0)
    hfar = jnp.concatenate([rfar[2 * NY : FAR, 128 * i : 128 * i + 128] for i in range(8)], axis=0)
    first_core = lax.axis_index("core") == 0
    halo_lo, halo_hi = jnp.where(first_core, hfar, hnear), jnp.where(first_core, hnear, hfar)
    for b in range(4):
        rows = slice(128 * b, 128 * b + 128)
        t = halved_x(
            jnp.concatenate(
                [
                    jnp.concatenate([paired(zs.at[0], i, 0, 32), ymid[i], paired(zs.at[1], i, 0, 32)], axis=0)
                    for i in (2 * b, 2 * b + 1)
                ],
                axis=1,
            )
        )
        hl = pltpu.roll(halo_lo, (128 - 32 * b) % 128, 1) if b else halo_lo
        hh = pltpu.roll(halo_hi, (96 - 32 * b) % 128, 1) if b != 3 else halo_hi
        halo = jnp.where(lane < 32, hl, hh)
        g = gcp[rows, :] + cb[rows, :] * halo
        g = jnp.where(lax.axis_index("tm") == 0, 0.0, g)
        gc[rows, :] = g
        jp[8 + 128 * b : 136 + 128 * b, :] = t - g
    jp[0:8, :] = jp[CX : CX + 8, :]
    jp[CX + 8 : CX + 24, :] = jp[8:24, :]
    for i in range(BLOCKS):
        msg[i] = jp[XB * i : XB * i + WIN, :]


def finish(messages, windows, fin, edge, fields, gcp, cb, ymid):
    return pl.pallas_call(
        finish_kernel,
        out_shape=[
            jax.ShapeDtypeStruct((4, NY, NX), F32),
            jax.ShapeDtypeStruct((BLOCKS, WIN, CL), F32),
            jax.ShapeDtypeStruct((CX, CL), F32),
            jax.ShapeDtypeStruct((QUAD, 4, WIN, CL), F32),
        ],
        in_specs=[whole()] * 19,
        out_specs=[whole()] * 4,
        scratch_shapes=[
            pltpu.VMEM((2, NY, NX), F32),
            pltpu.VMEM((2, 8, NY, 128), F32),
            pltpu.VMEM((CX + 24, CL), F32),
        ],
        compiler_params=params(16),
        name="finish",
    )(*messages, *windows, fin, edge, *fields, gcp, cb, ymid)


HALO = 13
SHARED = ((0, 6, 96), (1, 5, 64), (2, 4, 32))


def pick_kernel(got, quad, even, odd):
    lane = lax.broadcasted_iota(jnp.int32, (WIN, CL), 1)
    for parity, out in enumerate((even, odd)):
        up = lax.rem(lax.axis_index("px"), 2) == parity
        near, far = jnp.where(up, 3, 0), jnp.where(up, 2, 1)

        def shared(main, other, width):
            return jnp.where(
                up,
                jnp.where(lane >= CL - width, main, pltpu.roll(other, CL - width, 1)),
                jnp.where(lane < width, main, pltpu.roll(other, width, 1)),
            )

        for j in range(4):
            out[j] = got[QUAD * j + near]
            out[7 + j] = quad[near, j]
        for j, other, width in SHARED:
            out[4 + j] = shared(got[QUAD * j + far], got[QUAD * other + near], width)
        for j in range(2):
            out[11 + j] = shared(quad[far, 2 * j], quad[far, 2 * j + 1], 64)


def pick(got, quad):
    halo = jax.ShapeDtypeStruct((HALO, WIN, CL), F32)
    return pl.pallas_call(
        pick_kernel,
        out_shape=[halo, halo],
        in_specs=[whole()] * 2,
        out_specs=[whole(), whole()],
        compiler_params=params(16),
        name="pick",
    )(got, quad)


LANES = 8 * CL


def chain_kernel(got, quad, even, odd, out, src, cf, e):
    first = lax.rem(lax.axis_index("px"), 2) == 0

    def below(i):
        return jnp.where(first, odd[i], even[i])

    def above(i):
        return jnp.where(first, even[i], odd[i])

    def put_coefs(values, lanes):
        for i, value in enumerate(coarse_coefs(*values)):
            cf[i, :, lanes] = value

    for j in range(7):
        for q in range(QUAD):
            src[j, :, (2 + q) * CL : (3 + q) * CL] = got[QUAD * j + q]
        for halo, near, far in ((below, 1, 0), (above, 6, 7)):
            if j < 4:
                src[j, :, near * CL : near * CL + CL] = halo(j)
            if j >= 3:
                src[j, :, far * CL : far * CL + CL] = jnp.zeros((WIN, CL), F32)
    for halo, near, far in ((below, 1, 0), (above, 6, 7)):
        for j, other, width in SHARED:
            turn = width if near == 1 else CL - width
            block = halo(4 + j)
            src[j, :, far * CL : far * CL + CL] = block
            src[other, :, near * CL : near * CL + CL] = pltpu.roll(block, turn, 1)
        put_coefs([halo(7 + i) for i in range(4)], slice(near * CL, near * CL + CL))
        pairs = [halo(11), halo(12)]
        put_coefs(
            [pairs[0], pltpu.roll(pairs[0], 64, 1), pairs[1], pltpu.roll(pairs[1], 64, 1)],
            slice(far * CL, far * CL + CL),
        )
    for q in range(QUAD):
        put_coefs([quad[q, comp] for comp in range(4)], slice((2 + q) * CL, (3 + q) * CL))
    for q in range(QUAD):
        out[q] = jnp.zeros((XB, CL), F32)
    e[...] = src[0]
    for k in range(1, GROUPS):
        c = e[...]
        s, n = y_rolled(c, LANES, 1)
        w, x = pltpu.roll(c, 1, 0), pltpu.roll(c, WIN - 1, 0)
        b, t = pltpu.roll(c, 32, 1), pltpu.roll(c, LANES - 32, 1)
        y = c + (
            (cf[0] * (w - c) + cf[1] * (x - c))
            + (cf[2] * (s - c) + cf[3] * (n - c))
            + (cf[4] * (b - c) + cf[5] * (t - c))
        )
        for q in range(QUAD):
            out[QUAD * k + q] = y[8 : 8 + XB, (2 + q) * CL : (3 + q) * CL]
        if k < GROUPS - 1:
            e[...] = y + src[k]


def chain(got, quad, even, odd):
    return pl.pallas_call(
        chain_kernel,
        out_shape=jax.ShapeDtypeStruct((BLOCKS, XB, CL), F32),
        in_specs=[whole()] * 4,
        out_specs=whole(),
        scratch_shapes=[
            pltpu.VMEM((7, WIN, LANES), F32),
            pltpu.VMEM((6, WIN, LANES), F32),
            pltpu.VMEM((WIN, LANES), F32),
        ],
        compiler_params=params(24),
        name="chain",
    )(got, quad, even, odd)


def result_kernel(y, gc, fin, ub, out, buf, sems):
    copy_y = table((256, CL), lambda r, c: r // 2 == c)
    copy_x = table((128, 256), lambda r, c: r == c // 2)
    copies = []
    for b in range(4):
        rows = slice(128 * b, 128 * b + 128)
        cols = slice(256 * b, 256 * b + 256)
        parts = split3(y[rows, :] - gc[rows, :])
        fine = sum(dot(dot(copy_y, p, 1, 1).astype(BF16), copy_x, 1, 0) for p in parts)
        for z in range(LZ):
            base = fin[z - 1, :, cols] if 2 <= z < 6 else ub[z if z < 2 else z - 4, :, cols]
            buf[z, :, cols] = base + fine[z // 2 * NY : z // 2 * NY + NY, :]
        copies.append(pltpu.make_async_copy(buf.at[:, :, cols], out.at[:, :, cols], sems.at[b]))
        copies[b].start()
    for copy in copies:
        copy.wait()


def result(y, gc, fin, ub):
    return pl.pallas_call(
        result_kernel,
        out_shape=jax.ShapeDtypeStruct((LZ, NY, NX), F32),
        in_specs=[whole()] * 4,
        out_specs=remains(),
        scratch_shapes=[pltpu.VMEM((LZ, NY, NX), F32), pltpu.SemaphoreType.DMA((4,))],
        compiler_params=params(16),
        name="result",
    )(y, gc, fin, ub)


def swap(value, axes, partner):
    pairs = [(i, partner(i)) for i in range(lax.axis_size(axes))]
    return lax.ppermute(value, axes, [(i, j) for i, j in pairs if j is not None])


def off_chip(i):
    j = i + 1 if i % 2 else i - 1
    return j if 0 <= j < 16 else None


def off_chip_copy(i):
    j = off_chip(i % 16)
    return None if j is None else (i // 16 ^ 1) * 16 + j


def quad_beside(i):
    j = i + 1 if i % 2 else i - 1
    return j if 0 <= j < 4 else None


def shards(state_old, velocity, diffusivity):
    state = state_old[0]
    onear, ofar, ofac, u, *fields = edges(state, velocity, diffusivity)
    rnear = swap(onear, SPACE, lambda i: i ^ 1)
    rfar = swap(ofar, SPACE, off_chip)
    rfac = swap(ofac, ("tm",) + SPACE, off_chip_copy)
    ct, w0, w1, w2, w3 = coefs(fields)
    windows = (
        w0,
        swap(w1, SPACE, lambda i: i ^ 1),
        swap(w2, SPACE, lambda i: i ^ 2),
        swap(w3, SPACE, lambda i: i ^ 3),
    )
    fin, edge, gcp, cb, ymid = interior(u, fields, ct)
    messages = (rnear, rfar, rfac, onear, ofar, ofac)
    ub, msg, gc, quad = finish(messages, windows, fin, edge, fields, gcp, cb, ymid)
    got = lax.all_to_all(msg, GROUP, 0, 0)
    even, odd = pick(got, quad)
    even = swap(even, "px", lambda i: i ^ 1)
    odd = swap(odd, "px", quad_beside)
    back = lax.all_to_all(chain(got, quad, even, odd), GROUP, 0, 0)
    return result(back.reshape(CX, CL), gc, fin, ub)[None]


def solution(mesh):
    fine_mesh = Mesh(mesh.devices.reshape(GROUPS, 4, 2, 2), ("tm",) + SPACE)
    return jax.shard_map(
        shards,
        mesh=fine_mesh,
        in_specs=(
            P("tm", SPACE, None, None),
            P(None, SPACE, None, None),
            P(SPACE, None, None),
        ),
        out_specs=P("tm", SPACE, None, None),
        check_vma=False,
    )
```

```python
import jax
import jax.numpy as jnp
from jax import lax
from jax.experimental import pallas as pl
from jax.experimental.pallas import tpu as pltpu
from jax.sharding import Mesh
from jax.sharding import PartitionSpec as P

F32 = jnp.float32
BF16 = jnp.bfloat16
NY, NX = 64, 1024
LZ = 8
CX, CL = 512, 128
GROUPS = 8
QUAD = 4
BLOCKS = GROUPS * QUAD
XB = CX // BLOCKS
WIN = XB + 16
SPACE = ("px", "pz", "core")
GROUP = ("tm", "pz", "core")


def params(mib):
    return pltpu.CompilerParams(vmem_limit_bytes=mib * 1024 * 1024)


def split3(x):
    hi = x.astype(BF16)
    rest = x - hi.astype(F32)
    mid = rest.astype(BF16)
    return hi, mid, (rest - mid.astype(F32)).astype(BF16)


def dot(a, b, ca, cb):
    return lax.dot_general(a, b, (((ca,), (cb,)), ((), ())), preferred_element_type=F32)


def table(shape, test):
    rows = lax.broadcasted_iota(jnp.int32, shape, 0)
    cols = lax.broadcasted_iota(jnp.int32, shape, 1)
    return test(rows, cols).astype(F32).astype(BF16)


def halved_x(part):
    halve = table((128, 256), lambda r, c: r == c // 2)
    return sum(dot(halve, p, 1, 1) for p in split3(part)) * 0.125


def put_columns(ref, at, value):
    for i in range(NX // 128):
        ref[i, at, :] = value[:, 128 * i : 128 * i + 128]


def paired(ref, column, first, rows):
    return ref[column, pl.ds(first, rows, 2), :] + ref[column, pl.ds(first + 1, rows, 2), :]


def advanced(c, w, e, s, n, b, t, ax, ay, az, k):
    lap = ((w + e) + (s + n)) + ((b + t) - 6.0 * c)
    dx = jnp.abs(ax) * (jnp.where(ax > 0, w, e) - c)
    dy = jnp.abs(ay) * (jnp.where(ay > 0, s, n) - c)
    dz = jnp.abs(az) * (jnp.where(az > 0, b, t) - c)
    return (c + k * lap) + ((dx + dy) + dz)


def planes(ref, z):
    row = lax.broadcasted_iota(jnp.int32, (8, NX), 0)
    c = ref[z, 0:8, :]
    before = pltpu.roll(ref[z, NY - 8 : NY, :], 1, 0)
    for r in range(0, NY, 8):
        after = ref[z, (r + 8) % NY : (r + 8) % NY + 8, :]
        down = pltpu.roll(c, 1, 0)
        s = jnp.where(row == 0, before, down)
        n = jnp.where(row == 7, pltpu.roll(after, 7, 0), pltpu.roll(c, 7, 0))
        yield r, slice(r, r + 8), (c, pltpu.roll(c, 1, 1), pltpu.roll(c, NX - 1, 1), s, n)
        c, before = after, down


def coarse_coefs(vx, vy, vz, k):
    half = 0.5 * k
    out = []
    for a in (vx, vy, vz):
        out += [half + jnp.maximum(a, 0.0), half - jnp.minimum(a, 0.0)]
    return out


def y_rolled(u, width, axis):
    y = lax.broadcasted_iota(jnp.int32, u.shape, axis) % 32
    s = jnp.where(y == 0, pltpu.roll(u, width - 31, axis), pltpu.roll(u, 1, axis))
    n = jnp.where(y == 31, pltpu.roll(u, 31, axis), pltpu.roll(u, width - 1, axis))
    return s, n


FAR = 2 * NY + 16
NEAR = FAR + NY
CROWS = CX + 32


def edge_is_top(kind):
    return lax.axis_index("core") == kind


def edges_kernel(st, vel, dif, near, far, factor, u, v, d, zs, sems):
    tops = [edge_is_top(kind) for kind in range(2)]
    copies = []
    for kind, top in enumerate(tops):
        z, beside = jnp.where(top, LZ - 1, 0), jnp.where(top, LZ - 2, 1)
        pairs = (
            (st.at[z], u.at[kind]),
            (vel.at[:, z], v.at[kind]),
            (dif.at[z], d.at[kind]),
            (st.at[beside], u.at[2 + kind]),
        )
        copies.append([pltpu.make_async_copy(a, b, sems.at[kind, i]) for i, (a, b) in enumerate(pairs)])
    for kind in (1, 0):
        for copy in copies[kind]:
            copy.start()
    for kind in (1, 0):
        top, out = tops[kind], (near, far)[kind]
        for copy in copies[kind]:
            copy.wait()
        for r, rows, (c, w, e, s, n) in planes(u, kind):
            inside = u[2 + kind, rows, :]
            ax, ay, k = v[kind, 0, rows, :], v[kind, 1, rows, :], d[kind, rows, :]
            up = jnp.where(top, v[kind, 2, rows, :], -v[kind, 2, rows, :])
            out[r : r + 8, :] = c
            out[NY + r : NY + r + 8, :] = advanced(c, w, e, s, n, inside, jnp.zeros_like(c), ax, ay, up, k)
            b = k - jnp.minimum(up, 0.0)
            if kind == 0:
                near[FAR + r : FAR + r + 8, :] = b
            else:
                factor[rows, :] = b
            put_columns(zs, slice(kind * NY + r, kind * NY + r + 8), c + inside)
    lane = lax.broadcasted_iota(jnp.int32, (128, 128), 1)
    cnear = jnp.zeros((128, 128), F32)
    cfar = jnp.zeros((128, 128), F32)
    for b in range(4):
        part = jnp.concatenate([paired(zs, 2 * b + i, 0, 64) for i in range(2)], axis=1)
        t = halved_x(jnp.concatenate([part, jnp.zeros_like(part)], axis=0))
        tn = jnp.where(lane < 32, t, 0.0)
        tf = jnp.where((lane >= 32) & (lane < 64), t, 0.0)
        cnear += pltpu.roll(tn, 32 * b, 1) if b else tn
        cfar += pltpu.roll(tf, (32 * b - 32) % 128, 1) if b != 1 else tf
    for i in range(8):
        near[2 * NY : FAR, 128 * i : 128 * i + 128] = cnear[16 * i : 16 * i + 16, :]
        far[2 * NY : FAR, 128 * i : 128 * i + 128] = cfar[16 * i : 16 * i + 16, :]


def whole():
    return pl.BlockSpec(memory_space=pltpu.VMEM)


def remains():
    return pl.BlockSpec(memory_space=pltpu.HBM)


def edges(state, velocity, diffusivity):
    return pl.pallas_call(
        edges_kernel,
        out_shape=[
            jax.ShapeDtypeStruct((NEAR, NX), F32),
            jax.ShapeDtypeStruct((FAR, NX), F32),
            jax.ShapeDtypeStruct((NY, NX), F32),
        ],
        in_specs=[remains()] * 3,
        out_specs=[whole()] * 3,
        scratch_shapes=[
            pltpu.VMEM((4, NY, NX), F32),
            pltpu.VMEM((2, 3, NY, NX), F32),
            pltpu.VMEM((2, NY, NX), F32),
            pltpu.VMEM((8, 2 * NY, 128), F32),
            pltpu.SemaphoreType.DMA((2, 4)),
        ],
        compiler_params=params(52),
        name="edges",
    )(state, velocity, diffusivity)


def quad_rank():
    return lax.axis_index("pz") * 2 + lax.axis_index("core")


def coefs_kernel(st, vel, dif, ct, w0, w1, w2, w3, u, vx, vy, vz, d, zs, usem, sems):
    fields = (vx, vy, vz, d)

    def part(comp, zc):
        layers = slice(2 * zc, 2 * zc + 2)
        source = dif.at[layers] if comp == 3 else vel.at[comp, layers]
        return pltpu.make_async_copy(source, fields[comp].at[layers], sems.at[comp, zc])

    for comp in range(4):
        for zc in range(4):
            part(comp, zc).start()
    state = pltpu.make_async_copy(st, u, usem)
    state.start()
    for comp, ref in enumerate(fields):
        for zc in range(4):
            part(comp, zc).wait()
            for r in range(0, NY, 8):
                rows = slice(r, r + 8)
                put_columns(
                    zs.at[comp], slice(zc * NY + r, zc * NY + r + 8), ref[2 * zc, rows, :] + ref[2 * zc + 1, rows, :]
                )
        for b in range(4):
            ct[comp, 8 + 128 * b : 136 + 128 * b, :] = halved_x(
                jnp.concatenate([paired(zs.at[comp], 2 * b + i, 0, 128) for i in range(2)], axis=1)
            )
        ct[comp, 0:8, :] = ct[comp, CX : CX + 8, :]
        ct[comp, CX + 8 : CX + 32, :] = ct[comp, 8:32, :]
    mine = quad_rank()
    for i, out in enumerate((w0, w1, w2, w3)):
        slice_index = lax.axis_index("tm")
        block = (slice_index if i < 2 else slice_index ^ 1) * QUAD + (mine ^ i)
        for comp in range(4):
            out[comp] = ct[comp, pl.ds(pl.multiple_of(block * XB, XB), WIN), :]
    state.wait()


def coefs(state, velocity, diffusivity):
    window = jax.ShapeDtypeStruct((4, WIN, CL), F32)
    slab = jax.ShapeDtypeStruct((LZ, NY, NX), F32)
    return pl.pallas_call(
        coefs_kernel,
        out_shape=[jax.ShapeDtypeStruct((4, CROWS, CL), F32)] + [window] * 4 + [slab] * 5,
        in_specs=[remains()] * 3,
        out_specs=[whole()] * 10,
        scratch_shapes=[
            pltpu.VMEM((4, 8, 4 * NY, 128), F32),
            pltpu.SemaphoreType.DMA,
            pltpu.SemaphoreType.DMA((4, 4)),
        ],
        compiler_params=params(42),
        cost_estimate=pl.CostEstimate(flops=20_000_000, bytes_accessed=9_000_000, transcendentals=0),
        name="coefs",
    )(state, velocity, diffusivity)


def interior_kernel(u, vx, vy, vz, d, ct, fin, edge, gcp, cb, ymid, u1, zs, zf, ct0):
    def first(z, _):
        for _, rows, (c, w, e, s, n) in planes(u, z):
            u1[z, rows, :] = advanced(
                c, w, e, s, n, u[z - 1, rows, :], u[z + 1, rows, :],
                vx[z, rows, :], vy[z, rows, :], vz[z, rows, :], d[z, rows, :],
            )
        return 0

    lax.fori_loop(1, LZ - 1, first, 0)
    u1[0] = jnp.zeros((NY, NX), F32)
    u1[LZ - 1] = jnp.zeros((NY, NX), F32)
    edge[0] = u1[1]
    edge[1] = u1[LZ - 2]

    def second(z, _):
        for _, rows, (c, w, e, s, n) in planes(u1, z):
            fin[z - 1, rows, :] = advanced(
                c, w, e, s, n, u1[z - 1, rows, :], u1[z + 1, rows, :],
                vx[z, rows, :], vy[z, rows, :], vz[z, rows, :], d[z, rows, :],
            )
        return 0

    lax.fori_loop(1, LZ - 1, second, 0)
    edge[2] = d[1] + jnp.maximum(vz[1], 0.0)
    edge[3] = d[LZ - 2] - jnp.minimum(vz[LZ - 2], 0.0)
    for zc in (1, 2):
        for r in range(0, NY, 8):
            rows = slice(r, r + 8)
            put_columns(zf, slice((zc - 1) * NY + r, (zc - 1) * NY + r + 8), fin[2 * zc - 1, rows, :] + fin[2 * zc, rows, :])
    for i in range(8):
        ymid[i] = paired(zf, i, 0, 64)

    for zc in range(4):
        for r in range(0, NY, 8):
            rows = slice(r, r + 8)
            put_columns(zs, slice(zc * NY + r, zc * NY + r + 8), u[2 * zc, rows, :] + u[2 * zc + 1, rows, :])
    for b in range(4):
        ct0[8 + 128 * b : 136 + 128 * b, :] = halved_x(
            jnp.concatenate([paired(zs, 2 * b + i, 0, 128) for i in range(2)], axis=1)
        )
    ct0[0:8, :] = ct0[CX : CX + 8, :]
    ct0[CX + 8 : CX + 16, :] = ct0[8:16, :]
    lane = lax.broadcasted_iota(jnp.int32, (64, CL), 1)
    for r in range(0, CX, 64):
        c = ct0[8 + r : 72 + r, :]
        xl, xh, yl, yh, zl, zh = coarse_coefs(*(ct[i, 8 + r : 72 + r, :] for i in range(4)))
        s, n = y_rolled(c, CL, 1)
        b = jnp.where(lane < 32, 0.0, pltpu.roll(c, 32, 1))
        t = jnp.where(lane >= 96, 0.0, pltpu.roll(c, 96, 1))
        w = ct0[7 + r : 71 + r, :]
        e = ct0[9 + r : 73 + r, :]
        gcp[r : r + 64, :] = c + (
            (xl * (w - c) + xh * (e - c)) + (yl * (s - c) + yh * (n - c)) + (zl * (b - c) + zh * (t - c))
        )
        cb[r : r + 64, :] = jnp.where(lane < 32, zl, jnp.where(lane >= 96, zh, 0.0))


def interior(state, fields, ct):
    small = jax.ShapeDtypeStruct((CX, CL), F32)
    return pl.pallas_call(
        interior_kernel,
        out_shape=[
            jax.ShapeDtypeStruct((LZ - 2, NY, NX), F32),
            jax.ShapeDtypeStruct((4, NY, NX), F32),
            small,
            small,
            jax.ShapeDtypeStruct((8, 64, 128), F32),
        ],
        in_specs=[whole()] * 6,
        out_specs=[whole()] * 5,
        scratch_shapes=[
            pltpu.VMEM((LZ, NY, NX), F32),
            pltpu.VMEM((8, 4 * NY, 128), F32),
            pltpu.VMEM((8, 2 * NY, 128), F32),
            pltpu.VMEM((CX + 16, CL), F32),
        ],
        compiler_params=params(16),
        cost_estimate=pl.CostEstimate(flops=60_000_000, bytes_accessed=20_000_000, transcendentals=0),
        name="interior",
    )(state, *fields, ct)


def finish_kernel(
    rnear, rfar, rfac, onear, ofar, ofac, w0, w1, w2, w3, fin, edge, vx, vy, vz, d, gcp, cb, ymid, ub, msg, gc, quad, u1, zs, jp
):
    mine = quad_rank()
    for i, window in enumerate((w0, w1, w2, w3)):
        quad[mine ^ i] = window[...]
    for kind, (rec, own, recb, ownb, at) in enumerate(
        ((rnear, onear, rnear, onear, FAR), (rfar, ofar, rfac, ofac, 0))
    ):
        top = edge_is_top(kind)
        side = jnp.where(top, 1, 0)
        for r in range(0, NY, 8):
            u1[kind, r : r + 8, :] = (
                own[NY + r : NY + r + 8, :] + ownb[at + r : at + r + 8, :] * rec[r : r + 8, :]
            )
        z = side * (LZ - 1)
        for r, rows, (c, w, e, s, n) in planes(u1, kind):
            outside = rec[NY + r : NY + r + 8, :] + recb[at + r : at + r + 8, :] * own[r : r + 8, :]
            inside = edge[side, rows, :]
            ax, ay, az, k = vx[z, rows, :], vy[z, rows, :], vz[z, rows, :], d[z, rows, :]
            last = advanced(c, w, e, s, n, inside, outside, ax, ay, jnp.where(top, az, -az), k)
            near = fin[5 * side, rows, :] + edge[2 + side, rows, :] * c
            ub[3 * side, rows, :] = last
            ub[1 + side, rows, :] = near
            put_columns(zs.at[side], rows, last + near)
    lane = lax.broadcasted_iota(jnp.int32, (128, 128), 1)
    hnear = jnp.concatenate([rnear[2 * NY : FAR, 128 * i : 128 * i + 128] for i in range(8)], axis=0)
    hfar = jnp.concatenate([rfar[2 * NY : FAR, 128 * i : 128 * i + 128] for i in range(8)], axis=0)
    first_core = lax.axis_index("core") == 0
    halo_lo, halo_hi = jnp.where(first_core, hfar, hnear), jnp.where(first_core, hnear, hfar)
    for b in range(4):
        rows = slice(128 * b, 128 * b + 128)
        t = halved_x(
            jnp.concatenate(
                [
                    jnp.concatenate([paired(zs.at[0], i, 0, 32), ymid[i], paired(zs.at[1], i, 0, 32)], axis=0)
                    for i in (2 * b, 2 * b + 1)
                ],
                axis=1,
            )
        )
        hl = pltpu.roll(halo_lo, (128 - 32 * b) % 128, 1) if b else halo_lo
        hh = pltpu.roll(halo_hi, (96 - 32 * b) % 128, 1) if b != 3 else halo_hi
        halo = jnp.where(lane < 32, hl, hh)
        g = gcp[rows, :] + cb[rows, :] * halo
        g = jnp.where(lax.axis_index("tm") == 0, 0.0, g)
        gc[rows, :] = g
        jp[8 + 128 * b : 136 + 128 * b, :] = t - g
    jp[0:8, :] = jp[CX : CX + 8, :]
    jp[CX + 8 : CX + 24, :] = jp[8:24, :]
    for i in range(BLOCKS):
        msg[i] = jp[XB * i : XB * i + WIN, :]


def finish(messages, windows, fin, edge, fields, gcp, cb, ymid):
    return pl.pallas_call(
        finish_kernel,
        out_shape=[
            jax.ShapeDtypeStruct((4, NY, NX), F32),
            jax.ShapeDtypeStruct((BLOCKS, WIN, CL), F32),
            jax.ShapeDtypeStruct((CX, CL), F32),
            jax.ShapeDtypeStruct((QUAD, 4, WIN, CL), F32),
        ],
        in_specs=[whole()] * 19,
        out_specs=[whole()] * 4,
        scratch_shapes=[
            pltpu.VMEM((2, NY, NX), F32),
            pltpu.VMEM((2, 8, NY, 128), F32),
            pltpu.VMEM((CX + 24, CL), F32),
        ],
        compiler_params=params(16),
        name="finish",
    )(*messages, *windows, fin, edge, *fields, gcp, cb, ymid)


HALO = 13
SHARED = ((0, 6, 96), (1, 5, 64), (2, 4, 32))


def pick_kernel(got, quad, even, odd):
    lane = lax.broadcasted_iota(jnp.int32, (WIN, CL), 1)
    for parity, out in enumerate((even, odd)):
        up = lax.rem(lax.axis_index("px"), 2) == parity
        near, far = jnp.where(up, 3, 0), jnp.where(up, 2, 1)

        def shared(main, other, width):
            return jnp.where(
                up,
                jnp.where(lane >= CL - width, main, pltpu.roll(other, CL - width, 1)),
                jnp.where(lane < width, main, pltpu.roll(other, width, 1)),
            )

        for j in range(4):
            out[j] = got[QUAD * j + near]
            out[7 + j] = quad[near, j]
        for j, other, width in SHARED:
            out[4 + j] = shared(got[QUAD * j + far], got[QUAD * other + near], width)
        for j in range(2):
            out[11 + j] = shared(quad[far, 2 * j], quad[far, 2 * j + 1], 64)


def pick(got, quad):
    halo = jax.ShapeDtypeStruct((HALO, WIN, CL), F32)
    return pl.pallas_call(
        pick_kernel,
        out_shape=[halo, halo],
        in_specs=[whole()] * 2,
        out_specs=[whole(), whole()],
        compiler_params=params(16),
        name="pick",
    )(got, quad)


LANES = 8 * CL


def chain_kernel(got, quad, even, odd, out, src, cf, e):
    first = lax.rem(lax.axis_index("px"), 2) == 0

    def below(i):
        return jnp.where(first, odd[i], even[i])

    def above(i):
        return jnp.where(first, even[i], odd[i])

    def put_coefs(values, lanes):
        for i, value in enumerate(coarse_coefs(*values)):
            cf[i, :, lanes] = value

    for j in range(7):
        for q in range(QUAD):
            src[j, :, (2 + q) * CL : (3 + q) * CL] = got[QUAD * j + q]
        for halo, near, far in ((below, 1, 0), (above, 6, 7)):
            if j < 4:
                src[j, :, near * CL : near * CL + CL] = halo(j)
            if j >= 3:
                src[j, :, far * CL : far * CL + CL] = jnp.zeros((WIN, CL), F32)
    for halo, near, far in ((below, 1, 0), (above, 6, 7)):
        for j, other, width in SHARED:
            turn = width if near == 1 else CL - width
            block = halo(4 + j)
            src[j, :, far * CL : far * CL + CL] = block
            src[other, :, near * CL : near * CL + CL] = pltpu.roll(block, turn, 1)
        put_coefs([halo(7 + i) for i in range(4)], slice(near * CL, near * CL + CL))
        pairs = [halo(11), halo(12)]
        put_coefs(
            [pairs[0], pltpu.roll(pairs[0], 64, 1), pairs[1], pltpu.roll(pairs[1], 64, 1)],
            slice(far * CL, far * CL + CL),
        )
    for q in range(QUAD):
        put_coefs([quad[q, comp] for comp in range(4)], slice((2 + q) * CL, (3 + q) * CL))
    for q in range(QUAD):
        out[q] = jnp.zeros((XB, CL), F32)
    e[...] = src[0]
    for k in range(1, GROUPS):
        c = e[...]
        s, n = y_rolled(c, LANES, 1)
        w, x = pltpu.roll(c, 1, 0), pltpu.roll(c, WIN - 1, 0)
        b, t = pltpu.roll(c, 32, 1), pltpu.roll(c, LANES - 32, 1)
        y = c + (
            (cf[0] * (w - c) + cf[1] * (x - c))
            + (cf[2] * (s - c) + cf[3] * (n - c))
            + (cf[4] * (b - c) + cf[5] * (t - c))
        )
        for q in range(QUAD):
            out[QUAD * k + q] = y[8 : 8 + XB, (2 + q) * CL : (3 + q) * CL]
        if k < GROUPS - 1:
            e[...] = y + src[k]


def chain(got, quad, even, odd):
    return pl.pallas_call(
        chain_kernel,
        out_shape=jax.ShapeDtypeStruct((BLOCKS, XB, CL), F32),
        in_specs=[whole()] * 4,
        out_specs=whole(),
        scratch_shapes=[
            pltpu.VMEM((7, WIN, LANES), F32),
            pltpu.VMEM((6, WIN, LANES), F32),
            pltpu.VMEM((WIN, LANES), F32),
        ],
        compiler_params=params(24),
        name="chain",
    )(got, quad, even, odd)


def result_kernel(y, gc, fin, ub, out, buf, sems):
    copy_y = table((256, CL), lambda r, c: r // 2 == c)
    copy_x = table((128, 256), lambda r, c: r == c // 2)
    copies = []
    for b in range(4):
        rows = slice(128 * b, 128 * b + 128)
        cols = slice(256 * b, 256 * b + 256)
        parts = split3(y[rows, :] - gc[rows, :])
        fine = sum(dot(dot(copy_y, p, 1, 1).astype(BF16), copy_x, 1, 0) for p in parts)
        for z in range(LZ):
            base = fin[z - 1, :, cols] if 2 <= z < 6 else ub[z if z < 2 else z - 4, :, cols]
            buf[z, :, cols] = base + fine[z // 2 * NY : z // 2 * NY + NY, :]
        copies.append(pltpu.make_async_copy(buf.at[:, :, cols], out.at[:, :, cols], sems.at[b]))
        copies[b].start()
    for copy in copies:
        copy.wait()


def result(y, gc, fin, ub):
    return pl.pallas_call(
        result_kernel,
        out_shape=jax.ShapeDtypeStruct((LZ, NY, NX), F32),
        in_specs=[whole()] * 4,
        out_specs=remains(),
        scratch_shapes=[pltpu.VMEM((LZ, NY, NX), F32), pltpu.SemaphoreType.DMA((4,))],
        compiler_params=params(16),
        name="result",
    )(y, gc, fin, ub)


def swap(value, axes, partner):
    pairs = [(i, partner(i)) for i in range(lax.axis_size(axes))]
    return lax.ppermute(value, axes, [(i, j) for i, j in pairs if j is not None])


def off_chip(i):
    j = i + 1 if i % 2 else i - 1
    return j if 0 <= j < 16 else None


def off_chip_copy(i):
    j = off_chip(i % 16)
    return None if j is None else (i // 16 ^ 1) * 16 + j


def quad_beside(i):
    j = i + 1 if i % 2 else i - 1
    return j if 0 <= j < 4 else None


def shards(state_old, velocity, diffusivity):
    state = state_old[0]
    onear, ofar, ofac = edges(state, velocity, diffusivity)
    rnear = swap(onear, SPACE, lambda i: i ^ 1)
    rfar = swap(ofar, SPACE, off_chip)
    rfac = swap(ofac, ("tm",) + SPACE, off_chip_copy)
    ct, w0, w1, w2, w3, u, *fields = coefs(state, velocity, diffusivity)
    windows = (
        w0,
        swap(w1, SPACE, lambda i: i ^ 1),
        swap(w2, ("tm",) + SPACE, lambda i: i ^ 18),
        swap(w3, ("tm",) + SPACE, lambda i: i ^ 19),
    )
    fin, edge, gcp, cb, ymid = interior(u, fields, ct)
    messages = (rnear, rfar, rfac, onear, ofar, ofac)
    ub, msg, gc, quad = finish(messages, windows, fin, edge, fields, gcp, cb, ymid)
    got = lax.all_to_all(msg, GROUP, 0, 0)
    even, odd = pick(got, quad)
    even = swap(even, "px", lambda i: i ^ 1)
    odd = swap(odd, "px", quad_beside)
    back = lax.all_to_all(chain(got, quad, even, odd), GROUP, 0, 0)
    return result(back.reshape(CX, CL), gc, fin, ub)[None]


def solution(mesh):
    fine_mesh = Mesh(mesh.devices.reshape(GROUPS, 4, 2, 2), ("tm",) + SPACE)
    return jax.shard_map(
        shards,
        mesh=fine_mesh,
        in_specs=(
            P("tm", SPACE, None, None),
            P(None, SPACE, None, None),
            P(SPACE, None, None),
        ),
        out_specs=P("tm", SPACE, None, None),
        check_vma=False,
    )
```

```python
import jax
import jax.numpy as jnp
from jax import lax
from jax.experimental import pallas as pl
from jax.experimental.pallas import tpu as pltpu
from jax.sharding import Mesh
from jax.sharding import PartitionSpec as P

F32 = jnp.float32
BF16 = jnp.bfloat16
NY, NX = 64, 1024
LZ = 8
CX, CL = 512, 128
GROUPS = 8
QUAD = 4
BLOCKS = GROUPS * QUAD
XB = CX // BLOCKS
WIN = XB + 16
SPACE = ("px", "pz", "core")
GROUP = ("tm", "pz", "core")


def params(mib):
    return pltpu.CompilerParams(vmem_limit_bytes=mib * 1024 * 1024)


def split3(x):
    hi = x.astype(BF16)
    rest = x - hi.astype(F32)
    mid = rest.astype(BF16)
    return hi, mid, (rest - mid.astype(F32)).astype(BF16)


def dot(a, b, ca, cb):
    return lax.dot_general(a, b, (((ca,), (cb,)), ((), ())), preferred_element_type=F32)


def table(shape, test):
    rows = lax.broadcasted_iota(jnp.int32, shape, 0)
    cols = lax.broadcasted_iota(jnp.int32, shape, 1)
    return test(rows, cols).astype(F32).astype(BF16)


def halved_x(part):
    halve = table((128, 256), lambda r, c: r == c // 2)
    return sum(dot(halve, p, 1, 1) for p in split3(part)) * 0.125


def put_columns(ref, at, value):
    for i in range(NX // 128):
        ref[i, at, :] = value[:, 128 * i : 128 * i + 128]


def paired(ref, column, first, rows):
    return ref[column, pl.ds(first, rows, 2), :] + ref[column, pl.ds(first + 1, rows, 2), :]


def advanced(c, w, e, s, n, b, t, ax, ay, az, k):
    lap = ((w + e) + (s + n)) + ((b + t) - 6.0 * c)
    dx = jnp.abs(ax) * (jnp.where(ax > 0, w, e) - c)
    dy = jnp.abs(ay) * (jnp.where(ay > 0, s, n) - c)
    dz = jnp.abs(az) * (jnp.where(az > 0, b, t) - c)
    return (c + k * lap) + ((dx + dy) + dz)


def planes(ref, z):
    row = lax.broadcasted_iota(jnp.int32, (8, NX), 0)
    c = ref[z, 0:8, :]
    before = pltpu.roll(ref[z, NY - 8 : NY, :], 1, 0)
    for r in range(0, NY, 8):
        after = ref[z, (r + 8) % NY : (r + 8) % NY + 8, :]
        down = pltpu.roll(c, 1, 0)
        s = jnp.where(row == 0, before, down)
        n = jnp.where(row == 7, pltpu.roll(after, 7, 0), pltpu.roll(c, 7, 0))
        yield r, slice(r, r + 8), (c, pltpu.roll(c, 1, 1), pltpu.roll(c, NX - 1, 1), s, n)
        c, before = after, down


def coarse_coefs(vx, vy, vz, k):
    half = 0.5 * k
    out = []
    for a in (vx, vy, vz):
        out += [half + jnp.maximum(a, 0.0), half - jnp.minimum(a, 0.0)]
    return out


def lane_neighbours(c):
    y = lax.rem(lax.broadcasted_iota(jnp.int32, c.shape, 1), 32)
    below, above = pltpu.roll(c, 32, 1), pltpu.roll(c, CL - 32, 1)
    s = pltpu.roll(jnp.where(y == 31, above, c), 1, 1)
    n = pltpu.roll(jnp.where(y == 0, below, c), CL - 1, 1)
    return below, above, s, n


FAR = 2 * NY + 16
NEAR = FAR + NY
CROWS = CX + 32


def edge_is_top(kind):
    return lax.axis_index("core") == kind


def edges_kernel(st, vel, dif, near, far, factor, u, v, d, zs, sems):
    tops = [edge_is_top(kind) for kind in range(2)]
    copies = []
    for kind, top in enumerate(tops):
        z, beside = jnp.where(top, LZ - 1, 0), jnp.where(top, LZ - 2, 1)
        pairs = (
            (st.at[z], u.at[kind]),
            (vel.at[:, z], v.at[kind]),
            (dif.at[z], d.at[kind]),
            (st.at[beside], u.at[2 + kind]),
        )
        copies.append([pltpu.make_async_copy(a, b, sems.at[kind, i]) for i, (a, b) in enumerate(pairs)])
    for kind in (1, 0):
        for copy in copies[kind]:
            copy.start()
    for kind in (1, 0):
        top, out = tops[kind], (near, far)[kind]
        for copy in copies[kind]:
            copy.wait()
        for r, rows, (c, w, e, s, n) in planes(u, kind):
            inside = u[2 + kind, rows, :]
            ax, ay, k = v[kind, 0, rows, :], v[kind, 1, rows, :], d[kind, rows, :]
            up = jnp.where(top, v[kind, 2, rows, :], -v[kind, 2, rows, :])
            out[r : r + 8, :] = c
            out[NY + r : NY + r + 8, :] = advanced(c, w, e, s, n, inside, jnp.zeros_like(c), ax, ay, up, k)
            b = k - jnp.minimum(up, 0.0)
            if kind == 0:
                near[FAR + r : FAR + r + 8, :] = b
            else:
                factor[rows, :] = b
            put_columns(zs, slice(kind * NY + r, kind * NY + r + 8), c + inside)
    lane = lax.broadcasted_iota(jnp.int32, (128, 128), 1)
    cnear = jnp.zeros((128, 128), F32)
    cfar = jnp.zeros((128, 128), F32)
    for b in range(4):
        part = jnp.concatenate([paired(zs, 2 * b + i, 0, 64) for i in range(2)], axis=1)
        t = halved_x(jnp.concatenate([part, jnp.zeros_like(part)], axis=0))
        tn = jnp.where(lane < 32, t, 0.0)
        tf = jnp.where((lane >= 32) & (lane < 64), t, 0.0)
        cnear += pltpu.roll(tn, 32 * b, 1) if b else tn
        cfar += pltpu.roll(tf, (32 * b - 32) % 128, 1) if b != 1 else tf
    for i in range(8):
        near[2 * NY : FAR, 128 * i : 128 * i + 128] = cnear[16 * i : 16 * i + 16, :]
        far[2 * NY : FAR, 128 * i : 128 * i + 128] = cfar[16 * i : 16 * i + 16, :]


def whole():
    return pl.BlockSpec(memory_space=pltpu.VMEM)


def remains():
    return pl.BlockSpec(memory_space=pltpu.HBM)


def edges(state, velocity, diffusivity):
    return pl.pallas_call(
        edges_kernel,
        out_shape=[
            jax.ShapeDtypeStruct((NEAR, NX), F32),
            jax.ShapeDtypeStruct((FAR, NX), F32),
            jax.ShapeDtypeStruct((NY, NX), F32),
        ],
        in_specs=[remains()] * 3,
        out_specs=[whole()] * 3,
        scratch_shapes=[
            pltpu.VMEM((4, NY, NX), F32),
            pltpu.VMEM((2, 3, NY, NX), F32),
            pltpu.VMEM((2, NY, NX), F32),
            pltpu.VMEM((8, 2 * NY, 128), F32),
            pltpu.SemaphoreType.DMA((2, 4)),
        ],
        compiler_params=params(52),
        name="edges",
    )(state, velocity, diffusivity)


def quad_rank():
    return lax.axis_index("pz") * 2 + lax.axis_index("core")


def coefs_kernel(vel, dif, ct, w0, w1, w2, w3, vx, vy, vz, d, zs, sems):
    fields = (vx, vy, vz, d)

    def part(comp, zc):
        layers = slice(2 * zc, 2 * zc + 2)
        source = dif.at[layers] if comp == 3 else vel.at[comp, layers]
        return pltpu.make_async_copy(source, fields[comp].at[layers], sems.at[comp, zc])

    for comp in range(4):
        for zc in range(4):
            part(comp, zc).start()
    for comp, ref in enumerate(fields):
        for zc in range(4):
            part(comp, zc).wait()
            for r in range(0, NY, 8):
                rows = slice(r, r + 8)
                put_columns(
                    zs.at[comp], slice(zc * NY + r, zc * NY + r + 8), ref[2 * zc, rows, :] + ref[2 * zc + 1, rows, :]
                )
        for b in range(4):
            ct[comp, 8 + 128 * b : 136 + 128 * b, :] = halved_x(
                jnp.concatenate([paired(zs.at[comp], 2 * b + i, 0, 128) for i in range(2)], axis=1)
            )
        ct[comp, 0:8, :] = ct[comp, CX : CX + 8, :]
        ct[comp, CX + 8 : CX + 32, :] = ct[comp, 8:32, :]
    mine = quad_rank()
    for i, out in enumerate((w0, w1, w2, w3)):
        slice_index = lax.axis_index("tm")
        block = (slice_index if i < 2 else slice_index ^ 1) * QUAD + (mine ^ i)
        for comp in range(4):
            out[comp] = ct[comp, pl.ds(pl.multiple_of(block * XB, XB), WIN), :]


def coefs(velocity, diffusivity):
    window = jax.ShapeDtypeStruct((4, WIN, CL), F32)
    slab = jax.ShapeDtypeStruct((LZ, NY, NX), F32)
    return pl.pallas_call(
        coefs_kernel,
        out_shape=[jax.ShapeDtypeStruct((4, CROWS, CL), F32)] + [window] * 4 + [slab] * 4,
        in_specs=[remains()] * 2,
        out_specs=[whole()] * 9,
        scratch_shapes=[
            pltpu.VMEM((4, 8, 4 * NY, 128), F32),
            pltpu.SemaphoreType.DMA((4, 4)),
        ],
        compiler_params=params(44),
        cost_estimate=pl.CostEstimate(flops=20_000_000, bytes_accessed=9_000_000, transcendentals=0),
        name="coefs",
    )(velocity, diffusivity)


def interior_kernel(u, vx, vy, vz, d, ct, fin, edge, gcp, cb, ymid, u1, zs, zf, ct0):
    def first(z, _):
        for _, rows, (c, w, e, s, n) in planes(u, z):
            u1[z, rows, :] = advanced(
                c, w, e, s, n, u[z - 1, rows, :], u[z + 1, rows, :],
                vx[z, rows, :], vy[z, rows, :], vz[z, rows, :], d[z, rows, :],
            )
        return 0

    lax.fori_loop(1, LZ - 1, first, 0)
    u1[0] = jnp.zeros((NY, NX), F32)
    u1[LZ - 1] = jnp.zeros((NY, NX), F32)
    edge[0] = u1[1]
    edge[1] = u1[LZ - 2]

    def second(z, _):
        for _, rows, (c, w, e, s, n) in planes(u1, z):
            fin[z - 1, rows, :] = advanced(
                c, w, e, s, n, u1[z - 1, rows, :], u1[z + 1, rows, :],
                vx[z, rows, :], vy[z, rows, :], vz[z, rows, :], d[z, rows, :],
            )
        return 0

    lax.fori_loop(1, LZ - 1, second, 0)
    edge[2] = d[1] + jnp.maximum(vz[1], 0.0)
    edge[3] = d[LZ - 2] - jnp.minimum(vz[LZ - 2], 0.0)
    for zc in (1, 2):
        for r in range(0, NY, 8):
            rows = slice(r, r + 8)
            put_columns(zf, slice((zc - 1) * NY + r, (zc - 1) * NY + r + 8), fin[2 * zc - 1, rows, :] + fin[2 * zc, rows, :])
    for i in range(8):
        ymid[i] = paired(zf, i, 0, 64)

    for zc in range(4):
        for r in range(0, NY, 8):
            rows = slice(r, r + 8)
            put_columns(zs, slice(zc * NY + r, zc * NY + r + 8), u[2 * zc, rows, :] + u[2 * zc + 1, rows, :])
    for b in range(4):
        ct0[8 + 128 * b : 136 + 128 * b, :] = halved_x(
            jnp.concatenate([paired(zs, 2 * b + i, 0, 128) for i in range(2)], axis=1)
        )
    ct0[0:8, :] = ct0[CX : CX + 8, :]
    ct0[CX + 8 : CX + 16, :] = ct0[8:16, :]
    lane = lax.broadcasted_iota(jnp.int32, (64, CL), 1)
    for r in range(0, CX, 64):
        c = ct0[8 + r : 72 + r, :]
        xl, xh, yl, yh, zl, zh = coarse_coefs(*(ct[i, 8 + r : 72 + r, :] for i in range(4)))
        b, t, s, n = lane_neighbours(c)
        b = jnp.where(lane < 32, 0.0, b)
        t = jnp.where(lane >= 96, 0.0, t)
        w = ct0[7 + r : 71 + r, :]
        e = ct0[9 + r : 73 + r, :]
        gcp[r : r + 64, :] = c + (
            (xl * (w - c) + xh * (e - c)) + (yl * (s - c) + yh * (n - c)) + (zl * (b - c) + zh * (t - c))
        )
        cb[r : r + 64, :] = jnp.where(lane < 32, zl, jnp.where(lane >= 96, zh, 0.0))


def interior(state, fields, ct):
    small = jax.ShapeDtypeStruct((CX, CL), F32)
    return pl.pallas_call(
        interior_kernel,
        out_shape=[
            jax.ShapeDtypeStruct((LZ - 2, NY, NX), F32),
            jax.ShapeDtypeStruct((4, NY, NX), F32),
            small,
            small,
            jax.ShapeDtypeStruct((8, 64, 128), F32),
        ],
        in_specs=[whole()] * 6,
        out_specs=[whole()] * 5,
        scratch_shapes=[
            pltpu.VMEM((LZ, NY, NX), F32),
            pltpu.VMEM((8, 4 * NY, 128), F32),
            pltpu.VMEM((8, 2 * NY, 128), F32),
            pltpu.VMEM((CX + 16, CL), F32),
        ],
        compiler_params=params(16),
        cost_estimate=pl.CostEstimate(flops=60_000_000, bytes_accessed=20_000_000, transcendentals=0),
        name="interior",
    )(state, *fields, ct)


def finish_kernel(
    rnear, rfar, rfac, onear, ofar, ofac, w0, w1, w2, w3, fin, edge, vx, vy, vz, d, gcp, cb, ymid, ub, msg, gc, quad, u1, zs, jp
):
    mine = quad_rank()
    for i, window in enumerate((w0, w1, w2, w3)):
        quad[mine ^ i] = window[...]
    for kind, (rec, own, recb, ownb, at) in enumerate(
        ((rnear, onear, rnear, onear, FAR), (rfar, ofar, rfac, ofac, 0))
    ):
        top = edge_is_top(kind)
        side = jnp.where(top, 1, 0)
        for r in range(0, NY, 8):
            u1[kind, r : r + 8, :] = (
                own[NY + r : NY + r + 8, :] + ownb[at + r : at + r + 8, :] * rec[r : r + 8, :]
            )
        z = side * (LZ - 1)
        for r, rows, (c, w, e, s, n) in planes(u1, kind):
            outside = rec[NY + r : NY + r + 8, :] + recb[at + r : at + r + 8, :] * own[r : r + 8, :]
            inside = edge[side, rows, :]
            ax, ay, az, k = vx[z, rows, :], vy[z, rows, :], vz[z, rows, :], d[z, rows, :]
            last = advanced(c, w, e, s, n, inside, outside, ax, ay, jnp.where(top, az, -az), k)
            near = fin[5 * side, rows, :] + edge[2 + side, rows, :] * c
            ub[3 * side, rows, :] = last
            ub[1 + side, rows, :] = near
            put_columns(zs.at[side], rows, last + near)
    lane = lax.broadcasted_iota(jnp.int32, (128, 128), 1)
    hnear = jnp.concatenate([rnear[2 * NY : FAR, 128 * i : 128 * i + 128] for i in range(8)], axis=0)
    hfar = jnp.concatenate([rfar[2 * NY : FAR, 128 * i : 128 * i + 128] for i in range(8)], axis=0)
    first_core = lax.axis_index("core") == 0
    halo_lo, halo_hi = jnp.where(first_core, hfar, hnear), jnp.where(first_core, hnear, hfar)
    for b in range(4):
        rows = slice(128 * b, 128 * b + 128)
        t = halved_x(
            jnp.concatenate(
                [
                    jnp.concatenate([paired(zs.at[0], i, 0, 32), ymid[i], paired(zs.at[1], i, 0, 32)], axis=0)
                    for i in (2 * b, 2 * b + 1)
                ],
                axis=1,
            )
        )
        hl = pltpu.roll(halo_lo, (128 - 32 * b) % 128, 1) if b else halo_lo
        hh = pltpu.roll(halo_hi, (96 - 32 * b) % 128, 1) if b != 3 else halo_hi
        halo = jnp.where(lane < 32, hl, hh)
        g = gcp[rows, :] + cb[rows, :] * halo
        g = jnp.where(lax.axis_index("tm") == 0, 0.0, g)
        gc[rows, :] = g
        jp[8 + 128 * b : 136 + 128 * b, :] = t - g
    jp[0:8, :] = jp[CX : CX + 8, :]
    jp[CX + 8 : CX + 24, :] = jp[8:24, :]
    for i in range(BLOCKS):
        msg[i] = jp[XB * i : XB * i + WIN, :]


def finish(messages, windows, fin, edge, fields, gcp, cb, ymid):
    return pl.pallas_call(
        finish_kernel,
        out_shape=[
            jax.ShapeDtypeStruct((4, NY, NX), F32),
            jax.ShapeDtypeStruct((BLOCKS, WIN, CL), F32),
            jax.ShapeDtypeStruct((CX, CL), F32),
            jax.ShapeDtypeStruct((QUAD, 4, WIN, CL), F32),
        ],
        in_specs=[whole()] * 19,
        out_specs=[whole()] * 4,
        scratch_shapes=[
            pltpu.VMEM((2, NY, NX), F32),
            pltpu.VMEM((2, 8, NY, 128), F32),
            pltpu.VMEM((CX + 24, CL), F32),
        ],
        compiler_params=params(16),
        name="finish",
    )(*messages, *windows, fin, edge, *fields, gcp, cb, ymid)


HALO = 13
SHARED = ((0, 6, 96), (1, 5, 64), (2, 4, 32))


def pick_kernel(got, quad, even, odd):
    lane = lax.broadcasted_iota(jnp.int32, (WIN, CL), 1)
    for parity, out in enumerate((even, odd)):
        up = lax.rem(lax.axis_index("px"), 2) == parity
        near, far = jnp.where(up, 3, 0), jnp.where(up, 2, 1)

        def shared(main, other, width):
            return jnp.where(
                up,
                jnp.where(lane >= CL - width, main, pltpu.roll(other, CL - width, 1)),
                jnp.where(lane < width, main, pltpu.roll(other, width, 1)),
            )

        for j in range(4):
            out[j] = got[QUAD * j + near]
            out[7 + j] = quad[near, j]
        for j, other, width in SHARED:
            out[4 + j] = shared(got[QUAD * j + far], got[QUAD * other + near], width)
        for j in range(2):
            out[11 + j] = shared(quad[far, 2 * j], quad[far, 2 * j + 1], 64)


def pick(got, quad):
    halo = jax.ShapeDtypeStruct((HALO, WIN, CL), F32)
    return pl.pallas_call(
        pick_kernel,
        out_shape=[halo, halo],
        in_specs=[whole()] * 2,
        out_specs=[whole(), whole()],
        compiler_params=params(16),
        name="pick",
    )(got, quad)


def chain_kernel(got, quad, even, odd, out, cf, e):
    first = lax.rem(lax.axis_index("px"), 2) == 0

    def below(i):
        return jnp.where(first, odd[i], even[i])

    def above(i):
        return jnp.where(first, even[i], odd[i])

    def source(j, block):
        if 2 <= block < 6:
            return got[QUAD * j + block - 2]
        halo = below if block < 2 else above
        if block in (0, 7):
            return halo(4 + j) if j < 3 else None
        if j < 4:
            return halo(j)
        _, other, width = SHARED[6 - j]
        return pltpu.roll(halo(10 - j), width if block == 1 else CL - width, 1)

    for block in range(8):
        halo = below if block < 2 else above
        if 2 <= block < 6:
            values = [quad[block - 2, i] for i in range(4)]
        elif block in (1, 6):
            values = [halo(7 + i) for i in range(4)]
        else:
            values = []
            for i in (11, 12):
                values += [halo(i), pltpu.roll(halo(i), 64, 1)]
        for i, value in enumerate(coarse_coefs(*values)):
            cf[i, block] = value
        e[0, block] = source(0, block)
    for q in range(QUAD):
        out[q] = jnp.zeros((XB, CL), F32)
    lane = lax.broadcasted_iota(jnp.int32, (WIN, CL), 1)
    for k in range(1, GROUPS):
        now, later = (k - 1) % 2, k % 2
        low = 0 if k < 3 else 1 if k < 7 else 2
        reach = range(max(0, low - 1), min(8, 9 - low))
        near = {b: lane_neighbours(e[now, b]) for b in reach}
        for block in range(low, 8 - low):
            c = e[now, block]
            b, t, s, n = near[block]
            if block > 0:
                b = jnp.where(lane < 32, near[block - 1][0], b)
            if block < 7:
                t = jnp.where(lane >= 96, near[block + 1][1], t)
            w, x = pltpu.roll(c, 1, 0), pltpu.roll(c, WIN - 1, 0)
            y = c + (
                (cf[0, block] * (w - c) + cf[1, block] * (x - c))
                + (cf[2, block] * (s - c) + cf[3, block] * (n - c))
                + (cf[4, block] * (b - c) + cf[5, block] * (t - c))
            )
            if 2 <= block < 6:
                out[QUAD * k + block - 2] = y[8 : 8 + XB, :]
            if k < GROUPS - 1:
                more = source(k, block)
                e[later, block] = y if more is None else y + more


def chain(got, quad, even, odd):
    return pl.pallas_call(
        chain_kernel,
        out_shape=jax.ShapeDtypeStruct((BLOCKS, XB, CL), F32),
        in_specs=[whole()] * 4,
        out_specs=whole(),
        scratch_shapes=[
            pltpu.VMEM((6, 8, WIN, CL), F32),
            pltpu.VMEM((2, 8, WIN, CL), F32),
        ],
        compiler_params=params(24),
        name="chain",
    )(got, quad, even, odd)


def result_kernel(y, gc, fin, ub, out, copied, buf, sems):
    copy_y = table((256, CL), lambda r, c: r // 2 == c)
    copy_x = table((128, 256), lambda r, c: r == c // 2)
    for b in range(4):
        rows = slice(128 * b, 128 * b + 128)
        for i, part in enumerate(split3(y[rows, :] - gc[rows, :])):
            copied[i, :, rows] = dot(copy_y, part, 1, 1).astype(BF16)
    copies = []
    for zc in range(4):
        rows = slice(zc * NY, zc * NY + NY)
        for b in range(4):
            cols = slice(256 * b, 256 * b + 256)
            fine = sum(dot(copied[i, rows, 128 * b : 128 * b + 128], copy_x, 1, 0) for i in range(3))
            for z in (2 * zc, 2 * zc + 1):
                base = fin[z - 1, :, cols] if 2 <= z < 6 else ub[z if z < 2 else z - 4, :, cols]
                buf[z, :, cols] = base + fine
        layers = slice(2 * zc, 2 * zc + 2)
        copies.append(pltpu.make_async_copy(buf.at[layers], out.at[layers], sems.at[zc]))
        copies[zc].start()
    for copy in copies:
        copy.wait()


def result(y, gc, fin, ub):
    return pl.pallas_call(
        result_kernel,
        out_shape=jax.ShapeDtypeStruct((LZ, NY, NX), F32),
        in_specs=[whole()] * 4,
        out_specs=remains(),
        scratch_shapes=[
            pltpu.VMEM((3, 4 * NY, CX), BF16),
            pltpu.VMEM((LZ, NY, NX), F32),
            pltpu.SemaphoreType.DMA((4,)),
        ],
        compiler_params=params(16),
        name="result",
    )(y, gc, fin, ub)


def swap(value, axes, partner):
    pairs = [(i, partner(i)) for i in range(lax.axis_size(axes))]
    return lax.ppermute(value, axes, [(i, j) for i, j in pairs if j is not None])


def off_chip(i):
    j = i + 1 if i % 2 else i - 1
    return j if 0 <= j < 16 else None


def off_chip_copy(i):
    j = off_chip(i % 16)
    return None if j is None else (i // 16 ^ 1) * 16 + j


def quad_beside(i):
    j = i + 1 if i % 2 else i - 1
    return j if 0 <= j < 4 else None


def shards(state_old, velocity, diffusivity):
    state = state_old[0]
    onear, ofar, ofac = edges(state, velocity, diffusivity)
    rnear = swap(onear, SPACE, lambda i: i ^ 1)
    rfar = swap(ofar, SPACE, off_chip)
    rfac = swap(ofac, ("tm",) + SPACE, off_chip_copy)
    ct, w0, w1, w2, w3, *fields = coefs(velocity, diffusivity)
    windows = (
        w0,
        swap(w1, SPACE, lambda i: i ^ 1),
        swap(w2, ("tm",) + SPACE, lambda i: i ^ 18),
        swap(w3, ("tm",) + SPACE, lambda i: i ^ 19),
    )
    fin, edge, gcp, cb, ymid = interior(state, fields, ct)
    messages = (rnear, rfar, rfac, onear, ofar, ofac)
    ub, msg, gc, quad = finish(messages, windows, fin, edge, fields, gcp, cb, ymid)
    got = lax.all_to_all(msg, GROUP, 0, 0)
    even, odd = pick(got, quad)
    even = swap(even, "px", lambda i: i ^ 1)
    odd = swap(odd, "px", quad_beside)
    back = lax.all_to_all(chain(got, quad, even, odd), GROUP, 0, 0)
    return result(back.reshape(CX, CL), gc, fin, ub)[None]


def solution(mesh):
    fine_mesh = Mesh(mesh.devices.reshape(GROUPS, 4, 2, 2), ("tm",) + SPACE)
    return jax.shard_map(
        shards,
        mesh=fine_mesh,
        in_specs=(
            P("tm", SPACE, None, None),
            P(None, SPACE, None, None),
            P(SPACE, None, None),
        ),
        out_specs=P("tm", SPACE, None, None),
        check_vma=False,
    )
```

```python
import functools

import jax
import jax.numpy as jnp
from jax import lax
from jax.experimental import pallas as pl
from jax.experimental.pallas import tpu as pltpu
from jax.sharding import Mesh
from jax.sharding import PartitionSpec as P

F32 = jnp.float32
BF16 = jnp.bfloat16
NY, NX = 64, 1024
LZ = 8
CX, CL = 512, 128
GROUPS = 8
QUAD = 4
BLOCKS = GROUPS * QUAD
XB = CX // BLOCKS
WIN = XB + 16
SPACE = ("px", "pz", "core")
GROUP = ("tm", "pz", "core")


def params(mib):
    return pltpu.CompilerParams(vmem_limit_bytes=mib * 1024 * 1024)


def split3(x):
    hi = x.astype(BF16)
    rest = x - hi.astype(F32)
    mid = rest.astype(BF16)
    return hi, mid, (rest - mid.astype(F32)).astype(BF16)


def dot(a, b, ca, cb):
    return lax.dot_general(a, b, (((ca,), (cb,)), ((), ())), preferred_element_type=F32)


def table(shape, test):
    rows = lax.broadcasted_iota(jnp.int32, shape, 0)
    cols = lax.broadcasted_iota(jnp.int32, shape, 1)
    return test(rows, cols).astype(F32).astype(BF16)


def halved_x(part):
    halve = table((128, 256), lambda r, c: r == c // 2)
    return sum(dot(halve, p, 1, 1) for p in split3(part)) * 0.125


def put_columns(ref, at, value):
    for i in range(NX // 128):
        ref[i, at, :] = value[:, 128 * i : 128 * i + 128]


def paired(ref, column, first, rows):
    return ref[column, pl.ds(first, rows, 2), :] + ref[column, pl.ds(first + 1, rows, 2), :]


def advanced(c, w, e, s, n, b, t, ax, ay, az, k):
    lap = ((w + e) + (s + n)) + ((b + t) - 6.0 * c)
    dx = jnp.abs(ax) * (jnp.where(ax > 0, w, e) - c)
    dy = jnp.abs(ay) * (jnp.where(ay > 0, s, n) - c)
    dz = jnp.abs(az) * (jnp.where(az > 0, b, t) - c)
    return (c + k * lap) + ((dx + dy) + dz)


def planes(ref, z):
    row = lax.broadcasted_iota(jnp.int32, (8, NX), 0)
    c = ref[z, 0:8, :]
    before = pltpu.roll(ref[z, NY - 8 : NY, :], 1, 0)
    for r in range(0, NY, 8):
        after = ref[z, (r + 8) % NY : (r + 8) % NY + 8, :]
        down = pltpu.roll(c, 1, 0)
        s = jnp.where(row == 0, before, down)
        n = jnp.where(row == 7, pltpu.roll(after, 7, 0), pltpu.roll(c, 7, 0))
        yield r, slice(r, r + 8), (c, pltpu.roll(c, 1, 1), pltpu.roll(c, NX - 1, 1), s, n)
        c, before = after, down


def coarse_coefs(vx, vy, vz, k):
    half = 0.5 * k
    out = []
    for a in (vx, vy, vz):
        out += [half + jnp.maximum(a, 0.0), half - jnp.minimum(a, 0.0)]
    return out


def lane_neighbours(c):
    y = lax.rem(lax.broadcasted_iota(jnp.int32, c.shape, 1), 32)
    below, above = pltpu.roll(c, 32, 1), pltpu.roll(c, CL - 32, 1)
    s = jnp.where(y == 0, pltpu.roll(c, CL - 31, 1), pltpu.roll(c, 1, 1))
    n = jnp.where(y == 31, pltpu.roll(c, 31, 1), pltpu.roll(c, CL - 1, 1))
    return below, above, s, n


FAR = 2 * NY + 16
TAIL = 16 + NY
CROWS = CX + 32


def edge_is_top(kind):
    return lax.axis_index("core") == kind


def edge_kernel(kind, st, vel, dif, *rest):
    if kind == 0:
        _, out, tail, u, v, d, zs, sems = rest
        coarse_out, coarse_at, factor, factor_at = tail, 0, tail, 16
    else:
        out, factor, u, v, d, zs, sems = rest
        coarse_out, coarse_at, factor_at = out, 2 * NY, 0
    top = edge_is_top(kind)
    z, beside = jnp.where(top, LZ - 1, 0), jnp.where(top, LZ - 2, 1)
    pairs = ((st.at[z], u.at[0]), (vel.at[:, z], v), (dif.at[z], d), (st.at[beside], u.at[1]))
    copies = [pltpu.make_async_copy(a, b, sems.at[i]) for i, (a, b) in enumerate(pairs)]
    for copy in copies:
        copy.start()
    for copy in copies:
        copy.wait()
    for r, rows, (c, w, e, s, n) in planes(u, 0):
        inside = u[1, rows, :]
        ax, ay, k = v[0, rows, :], v[1, rows, :], d[rows, :]
        up = jnp.where(top, v[2, rows, :], -v[2, rows, :])
        out[r : r + 8, :] = c
        out[NY + r : NY + r + 8, :] = advanced(c, w, e, s, n, inside, jnp.zeros_like(c), ax, ay, up, k)
        factor[factor_at + r : factor_at + r + 8, :] = k - jnp.minimum(up, 0.0)
        put_columns(zs, rows, c + inside)
    coarse = jnp.zeros((128, 128), F32)
    for b in range(4):
        part = jnp.concatenate([paired(zs, 2 * b + i, 0, 32) for i in range(2)], axis=1)
        t = halved_x(jnp.concatenate([part, jnp.zeros((96, 256), F32)], axis=0))
        coarse += pltpu.roll(t, 32 * b, 1) if b else t
    for i in range(8):
        coarse_out[coarse_at : coarse_at + 16, 128 * i : 128 * i + 128] = coarse[16 * i : 16 * i + 16, :]


def whole():
    return pl.BlockSpec(memory_space=pltpu.VMEM)


def remains():
    return pl.BlockSpec(memory_space=pltpu.HBM)


def edge_message(kind, state, velocity, diffusivity, *after):
    shapes = [((2 * NY, NX), (TAIL, NX)), ((FAR, NX), (NY, NX))][kind]
    return pl.pallas_call(
        functools.partial(edge_kernel, kind),
        out_shape=[jax.ShapeDtypeStruct(shape, F32) for shape in shapes],
        in_specs=[remains()] * 3 + [whole()] * len(after),
        out_specs=[whole()] * len(shapes),
        scratch_shapes=[
            pltpu.VMEM((2, NY, NX), F32),
            pltpu.VMEM((3, NY, NX), F32),
            pltpu.VMEM((NY, NX), F32),
            pltpu.VMEM((8, NY, 128), F32),
            pltpu.SemaphoreType.DMA((4,)),
        ],
        compiler_params=params([8, 52][kind]),
        cost_estimate=pl.CostEstimate(flops=15_000_000, bytes_accessed=[12_000_000, 3_000_000][kind], transcendentals=0),
        name=["near_message", "far_message"][kind],
    )(state, velocity, diffusivity, *after)


def quad_rank():
    return lax.axis_index("pz") * 2 + lax.axis_index("core")


def coefs_kernel(vel, dif, after, ct, w0, w1, w2, w3, zs):
    for comp in range(4):
        for zc in range(4):
            for r in range(0, NY, 8):
                rows = slice(r, r + 8)
                two = [dif[z, rows, :] if comp == 3 else vel[comp, z, rows, :] for z in (2 * zc, 2 * zc + 1)]
                put_columns(zs.at[comp], slice(zc * NY + r, zc * NY + r + 8), two[0] + two[1])
        for b in range(4):
            ct[comp, 8 + 128 * b : 136 + 128 * b, :] = halved_x(
                jnp.concatenate([paired(zs.at[comp], 2 * b + i, 0, 128) for i in range(2)], axis=1)
            )
        ct[comp, 0:8, :] = ct[comp, CX : CX + 8, :]
        ct[comp, CX + 8 : CX + 32, :] = ct[comp, 8:32, :]
    mine = quad_rank()
    slice_index = lax.axis_index("tm")
    for i, out in enumerate((w0, w1, w2, w3)):
        block = (slice_index if i < 2 else slice_index ^ 1) * QUAD + (mine ^ i)
        for comp in range(4):
            out[comp] = ct[comp, pl.ds(pl.multiple_of(block * XB, XB), WIN), :]


def coefs(velocity, diffusivity, after):
    window = jax.ShapeDtypeStruct((4, WIN, CL), F32)
    return pl.pallas_call(
        coefs_kernel,
        out_shape=[jax.ShapeDtypeStruct((4, CROWS, CL), F32)] + [window] * 4,
        in_specs=[whole()] * 3,
        out_specs=[whole()] * 5,
        scratch_shapes=[pltpu.VMEM((4, 8, 4 * NY, 128), F32)],
        compiler_params=params(12),
        cost_estimate=pl.CostEstimate(flops=20_000_000, bytes_accessed=9_000_000, transcendentals=0),
        name="coefs",
    )(velocity, diffusivity, after)


def interior_kernel(u, v, d, ct, after, fin, edge, gcp, cb, ymid, u1, zs, zf, ct0):
    def first(z, _):
        for _, rows, (c, w, e, s, n) in planes(u, z):
            u1[z, rows, :] = advanced(
                c, w, e, s, n, u[z - 1, rows, :], u[z + 1, rows, :],
                v[0, z, rows, :], v[1, z, rows, :], v[2, z, rows, :], d[z, rows, :],
            )
        return 0

    lax.fori_loop(1, LZ - 1, first, 0)
    u1[0] = jnp.zeros((NY, NX), F32)
    u1[LZ - 1] = jnp.zeros((NY, NX), F32)
    edge[0] = u1[1]
    edge[1] = u1[LZ - 2]

    def second(z, _):
        for _, rows, (c, w, e, s, n) in planes(u1, z):
            fin[z - 1, rows, :] = advanced(
                c, w, e, s, n, u1[z - 1, rows, :], u1[z + 1, rows, :],
                v[0, z, rows, :], v[1, z, rows, :], v[2, z, rows, :], d[z, rows, :],
            )
        return 0

    lax.fori_loop(1, LZ - 1, second, 0)
    edge[2] = d[1] + jnp.maximum(v[2, 1], 0.0)
    edge[3] = d[LZ - 2] - jnp.minimum(v[2, LZ - 2], 0.0)
    for zc in (1, 2):
        for r in range(0, NY, 8):
            rows = slice(r, r + 8)
            put_columns(zf, slice((zc - 1) * NY + r, (zc - 1) * NY + r + 8), fin[2 * zc - 1, rows, :] + fin[2 * zc, rows, :])
    for i in range(8):
        ymid[i] = paired(zf, i, 0, 64)

    for zc in range(4):
        for r in range(0, NY, 8):
            rows = slice(r, r + 8)
            put_columns(zs, slice(zc * NY + r, zc * NY + r + 8), u[2 * zc, rows, :] + u[2 * zc + 1, rows, :])
    for b in range(4):
        ct0[8 + 128 * b : 136 + 128 * b, :] = halved_x(
            jnp.concatenate([paired(zs, 2 * b + i, 0, 128) for i in range(2)], axis=1)
        )
    ct0[0:8, :] = ct0[CX : CX + 8, :]
    ct0[CX + 8 : CX + 16, :] = ct0[8:16, :]
    lane = lax.broadcasted_iota(jnp.int32, (64, CL), 1)
    for r in range(0, CX, 64):
        c = ct0[8 + r : 72 + r, :]
        xl, xh, yl, yh, zl, zh = coarse_coefs(*(ct[i, 8 + r : 72 + r, :] for i in range(4)))
        b, t, s, n = lane_neighbours(c)
        b = jnp.where(lane < 32, 0.0, b)
        t = jnp.where(lane >= 96, 0.0, t)
        w = ct0[7 + r : 71 + r, :]
        e = ct0[9 + r : 73 + r, :]
        gcp[r : r + 64, :] = c + (
            (xl * (w - c) + xh * (e - c)) + (yl * (s - c) + yh * (n - c)) + (zl * (b - c) + zh * (t - c))
        )
        cb[r : r + 64, :] = jnp.where(lane < 32, zl, jnp.where(lane >= 96, zh, 0.0))


def interior(state, velocity, diffusivity, ct, after):
    small = jax.ShapeDtypeStruct((CX, CL), F32)
    return pl.pallas_call(
        interior_kernel,
        out_shape=[
            jax.ShapeDtypeStruct((LZ - 2, NY, NX), F32),
            jax.ShapeDtypeStruct((4, NY, NX), F32),
            small,
            small,
            jax.ShapeDtypeStruct((8, 64, 128), F32),
        ],
        in_specs=[whole()] * 5,
        out_specs=[whole()] * 5,
        scratch_shapes=[
            pltpu.VMEM((LZ, NY, NX), F32),
            pltpu.VMEM((8, 4 * NY, 128), F32),
            pltpu.VMEM((8, 2 * NY, 128), F32),
            pltpu.VMEM((CX + 16, CL), F32),
        ],
        compiler_params=params(16),
        cost_estimate=pl.CostEstimate(flops=60_000_000, bytes_accessed=20_000_000, transcendentals=0),
        name="interior",
    )(state, velocity, diffusivity, ct, after)


def finish_kernel(
    rnear, rtail, rfar, rfac, onear, otail, ofar, ofac, w0, w1, w2, w3, fin, edge, v, d, gcp, cb, ymid,
    ub, msg, gc, quad, u1, zs, jp,
):
    mine = quad_rank()
    for i, window in enumerate((w0, w1, w2, w3)):
        quad[mine ^ i] = window[...]
    for kind, (rec, own, recb, ownb, at) in enumerate(((rnear, onear, rtail, otail, 16), (rfar, ofar, rfac, ofac, 0))):
        top = edge_is_top(kind)
        side = jnp.where(top, 1, 0)
        for r in range(0, NY, 8):
            u1[kind, r : r + 8, :] = (
                own[NY + r : NY + r + 8, :] + ownb[at + r : at + r + 8, :] * rec[r : r + 8, :]
            )
        z = side * (LZ - 1)
        for r, rows, (c, w, e, s, n) in planes(u1, kind):
            outside = rec[NY + r : NY + r + 8, :] + recb[at + r : at + r + 8, :] * own[r : r + 8, :]
            inside = edge[side, rows, :]
            ax, ay, az, k = v[0, z, rows, :], v[1, z, rows, :], v[2, z, rows, :], d[z, rows, :]
            last = advanced(c, w, e, s, n, inside, outside, ax, ay, jnp.where(top, az, -az), k)
            near = fin[5 * side, rows, :] + edge[2 + side, rows, :] * c
            ub[3 * side, rows, :] = last
            ub[1 + side, rows, :] = near
            put_columns(zs.at[side], rows, last + near)
    lane = lax.broadcasted_iota(jnp.int32, (128, 128), 1)
    hnear = jnp.concatenate([rtail[0:16, 128 * i : 128 * i + 128] for i in range(8)], axis=0)
    hfar = jnp.concatenate([rfar[2 * NY : FAR, 128 * i : 128 * i + 128] for i in range(8)], axis=0)
    first_core = lax.axis_index("core") == 0
    halo_lo, halo_hi = jnp.where(first_core, hfar, hnear), jnp.where(first_core, hnear, hfar)
    for b in range(4):
        rows = slice(128 * b, 128 * b + 128)
        t = halved_x(
            jnp.concatenate(
                [
                    jnp.concatenate([paired(zs.at[0], i, 0, 32), ymid[i], paired(zs.at[1], i, 0, 32)], axis=0)
                    for i in (2 * b, 2 * b + 1)
                ],
                axis=1,
            )
        )
        hl = pltpu.roll(halo_lo, (128 - 32 * b) % 128, 1) if b else halo_lo
        hh = pltpu.roll(halo_hi, (96 - 32 * b) % 128, 1) if b != 3 else halo_hi
        halo = jnp.where(lane < 32, hl, hh)
        g = gcp[rows, :] + cb[rows, :] * halo
        g = jnp.where(lax.axis_index("tm") == 0, 0.0, g)
        gc[rows, :] = g
        jp[8 + 128 * b : 136 + 128 * b, :] = t - g
    jp[0:8, :] = jp[CX : CX + 8, :]
    jp[CX + 8 : CX + 24, :] = jp[8:24, :]
    for i in range(BLOCKS):
        msg[i] = jp[XB * i : XB * i + WIN, :]


def finish(messages, windows, fin, edge, velocity, diffusivity, gcp, cb, ymid):
    return pl.pallas_call(
        finish_kernel,
        out_shape=[
            jax.ShapeDtypeStruct((4, NY, NX), F32),
            jax.ShapeDtypeStruct((BLOCKS, WIN, CL), F32),
            jax.ShapeDtypeStruct((CX, CL), F32),
            jax.ShapeDtypeStruct((QUAD, 4, WIN, CL), F32),
        ],
        in_specs=[whole()] * 19,
        out_specs=[whole()] * 4,
        scratch_shapes=[
            pltpu.VMEM((2, NY, NX), F32),
            pltpu.VMEM((2, 8, NY, 128), F32),
            pltpu.VMEM((CX + 24, CL), F32),
        ],
        compiler_params=params(16),
        name="finish",
    )(*messages, *windows, fin, edge, velocity, diffusivity, gcp, cb, ymid)


HALO = 13
SHARED = ((0, 6, 96), (1, 5, 64), (2, 4, 32))


def pick_kernel(got, quad, even, odd):
    lane = lax.broadcasted_iota(jnp.int32, (WIN, CL), 1)
    for parity, out in enumerate((even, odd)):
        up = lax.rem(lax.axis_index("px"), 2) == parity
        near, far = jnp.where(up, 3, 0), jnp.where(up, 2, 1)

        def shared(main, other, width):
            return jnp.where(
                up,
                jnp.where(lane >= CL - width, main, pltpu.roll(other, CL - width, 1)),
                jnp.where(lane < width, main, pltpu.roll(other, width, 1)),
            )

        for j in range(4):
            out[j] = got[QUAD * j + near]
            out[7 + j] = quad[near, j]
        for j, other, width in SHARED:
            out[4 + j] = shared(got[QUAD * j + far], got[QUAD * other + near], width)
        for j in range(2):
            out[11 + j] = shared(quad[far, 2 * j], quad[far, 2 * j + 1], 64)


def pick(got, quad):
    halo = jax.ShapeDtypeStruct((HALO, WIN, CL), F32)
    return pl.pallas_call(
        pick_kernel,
        out_shape=[halo, halo],
        in_specs=[whole()] * 2,
        out_specs=[whole(), whole()],
        compiler_params=params(16),
        name="pick",
    )(got, quad)


def chain_kernel(got, quad, even, odd, out, cf, e):
    first = lax.rem(lax.axis_index("px"), 2) == 0

    def below(i):
        return jnp.where(first, odd[i], even[i])

    def above(i):
        return jnp.where(first, even[i], odd[i])

    def source(j, block):
        if 2 <= block < 6:
            return got[QUAD * j + block - 2]
        halo = below if block < 2 else above
        if block in (0, 7):
            return halo(4 + j) if j < 3 else None
        if j < 4:
            return halo(j)
        _, other, width = SHARED[6 - j]
        return pltpu.roll(halo(10 - j), width if block == 1 else CL - width, 1)

    for block in range(8):
        halo = below if block < 2 else above
        if 2 <= block < 6:
            values = [quad[block - 2, i] for i in range(4)]
        elif block in (1, 6):
            values = [halo(7 + i) for i in range(4)]
        else:
            values = []
            for i in (11, 12):
                values += [halo(i), pltpu.roll(halo(i), 64, 1)]
        for i, value in enumerate(coarse_coefs(*values)):
            cf[i, block] = value
        e[0, block] = source(0, block)
    for q in range(QUAD):
        out[q] = jnp.zeros((XB, CL), F32)
    lane = lax.broadcasted_iota(jnp.int32, (WIN, CL), 1)
    for k in range(1, GROUPS):
        now, later = (k - 1) % 2, k % 2
        low = 0 if k < 3 else 1 if k < 7 else 2
        reach = range(max(0, low - 1), min(8, 9 - low))
        near = {b: lane_neighbours(e[now, b]) for b in reach}
        for block in range(low, 8 - low):
            c = e[now, block]
            b, t, s, n = near[block]
            if block > 0:
                b = jnp.where(lane < 32, near[block - 1][0], b)
            if block < 7:
                t = jnp.where(lane >= 96, near[block + 1][1], t)
            w, x = pltpu.roll(c, 1, 0), pltpu.roll(c, WIN - 1, 0)
            y = c + (
                (cf[0, block] * (w - c) + cf[1, block] * (x - c))
                + (cf[2, block] * (s - c) + cf[3, block] * (n - c))
                + (cf[4, block] * (b - c) + cf[5, block] * (t - c))
            )
            if 2 <= block < 6:
                out[QUAD * k + block - 2] = y[8 : 8 + XB, :]
            if k < GROUPS - 1:
                more = source(k, block)
                e[later, block] = y if more is None else y + more


def chain(got, quad, even, odd):
    return pl.pallas_call(
        chain_kernel,
        out_shape=jax.ShapeDtypeStruct((BLOCKS, XB, CL), F32),
        in_specs=[whole()] * 4,
        out_specs=whole(),
        scratch_shapes=[
            pltpu.VMEM((6, 8, WIN, CL), F32),
            pltpu.VMEM((2, 8, WIN, CL), F32),
        ],
        compiler_params=params(24),
        name="chain",
    )(got, quad, even, odd)


def result_kernel(y, gc, fin, ub, out, copied, buf, sems):
    copy_y = table((256, CL), lambda r, c: r // 2 == c)
    copy_x = table((128, 256), lambda r, c: r == c // 2)
    for b in range(4):
        rows = slice(128 * b, 128 * b + 128)
        for i, part in enumerate(split3(y[rows, :] - gc[rows, :])):
            copied[i, :, rows] = dot(copy_y, part, 1, 1).astype(BF16)
    copies = []
    for zc in range(4):
        rows = slice(zc * NY, zc * NY + NY)
        for b in range(4):
            cols = slice(256 * b, 256 * b + 256)
            fine = sum(dot(copied[i, rows, 128 * b : 128 * b + 128], copy_x, 1, 0) for i in range(3))
            for z in (2 * zc, 2 * zc + 1):
                base = fin[z - 1, :, cols] if 2 <= z < 6 else ub[z if z < 2 else z - 4, :, cols]
                buf[z, :, cols] = base + fine
        layers = slice(2 * zc, 2 * zc + 2)
        copies.append(pltpu.make_async_copy(buf.at[layers], out.at[layers], sems.at[zc]))
        copies[zc].start()
    for copy in copies:
        copy.wait()


def result(y, gc, fin, ub):
    return pl.pallas_call(
        result_kernel,
        out_shape=jax.ShapeDtypeStruct((LZ, NY, NX), F32),
        in_specs=[whole()] * 4,
        out_specs=remains(),
        scratch_shapes=[
            pltpu.VMEM((3, 4 * NY, CX), BF16),
            pltpu.VMEM((LZ, NY, NX), F32),
            pltpu.SemaphoreType.DMA((4,)),
        ],
        compiler_params=params(16),
        name="result",
    )(y, gc, fin, ub)


def swap(value, axes, partner):
    pairs = [(i, partner(i)) for i in range(lax.axis_size(axes))]
    return lax.ppermute(value, axes, [(i, j) for i, j in pairs if j is not None])


def off_chip(i):
    j = i + 1 if i % 2 else i - 1
    return j if 0 <= j < 16 else None


def off_chip_copy(i):
    j = off_chip(i % 16)
    return None if j is None else (i // 16 ^ 1) * 16 + j


def quad_beside(i):
    j = i + 1 if i % 2 else i - 1
    return j if 0 <= j < 4 else None


def shards(state_old, velocity, diffusivity):
    state = state_old[0]
    ofar, ofac = edge_message(1, state, velocity, diffusivity)
    rfar = swap(ofar, SPACE, off_chip)
    rfac = swap(ofac, ("tm",) + SPACE, off_chip_copy)
    onear, otail = edge_message(0, state, velocity, diffusivity, ofac)
    rnear = swap(onear, SPACE, lambda i: i ^ 1)
    rtail = swap(otail, SPACE, lambda i: i ^ 1)
    ct, w0, w1, w2, w3 = coefs(velocity, diffusivity, rtail)
    windows = (
        w0,
        swap(w1, SPACE, lambda i: i ^ 1),
        swap(w2, ("tm",) + SPACE, lambda i: i ^ 18),
        swap(w3, ("tm",) + SPACE, lambda i: i ^ 19),
    )
    fin, edge, gcp, cb, ymid = interior(state, velocity, diffusivity, ct, windows[1])
    messages = (rnear, rtail, rfar, rfac, onear, otail, ofar, ofac)
    ub, msg, gc, quad = finish(messages, windows, fin, edge, velocity, diffusivity, gcp, cb, ymid)
    got = lax.all_to_all(msg, GROUP, 0, 0)
    even, odd = pick(got, quad)
    even = swap(even, "px", lambda i: i ^ 1)
    odd = swap(odd, "px", quad_beside)
    back = lax.all_to_all(chain(got, quad, even, odd), GROUP, 0, 0)
    return result(back.reshape(CX, CL), gc, fin, ub)[None]


def solution(mesh):
    fine_mesh = Mesh(mesh.devices.reshape(GROUPS, 4, 2, 2), ("tm",) + SPACE)
    return jax.shard_map(
        shards,
        mesh=fine_mesh,
        in_specs=(
            P("tm", SPACE, None, None),
            P(None, SPACE, None, None),
            P(SPACE, None, None),
        ),
        out_specs=P("tm", SPACE, None, None),
        check_vma=False,
    )
```

```python
import functools

import jax
import jax.numpy as jnp
from jax import lax
from jax.experimental import pallas as pl
from jax.experimental.pallas import tpu as pltpu
from jax.sharding import Mesh
from jax.sharding import PartitionSpec as P

F32 = jnp.float32
BF16 = jnp.bfloat16
NY, NX = 64, 1024
LZ = 8
CX, CL = 512, 128
GROUPS = 8
QUAD = 4
BLOCKS = GROUPS * QUAD
XB = CX // BLOCKS
WIN = XB + 16
SPACE = ("px", "pz", "core")
GROUP = ("tm", "pz", "core")


def params(mib):
    return pltpu.CompilerParams(vmem_limit_bytes=mib * 1024 * 1024)


def split3(x):
    hi = x.astype(BF16)
    rest = x - hi.astype(F32)
    mid = rest.astype(BF16)
    return hi, mid, (rest - mid.astype(F32)).astype(BF16)


def dot(a, b, ca, cb):
    return lax.dot_general(a, b, (((ca,), (cb,)), ((), ())), preferred_element_type=F32)


def table(shape, test):
    rows = lax.broadcasted_iota(jnp.int32, shape, 0)
    cols = lax.broadcasted_iota(jnp.int32, shape, 1)
    return test(rows, cols).astype(F32).astype(BF16)


def halved_x(part):
    halve = table((128, 256), lambda r, c: r == c // 2)
    return sum(dot(halve, p, 1, 1) for p in split3(part)) * 0.125


def put_columns(ref, at, value):
    for i in range(NX // 128):
        ref[i, at, :] = value[:, 128 * i : 128 * i + 128]


def paired(ref, column, first, rows):
    return ref[column, pl.ds(first, rows, 2), :] + ref[column, pl.ds(first + 1, rows, 2), :]


def advanced(c, w, e, s, n, b, t, ax, ay, az, k):
    lap = ((w + e) + (s + n)) + ((b + t) - 6.0 * c)
    dx = jnp.abs(ax) * (jnp.where(ax > 0, w, e) - c)
    dy = jnp.abs(ay) * (jnp.where(ay > 0, s, n) - c)
    dz = jnp.abs(az) * (jnp.where(az > 0, b, t) - c)
    return (c + k * lap) + ((dx + dy) + dz)


def planes(ref, z):
    row = lax.broadcasted_iota(jnp.int32, (8, NX), 0)
    c = ref[z, 0:8, :]
    before = pltpu.roll(ref[z, NY - 8 : NY, :], 1, 0)
    for r in range(0, NY, 8):
        after = ref[z, (r + 8) % NY : (r + 8) % NY + 8, :]
        down = pltpu.roll(c, 1, 0)
        s = jnp.where(row == 0, before, down)
        n = jnp.where(row == 7, pltpu.roll(after, 7, 0), pltpu.roll(c, 7, 0))
        yield r, slice(r, r + 8), (c, pltpu.roll(c, 1, 1), pltpu.roll(c, NX - 1, 1), s, n)
        c, before = after, down


def coarse_coefs(vx, vy, vz, k):
    half = 0.5 * k
    out = []
    for a in (vx, vy, vz):
        out += [half + jnp.maximum(a, 0.0), half - jnp.minimum(a, 0.0)]
    return out


def lane_neighbours(c):
    y = lax.rem(lax.broadcasted_iota(jnp.int32, c.shape, 1), 32)
    below, above = pltpu.roll(c, 32, 1), pltpu.roll(c, CL - 32, 1)
    s = jnp.where(y == 0, pltpu.roll(c, CL - 31, 1), pltpu.roll(c, 1, 1))
    n = jnp.where(y == 31, pltpu.roll(c, 31, 1), pltpu.roll(c, CL - 1, 1))
    return below, above, s, n


FAR = 2 * NY + 16
TAIL = 16 + NY
CROWS = CX + 32


def edge_is_top(kind):
    return lax.axis_index("core") == kind


def edge_kernel(kind, st, vel, dif, *rest):
    if kind == 0:
        _, out, tail, u, v, d, zs, sems = rest
        coarse_out, coarse_at, factor, factor_at = tail, 0, tail, 16
    else:
        out, factor, u, v, d, zs, sems = rest
        coarse_out, coarse_at, factor_at = out, 2 * NY, 0
    top = edge_is_top(kind)
    z, beside = jnp.where(top, LZ - 1, 0), jnp.where(top, LZ - 2, 1)
    pairs = ((st.at[z], u.at[0]), (vel.at[:, z], v), (dif.at[z], d), (st.at[beside], u.at[1]))
    copies = [pltpu.make_async_copy(a, b, sems.at[i]) for i, (a, b) in enumerate(pairs)]
    for copy in copies:
        copy.start()
    for copy in copies:
        copy.wait()
    for r, rows, (c, w, e, s, n) in planes(u, 0):
        inside = u[1, rows, :]
        ax, ay, k = v[0, rows, :], v[1, rows, :], d[rows, :]
        up = jnp.where(top, v[2, rows, :], -v[2, rows, :])
        out[r : r + 8, :] = c
        out[NY + r : NY + r + 8, :] = advanced(c, w, e, s, n, inside, jnp.zeros_like(c), ax, ay, up, k)
        factor[factor_at + r : factor_at + r + 8, :] = k - jnp.minimum(up, 0.0)
        put_columns(zs, rows, c + inside)
    coarse = jnp.zeros((128, 128), F32)
    for b in range(4):
        part = jnp.concatenate([paired(zs, 2 * b + i, 0, 32) for i in range(2)], axis=1)
        t = halved_x(jnp.concatenate([part, jnp.zeros((96, 256), F32)], axis=0))
        coarse += pltpu.roll(t, 32 * b, 1) if b else t
    for i in range(8):
        coarse_out[coarse_at : coarse_at + 16, 128 * i : 128 * i + 128] = coarse[16 * i : 16 * i + 16, :]


def whole():
    return pl.BlockSpec(memory_space=pltpu.VMEM)


def remains():
    return pl.BlockSpec(memory_space=pltpu.HBM)


def edge_message(kind, state, velocity, diffusivity, *after):
    shapes = [((2 * NY, NX), (TAIL, NX)), ((FAR, NX), (NY, NX))][kind]
    return pl.pallas_call(
        functools.partial(edge_kernel, kind),
        out_shape=[jax.ShapeDtypeStruct(shape, F32) for shape in shapes],
        in_specs=[remains()] * 3 + [whole()] * len(after),
        out_specs=[whole()] * len(shapes),
        scratch_shapes=[
            pltpu.VMEM((2, NY, NX), F32),
            pltpu.VMEM((3, NY, NX), F32),
            pltpu.VMEM((NY, NX), F32),
            pltpu.VMEM((8, NY, 128), F32),
            pltpu.SemaphoreType.DMA((4,)),
        ],
        compiler_params=params([8, 52][kind]),
        cost_estimate=pl.CostEstimate(flops=15_000_000, bytes_accessed=[12_000_000, 3_000_000][kind], transcendentals=0),
        name=["near_message", "far_message"][kind],
    )(state, velocity, diffusivity, *after)


def quad_rank():
    return lax.axis_index("pz") * 2 + lax.axis_index("core")


def coefs_kernel(vel, dif, after, ct, w0, w1, w2, w3, zs):
    for comp in range(4):
        for zc in range(4):
            for r in range(0, NY, 8):
                rows = slice(r, r + 8)
                two = [dif[z, rows, :] if comp == 3 else vel[comp, z, rows, :] for z in (2 * zc, 2 * zc + 1)]
                put_columns(zs.at[comp], slice(zc * NY + r, zc * NY + r + 8), two[0] + two[1])
        for b in range(4):
            ct[comp, 8 + 128 * b : 136 + 128 * b, :] = halved_x(
                jnp.concatenate([paired(zs.at[comp], 2 * b + i, 0, 128) for i in range(2)], axis=1)
            )
        ct[comp, 0:8, :] = ct[comp, CX : CX + 8, :]
        ct[comp, CX + 8 : CX + 32, :] = ct[comp, 8:32, :]
    mine = quad_rank()
    slice_index = lax.axis_index("tm")
    for i, out in enumerate((w0, w1, w2, w3)):
        block = (slice_index if i < 2 else slice_index ^ 1) * QUAD + (mine ^ i)
        for comp in range(4):
            out[comp] = ct[comp, pl.ds(pl.multiple_of(block * XB, XB), WIN), :]


def coefs(velocity, diffusivity, after):
    window = jax.ShapeDtypeStruct((4, WIN, CL), F32)
    return pl.pallas_call(
        coefs_kernel,
        out_shape=[jax.ShapeDtypeStruct((4, CROWS, CL), F32)] + [window] * 4,
        in_specs=[whole()] * 3,
        out_specs=[whole()] * 5,
        scratch_shapes=[pltpu.VMEM((4, 8, 4 * NY, 128), F32)],
        compiler_params=params(12),
        cost_estimate=pl.CostEstimate(flops=20_000_000, bytes_accessed=9_000_000, transcendentals=0),
        name="coefs",
    )(velocity, diffusivity, after)


def interior_kernel(u, v, d, ct, after, fin, edge, gcp, cb, ymid, u1, zs, zf, ct0):
    def first(z, _):
        for _, rows, (c, w, e, s, n) in planes(u, z):
            u1[z, rows, :] = advanced(
                c, w, e, s, n, u[z - 1, rows, :], u[z + 1, rows, :],
                v[0, z, rows, :], v[1, z, rows, :], v[2, z, rows, :], d[z, rows, :],
            )
        return 0

    lax.fori_loop(1, LZ - 1, first, 0)
    u1[0] = jnp.zeros((NY, NX), F32)
    u1[LZ - 1] = jnp.zeros((NY, NX), F32)
    edge[0] = u1[1]
    edge[1] = u1[LZ - 2]

    def second(z, _):
        for _, rows, (c, w, e, s, n) in planes(u1, z):
            fin[z - 1, rows, :] = advanced(
                c, w, e, s, n, u1[z - 1, rows, :], u1[z + 1, rows, :],
                v[0, z, rows, :], v[1, z, rows, :], v[2, z, rows, :], d[z, rows, :],
            )
        return 0

    lax.fori_loop(1, LZ - 1, second, 0)
    edge[2] = d[1] + jnp.maximum(v[2, 1], 0.0)
    edge[3] = d[LZ - 2] - jnp.minimum(v[2, LZ - 2], 0.0)
    for zc in (1, 2):
        for r in range(0, NY, 8):
            rows = slice(r, r + 8)
            put_columns(zf, slice((zc - 1) * NY + r, (zc - 1) * NY + r + 8), fin[2 * zc - 1, rows, :] + fin[2 * zc, rows, :])
    for i in range(8):
        ymid[i] = paired(zf, i, 0, 64)

    for zc in range(4):
        for r in range(0, NY, 8):
            rows = slice(r, r + 8)
            put_columns(zs, slice(zc * NY + r, zc * NY + r + 8), u[2 * zc, rows, :] + u[2 * zc + 1, rows, :])
    for b in range(4):
        ct0[8 + 128 * b : 136 + 128 * b, :] = halved_x(
            jnp.concatenate([paired(zs, 2 * b + i, 0, 128) for i in range(2)], axis=1)
        )
    ct0[0:8, :] = ct0[CX : CX + 8, :]
    ct0[CX + 8 : CX + 16, :] = ct0[8:16, :]
    lane = lax.broadcasted_iota(jnp.int32, (64, CL), 1)
    for r in range(0, CX, 64):
        c = ct0[8 + r : 72 + r, :]
        xl, xh, yl, yh, zl, zh = coarse_coefs(*(ct[i, 8 + r : 72 + r, :] for i in range(4)))
        b, t, s, n = lane_neighbours(c)
        b = jnp.where(lane < 32, 0.0, b)
        t = jnp.where(lane >= 96, 0.0, t)
        w = ct0[7 + r : 71 + r, :]
        e = ct0[9 + r : 73 + r, :]
        gcp[r : r + 64, :] = c + (
            (xl * (w - c) + xh * (e - c)) + (yl * (s - c) + yh * (n - c)) + (zl * (b - c) + zh * (t - c))
        )
        cb[r : r + 64, :] = jnp.where(lane < 32, zl, jnp.where(lane >= 96, zh, 0.0))


def interior(state, velocity, diffusivity, ct, after):
    small = jax.ShapeDtypeStruct((CX, CL), F32)
    return pl.pallas_call(
        interior_kernel,
        out_shape=[
            jax.ShapeDtypeStruct((LZ - 2, NY, NX), F32),
            jax.ShapeDtypeStruct((4, NY, NX), F32),
            small,
            small,
            jax.ShapeDtypeStruct((8, 64, 128), F32),
        ],
        in_specs=[whole()] * 5,
        out_specs=[whole()] * 5,
        scratch_shapes=[
            pltpu.VMEM((LZ, NY, NX), F32),
            pltpu.VMEM((8, 4 * NY, 128), F32),
            pltpu.VMEM((8, 2 * NY, 128), F32),
            pltpu.VMEM((CX + 16, CL), F32),
        ],
        compiler_params=params(16),
        cost_estimate=pl.CostEstimate(flops=60_000_000, bytes_accessed=20_000_000, transcendentals=0),
        name="interior",
    )(state, velocity, diffusivity, ct, after)


def at_end():
    slab = lax.axis_index("px") * QUAD + quad_rank()
    return (slab == 0) | (slab == 15)


def dropped(beyond, value):
    return value if beyond is False else jnp.where(beyond, 0.0, value)


def finish_kernel(
    rnear, rtail, rfar, rfac, onear, otail, ofar, ofac, w0, w1, w2, w3, fin, edge, v, d, gcp, cb, ymid,
    ub, msg, gc, quad, u1, zs, jp,
):
    mine = quad_rank()
    for i, window in enumerate((w0, w1, w2, w3)):
        quad[mine ^ i] = window[...]
    for kind, (rec, own, recb, ownb, at) in enumerate(((rnear, onear, rtail, otail, 16), (rfar, ofar, rfac, ofac, 0))):
        top = edge_is_top(kind)
        side = jnp.where(top, 1, 0)
        beyond = kind == 1 and at_end()
        for r in range(0, NY, 8):
            u1[kind, r : r + 8, :] = (
                own[NY + r : NY + r + 8, :] + ownb[at + r : at + r + 8, :] * dropped(beyond, rec[r : r + 8, :])
            )
        z = side * (LZ - 1)
        for r, rows, (c, w, e, s, n) in planes(u1, kind):
            outside = rec[NY + r : NY + r + 8, :] + recb[at + r : at + r + 8, :] * own[r : r + 8, :]
            outside = dropped(beyond, outside)
            inside = edge[side, rows, :]
            ax, ay, az, k = v[0, z, rows, :], v[1, z, rows, :], v[2, z, rows, :], d[z, rows, :]
            last = advanced(c, w, e, s, n, inside, outside, ax, ay, jnp.where(top, az, -az), k)
            near = fin[5 * side, rows, :] + edge[2 + side, rows, :] * c
            ub[3 * side, rows, :] = last
            ub[1 + side, rows, :] = near
            put_columns(zs.at[side], rows, last + near)
    lane = lax.broadcasted_iota(jnp.int32, (128, 128), 1)
    hnear = jnp.concatenate([rtail[0:16, 128 * i : 128 * i + 128] for i in range(8)], axis=0)
    hfar = jnp.concatenate([rfar[2 * NY : FAR, 128 * i : 128 * i + 128] for i in range(8)], axis=0)
    hfar = dropped(at_end(), hfar)
    first_core = lax.axis_index("core") == 0
    halo_lo, halo_hi = jnp.where(first_core, hfar, hnear), jnp.where(first_core, hnear, hfar)
    for b in range(4):
        rows = slice(128 * b, 128 * b + 128)
        t = halved_x(
            jnp.concatenate(
                [
                    jnp.concatenate([paired(zs.at[0], i, 0, 32), ymid[i], paired(zs.at[1], i, 0, 32)], axis=0)
                    for i in (2 * b, 2 * b + 1)
                ],
                axis=1,
            )
        )
        hl = pltpu.roll(halo_lo, (128 - 32 * b) % 128, 1) if b else halo_lo
        hh = pltpu.roll(halo_hi, (96 - 32 * b) % 128, 1) if b != 3 else halo_hi
        halo = jnp.where(lane < 32, hl, hh)
        g = gcp[rows, :] + cb[rows, :] * halo
        g = jnp.where(lax.axis_index("tm") == 0, 0.0, g)
        gc[rows, :] = g
        jp[8 + 128 * b : 136 + 128 * b, :] = t - g
    jp[0:8, :] = jp[CX : CX + 8, :]
    jp[CX + 8 : CX + 24, :] = jp[8:24, :]
    for i in range(BLOCKS):
        msg[i] = jp[XB * i : XB * i + WIN, :]


def finish(messages, windows, fin, edge, velocity, diffusivity, gcp, cb, ymid):
    return pl.pallas_call(
        finish_kernel,
        out_shape=[
            jax.ShapeDtypeStruct((4, NY, NX), F32),
            jax.ShapeDtypeStruct((BLOCKS, WIN, CL), F32),
            jax.ShapeDtypeStruct((CX, CL), F32),
            jax.ShapeDtypeStruct((QUAD, 4, WIN, CL), F32),
        ],
        in_specs=[whole()] * 19,
        out_specs=[whole()] * 4,
        scratch_shapes=[
            pltpu.VMEM((2, NY, NX), F32),
            pltpu.VMEM((2, 8, NY, 128), F32),
            pltpu.VMEM((CX + 24, CL), F32),
        ],
        compiler_params=params(16),
        name="finish",
    )(*messages, *windows, fin, edge, velocity, diffusivity, gcp, cb, ymid)


HALO = 13
SHARED = ((0, 6, 96), (1, 5, 64), (2, 4, 32))


def pick_kernel(got, quad, even, odd):
    lane = lax.broadcasted_iota(jnp.int32, (WIN, CL), 1)
    for parity, out in enumerate((even, odd)):
        up = lax.rem(lax.axis_index("px"), 2) == parity
        near, far = jnp.where(up, 3, 0), jnp.where(up, 2, 1)

        def shared(main, other, width):
            return jnp.where(
                up,
                jnp.where(lane >= CL - width, main, pltpu.roll(other, CL - width, 1)),
                jnp.where(lane < width, main, pltpu.roll(other, width, 1)),
            )

        for j in range(4):
            out[j] = got[QUAD * j + near]
            out[7 + j] = quad[near, j]
        for j, other, width in SHARED:
            out[4 + j] = shared(got[QUAD * j + far], got[QUAD * other + near], width)
        for j in range(2):
            out[11 + j] = shared(quad[far, 2 * j], quad[far, 2 * j + 1], 64)


def pick(got, quad):
    halo = jax.ShapeDtypeStruct((HALO, WIN, CL), F32)
    return pl.pallas_call(
        pick_kernel,
        out_shape=[halo, halo],
        in_specs=[whole()] * 2,
        out_specs=[whole(), whole()],
        compiler_params=params(16),
        name="pick",
    )(got, quad)


def chain_kernel(got, quad, even, odd, out, cf, e):
    place = lax.axis_index("px")
    first = lax.rem(place, 2) == 0

    def below(i):
        return jnp.where(place == 0, 0.0, jnp.where(first, odd[i], even[i]))

    def above(i):
        return jnp.where(place == 3, 0.0, jnp.where(first, even[i], odd[i]))

    def source(j, block):
        if 2 <= block < 6:
            return got[QUAD * j + block - 2]
        halo = below if block < 2 else above
        if block in (0, 7):
            return halo(4 + j) if j < 3 else None
        if j < 4:
            return halo(j)
        _, other, width = SHARED[6 - j]
        return pltpu.roll(halo(10 - j), width if block == 1 else CL - width, 1)

    for block in range(8):
        halo = below if block < 2 else above
        if 2 <= block < 6:
            values = [quad[block - 2, i] for i in range(4)]
        elif block in (1, 6):
            values = [halo(7 + i) for i in range(4)]
        else:
            values = []
            for i in (11, 12):
                values += [halo(i), pltpu.roll(halo(i), 64, 1)]
        for i, value in enumerate(coarse_coefs(*values)):
            cf[i, block] = value
        e[0, block] = source(0, block)
    for q in range(QUAD):
        out[q] = jnp.zeros((XB, CL), F32)
    lane = lax.broadcasted_iota(jnp.int32, (WIN, CL), 1)
    for k in range(1, GROUPS):
        now, later = (k - 1) % 2, k % 2
        low = 0 if k < 3 else 1 if k < 7 else 2
        reach = range(max(0, low - 1), min(8, 9 - low))
        near = {b: lane_neighbours(e[now, b]) for b in reach}
        for block in range(low, 8 - low):
            c = e[now, block]
            b, t, s, n = near[block]
            if block > 0:
                b = jnp.where(lane < 32, near[block - 1][0], b)
            if block < 7:
                t = jnp.where(lane >= 96, near[block + 1][1], t)
            w, x = pltpu.roll(c, 1, 0), pltpu.roll(c, WIN - 1, 0)
            y = c + (
                (cf[0, block] * (w - c) + cf[1, block] * (x - c))
                + (cf[2, block] * (s - c) + cf[3, block] * (n - c))
                + (cf[4, block] * (b - c) + cf[5, block] * (t - c))
            )
            if 2 <= block < 6:
                out[QUAD * k + block - 2] = y[8 : 8 + XB, :]
            if k < GROUPS - 1:
                more = source(k, block)
                e[later, block] = y if more is None else y + more


def chain(got, quad, even, odd):
    return pl.pallas_call(
        chain_kernel,
        out_shape=jax.ShapeDtypeStruct((BLOCKS, XB, CL), F32),
        in_specs=[whole()] * 4,
        out_specs=whole(),
        scratch_shapes=[
            pltpu.VMEM((6, 8, WIN, CL), F32),
            pltpu.VMEM((2, 8, WIN, CL), F32),
        ],
        compiler_params=params(24),
        name="chain",
    )(got, quad, even, odd)


def result_kernel(y, gc, fin, ub, out, copied, buf, sems):
    copy_y = table((256, CL), lambda r, c: r // 2 == c)
    copy_x = table((128, 256), lambda r, c: r == c // 2)
    for b in range(4):
        rows = slice(128 * b, 128 * b + 128)
        for i, part in enumerate(split3(y[rows, :] - gc[rows, :])):
            copied[i, :, rows] = dot(copy_y, part, 1, 1).astype(BF16)
    copies = []
    for zc in range(4):
        rows = slice(zc * NY, zc * NY + NY)
        for b in range(4):
            cols = slice(256 * b, 256 * b + 256)
            fine = sum(dot(copied[i, rows, 128 * b : 128 * b + 128], copy_x, 1, 0) for i in range(3))
            for z in (2 * zc, 2 * zc + 1):
                base = fin[z - 1, :, cols] if 2 <= z < 6 else ub[z if z < 2 else z - 4, :, cols]
                buf[z, :, cols] = base + fine
        layers = slice(2 * zc, 2 * zc + 2)
        copies.append(pltpu.make_async_copy(buf.at[layers], out.at[layers], sems.at[zc]))
        copies[zc].start()
    for copy in copies:
        copy.wait()


def result(y, gc, fin, ub):
    return pl.pallas_call(
        result_kernel,
        out_shape=jax.ShapeDtypeStruct((LZ, NY, NX), F32),
        in_specs=[whole()] * 4,
        out_specs=remains(),
        scratch_shapes=[
            pltpu.VMEM((3, 4 * NY, CX), BF16),
            pltpu.VMEM((LZ, NY, NX), F32),
            pltpu.SemaphoreType.DMA((4,)),
        ],
        compiler_params=params(16),
        name="result",
    )(y, gc, fin, ub)


def swap(value, axes, partner):
    return lax.ppermute(value, axes, [(i, partner(i)) for i in range(lax.axis_size(axes))])


def off_chip(i):
    return (i + 1 if i % 2 else i - 1) % 16


def off_chip_copy(i):
    return (i // 16 ^ 1) * 16 + off_chip(i % 16)


def quad_beside(i):
    return (i + 1 if i % 2 else i - 1) % 4


def shards(state_old, velocity, diffusivity):
    state = state_old[0]
    ofar, ofac = edge_message(1, state, velocity, diffusivity)
    rfar = swap(ofar, SPACE, off_chip)
    rfac = swap(ofac, ("tm",) + SPACE, off_chip_copy)
    onear, otail = edge_message(0, state, velocity, diffusivity, ofac)
    rnear = swap(onear, SPACE, lambda i: i ^ 1)
    rtail = swap(otail, SPACE, lambda i: i ^ 1)
    ct, w0, w1, w2, w3 = coefs(velocity, diffusivity, rtail)
    windows = (
        w0,
        swap(w1, SPACE, lambda i: i ^ 1),
        swap(w2, ("tm",) + SPACE, lambda i: i ^ 18),
        swap(w3, ("tm",) + SPACE, lambda i: i ^ 19),
    )
    fin, edge, gcp, cb, ymid = interior(state, velocity, diffusivity, ct, windows[1])
    messages = (rnear, rtail, rfar, rfac, onear, otail, ofar, ofac)
    ub, msg, gc, quad = finish(messages, windows, fin, edge, velocity, diffusivity, gcp, cb, ymid)
    got = lax.all_to_all(msg, GROUP, 0, 0)
    even, odd = pick(got, quad)
    even = swap(even, "px", lambda i: i ^ 1)
    odd = swap(odd, "px", quad_beside)
    back = lax.all_to_all(chain(got, quad, even, odd), GROUP, 0, 0)
    return result(back.reshape(CX, CL), gc, fin, ub)[None]


def solution(mesh):
    fine_mesh = Mesh(mesh.devices.reshape(GROUPS, 4, 2, 2), ("tm",) + SPACE)
    return jax.shard_map(
        shards,
        mesh=fine_mesh,
        in_specs=(
            P("tm", SPACE, None, None),
            P(None, SPACE, None, None),
            P(SPACE, None, None),
        ),
        out_specs=P("tm", SPACE, None, None),
        check_vma=False,
    )
```

```python
import functools

import jax
import jax.numpy as jnp
from jax import lax
from jax.experimental import pallas as pl
from jax.experimental.pallas import tpu as pltpu
from jax.sharding import Mesh
from jax.sharding import PartitionSpec as P

F32 = jnp.float32
BF16 = jnp.bfloat16
NY, NX = 64, 1024
LZ = 8
CX, CL = 512, 128
GROUPS = 8
QUAD = 4
BLOCKS = GROUPS * QUAD
XB = CX // BLOCKS
WIN = XB + 16
SPACE = ("px", "pz", "core")
GROUP = ("tm", "pz", "core")


def params(mib):
    return pltpu.CompilerParams(vmem_limit_bytes=mib * 1024 * 1024)


def split3(x):
    hi = x.astype(BF16)
    rest = x - hi.astype(F32)
    mid = rest.astype(BF16)
    return hi, mid, (rest - mid.astype(F32)).astype(BF16)


def dot(a, b, ca, cb):
    return lax.dot_general(a, b, (((ca,), (cb,)), ((), ())), preferred_element_type=F32)


def table(shape, test):
    rows = lax.broadcasted_iota(jnp.int32, shape, 0)
    cols = lax.broadcasted_iota(jnp.int32, shape, 1)
    return test(rows, cols).astype(F32).astype(BF16)


def halved_x(part):
    halve = table((128, 256), lambda r, c: r == c // 2)
    return sum(dot(halve, p, 1, 1) for p in split3(part)) * 0.125


def put_columns(ref, at, value):
    for i in range(NX // 128):
        ref[i, at, :] = value[:, 128 * i : 128 * i + 128]


def paired(ref, column, first, rows):
    return ref[column, pl.ds(first, rows, 2), :] + ref[column, pl.ds(first + 1, rows, 2), :]


def advanced(c, w, e, s, n, b, t, ax, ay, az, k):
    lap = ((w + e) + (s + n)) + ((b + t) - 6.0 * c)
    dx = jnp.abs(ax) * (jnp.where(ax > 0, w, e) - c)
    dy = jnp.abs(ay) * (jnp.where(ay > 0, s, n) - c)
    dz = jnp.abs(az) * (jnp.where(az > 0, b, t) - c)
    return (c + k * lap) + ((dx + dy) + dz)


def planes(ref, z):
    row = lax.broadcasted_iota(jnp.int32, (8, NX), 0)
    c = ref[z, 0:8, :]
    before = pltpu.roll(ref[z, NY - 8 : NY, :], 1, 0)
    for r in range(0, NY, 8):
        after = ref[z, (r + 8) % NY : (r + 8) % NY + 8, :]
        down = pltpu.roll(c, 1, 0)
        s = jnp.where(row == 0, before, down)
        n = jnp.where(row == 7, pltpu.roll(after, 7, 0), pltpu.roll(c, 7, 0))
        yield r, slice(r, r + 8), (c, pltpu.roll(c, 1, 1), pltpu.roll(c, NX - 1, 1), s, n)
        c, before = after, down


def coarse_coefs(vx, vy, vz, k):
    half = 0.5 * k
    out = []
    for a in (vx, vy, vz):
        out += [half + jnp.maximum(a, 0.0), half - jnp.minimum(a, 0.0)]
    return out


def lane_neighbours(c):
    y = lax.rem(lax.broadcasted_iota(jnp.int32, c.shape, 1), 32)
    below, above = pltpu.roll(c, 32, 1), pltpu.roll(c, CL - 32, 1)
    s = jnp.where(y == 0, pltpu.roll(c, CL - 31, 1), pltpu.roll(c, 1, 1))
    n = jnp.where(y == 31, pltpu.roll(c, 31, 1), pltpu.roll(c, CL - 1, 1))
    return below, above, s, n


FAR = 2 * NY + 16
TAIL = 16 + NY
CROWS = CX + 32


def edge_is_top(kind):
    return lax.axis_index("core") == kind


def edge_kernel(kind, st, vel, dif, *rest):
    if kind == 0:
        _, out, tail, u, v, d, zs, sems = rest
        coarse_out, coarse_at, factor, factor_at = tail, 0, tail, 16
    else:
        out, factor, u, v, d, zs, sems = rest
        coarse_out, coarse_at, factor_at = out, 2 * NY, 0
    top = edge_is_top(kind)
    z, beside = jnp.where(top, LZ - 1, 0), jnp.where(top, LZ - 2, 1)
    pairs = ((st.at[z], u.at[0]), (vel.at[:, z], v), (dif.at[z], d), (st.at[beside], u.at[1]))
    copies = [pltpu.make_async_copy(a, b, sems.at[i]) for i, (a, b) in enumerate(pairs)]
    for copy in copies:
        copy.start()
    for copy in copies:
        copy.wait()
    for r, rows, (c, w, e, s, n) in planes(u, 0):
        inside = u[1, rows, :]
        ax, ay, k = v[0, rows, :], v[1, rows, :], d[rows, :]
        up = jnp.where(top, v[2, rows, :], -v[2, rows, :])
        out[r : r + 8, :] = c
        out[NY + r : NY + r + 8, :] = advanced(c, w, e, s, n, inside, jnp.zeros_like(c), ax, ay, up, k)
        factor[factor_at + r : factor_at + r + 8, :] = k - jnp.minimum(up, 0.0)
        put_columns(zs, rows, c + inside)
    coarse = jnp.zeros((128, 128), F32)
    for b in range(4):
        part = jnp.concatenate([paired(zs, 2 * b + i, 0, 32) for i in range(2)], axis=1)
        t = halved_x(jnp.concatenate([part, jnp.zeros((96, 256), F32)], axis=0))
        coarse += pltpu.roll(t, 32 * b, 1) if b else t
    for i in range(8):
        coarse_out[coarse_at : coarse_at + 16, 128 * i : 128 * i + 128] = coarse[16 * i : 16 * i + 16, :]


def whole():
    return pl.BlockSpec(memory_space=pltpu.VMEM)


def remains():
    return pl.BlockSpec(memory_space=pltpu.HBM)


def edge_message(kind, state, velocity, diffusivity, *after):
    shapes = [((2 * NY, NX), (TAIL, NX)), ((FAR, NX), (NY, NX))][kind]
    return pl.pallas_call(
        functools.partial(edge_kernel, kind),
        out_shape=[jax.ShapeDtypeStruct(shape, F32) for shape in shapes],
        in_specs=[remains()] * 3 + [whole()] * len(after),
        out_specs=[whole()] * len(shapes),
        scratch_shapes=[
            pltpu.VMEM((2, NY, NX), F32),
            pltpu.VMEM((3, NY, NX), F32),
            pltpu.VMEM((NY, NX), F32),
            pltpu.VMEM((8, NY, 128), F32),
            pltpu.SemaphoreType.DMA((4,)),
        ],
        compiler_params=params([8, 52][kind]),
        cost_estimate=pl.CostEstimate(flops=15_000_000, bytes_accessed=[12_000_000, 3_000_000][kind], transcendentals=0),
        name=["near_message", "far_message"][kind],
    )(state, velocity, diffusivity, *after)


def quad_rank():
    return lax.axis_index("pz") * 2 + lax.axis_index("core")


def coefs_kernel(vel, dif, after, ct, w0, w1, w2, w3, zs):
    for comp in range(4):
        for zc in range(4):
            for r in range(0, NY, 8):
                rows = slice(r, r + 8)
                two = [dif[z, rows, :] if comp == 3 else vel[comp, z, rows, :] for z in (2 * zc, 2 * zc + 1)]
                put_columns(zs.at[comp], slice(zc * NY + r, zc * NY + r + 8), two[0] + two[1])
        for b in range(4):
            ct[comp, 8 + 128 * b : 136 + 128 * b, :] = halved_x(
                jnp.concatenate([paired(zs.at[comp], 2 * b + i, 0, 128) for i in range(2)], axis=1)
            )
        ct[comp, 0:8, :] = ct[comp, CX : CX + 8, :]
        ct[comp, CX + 8 : CX + 32, :] = ct[comp, 8:32, :]
    mine = quad_rank()
    slice_index = lax.axis_index("tm")
    for i, out in enumerate((w0, w1, w2, w3)):
        block = (slice_index if i < 2 else slice_index ^ 1) * QUAD + (mine ^ i)
        for comp in range(4):
            out[comp] = ct[comp, pl.ds(pl.multiple_of(block * XB, XB), WIN), :]


def coefs(velocity, diffusivity, after):
    window = jax.ShapeDtypeStruct((4, WIN, CL), F32)
    return pl.pallas_call(
        coefs_kernel,
        out_shape=[jax.ShapeDtypeStruct((4, CROWS, CL), F32)] + [window] * 4,
        in_specs=[whole()] * 3,
        out_specs=[whole()] * 5,
        scratch_shapes=[pltpu.VMEM((4, 8, 4 * NY, 128), F32)],
        compiler_params=params(12),
        cost_estimate=pl.CostEstimate(flops=20_000_000, bytes_accessed=9_000_000, transcendentals=0),
        name="coefs",
    )(velocity, diffusivity, after)


def interior_kernel(u, v, d, ct, after, fin, edge, gcp, cb, ymid, u1, zs, zf, ct0):
    def first(z, _):
        for _, rows, (c, w, e, s, n) in planes(u, z):
            u1[z, rows, :] = advanced(
                c, w, e, s, n, u[z - 1, rows, :], u[z + 1, rows, :],
                v[0, z, rows, :], v[1, z, rows, :], v[2, z, rows, :], d[z, rows, :],
            )
        return 0

    lax.fori_loop(1, LZ - 1, first, 0)
    u1[0] = jnp.zeros((NY, NX), F32)
    u1[LZ - 1] = jnp.zeros((NY, NX), F32)
    edge[0] = u1[1]
    edge[1] = u1[LZ - 2]

    def second(z, _):
        for _, rows, (c, w, e, s, n) in planes(u1, z):
            fin[z - 1, rows, :] = advanced(
                c, w, e, s, n, u1[z - 1, rows, :], u1[z + 1, rows, :],
                v[0, z, rows, :], v[1, z, rows, :], v[2, z, rows, :], d[z, rows, :],
            )
        return 0

    lax.fori_loop(1, LZ - 1, second, 0)
    edge[2] = d[1] + jnp.maximum(v[2, 1], 0.0)
    edge[3] = d[LZ - 2] - jnp.minimum(v[2, LZ - 2], 0.0)
    for zc in (1, 2):
        for r in range(0, NY, 8):
            rows = slice(r, r + 8)
            put_columns(zf, slice((zc - 1) * NY + r, (zc - 1) * NY + r + 8), fin[2 * zc - 1, rows, :] + fin[2 * zc, rows, :])
    for i in range(8):
        ymid[i] = paired(zf, i, 0, 64)

    for zc in range(4):
        for r in range(0, NY, 8):
            rows = slice(r, r + 8)
            put_columns(zs, slice(zc * NY + r, zc * NY + r + 8), u[2 * zc, rows, :] + u[2 * zc + 1, rows, :])
    for b in range(4):
        ct0[8 + 128 * b : 136 + 128 * b, :] = halved_x(
            jnp.concatenate([paired(zs, 2 * b + i, 0, 128) for i in range(2)], axis=1)
        )
    ct0[0:8, :] = ct0[CX : CX + 8, :]
    ct0[CX + 8 : CX + 16, :] = ct0[8:16, :]
    lane = lax.broadcasted_iota(jnp.int32, (64, CL), 1)
    for r in range(0, CX, 64):
        c = ct0[8 + r : 72 + r, :]
        xl, xh, yl, yh, zl, zh = coarse_coefs(*(ct[i, 8 + r : 72 + r, :] for i in range(4)))
        b, t, s, n = lane_neighbours(c)
        b = jnp.where(lane < 32, 0.0, b)
        t = jnp.where(lane >= 96, 0.0, t)
        w = ct0[7 + r : 71 + r, :]
        e = ct0[9 + r : 73 + r, :]
        gcp[r : r + 64, :] = c + (
            (xl * (w - c) + xh * (e - c)) + (yl * (s - c) + yh * (n - c)) + (zl * (b - c) + zh * (t - c))
        )
        cb[r : r + 64, :] = jnp.where(lane < 32, zl, jnp.where(lane >= 96, zh, 0.0))


def interior(state, velocity, diffusivity, ct, after):
    small = jax.ShapeDtypeStruct((CX, CL), F32)
    return pl.pallas_call(
        interior_kernel,
        out_shape=[
            jax.ShapeDtypeStruct((LZ - 2, NY, NX), F32),
            jax.ShapeDtypeStruct((4, NY, NX), F32),
            small,
            small,
            jax.ShapeDtypeStruct((8, 64, 128), F32),
        ],
        in_specs=[whole()] * 5,
        out_specs=[whole()] * 5,
        scratch_shapes=[
            pltpu.VMEM((LZ, NY, NX), F32),
            pltpu.VMEM((8, 4 * NY, 128), F32),
            pltpu.VMEM((8, 2 * NY, 128), F32),
            pltpu.VMEM((CX + 16, CL), F32),
        ],
        compiler_params=params(16),
        cost_estimate=pl.CostEstimate(flops=60_000_000, bytes_accessed=20_000_000, transcendentals=0),
        name="interior",
    )(state, velocity, diffusivity, ct, after)


def at_end():
    slab = lax.axis_index("px") * QUAD + quad_rank()
    return (slab == 0) | (slab == 15)


def dropped(beyond, value):
    return value if beyond is False else jnp.where(beyond, 0.0, value)


def finish_kernel(
    rnear, rtail, rfar, rfac, onear, otail, ofar, ofac, fin, edge, v, d, gcp, cb, ymid,
    ub, jp, gc, u1, zs,
):
    for kind, (rec, own, recb, ownb, at) in enumerate(((rnear, onear, rtail, otail, 16), (rfar, ofar, rfac, ofac, 0))):
        top = edge_is_top(kind)
        side = jnp.where(top, 1, 0)
        beyond = kind == 1 and at_end()
        for r in range(0, NY, 8):
            u1[kind, r : r + 8, :] = (
                own[NY + r : NY + r + 8, :] + ownb[at + r : at + r + 8, :] * dropped(beyond, rec[r : r + 8, :])
            )
        z = side * (LZ - 1)
        for r, rows, (c, w, e, s, n) in planes(u1, kind):
            outside = rec[NY + r : NY + r + 8, :] + recb[at + r : at + r + 8, :] * own[r : r + 8, :]
            outside = dropped(beyond, outside)
            inside = edge[side, rows, :]
            ax, ay, az, k = v[0, z, rows, :], v[1, z, rows, :], v[2, z, rows, :], d[z, rows, :]
            last = advanced(c, w, e, s, n, inside, outside, ax, ay, jnp.where(top, az, -az), k)
            near = fin[5 * side, rows, :] + edge[2 + side, rows, :] * c
            ub[3 * side, rows, :] = last
            ub[1 + side, rows, :] = near
            put_columns(zs.at[side], rows, last + near)
    lane = lax.broadcasted_iota(jnp.int32, (128, 128), 1)
    hnear = jnp.concatenate([rtail[0:16, 128 * i : 128 * i + 128] for i in range(8)], axis=0)
    hfar = jnp.concatenate([rfar[2 * NY : FAR, 128 * i : 128 * i + 128] for i in range(8)], axis=0)
    hfar = dropped(at_end(), hfar)
    first_core = lax.axis_index("core") == 0
    halo_lo, halo_hi = jnp.where(first_core, hfar, hnear), jnp.where(first_core, hnear, hfar)
    for b in range(4):
        rows = slice(128 * b, 128 * b + 128)
        t = halved_x(
            jnp.concatenate(
                [
                    jnp.concatenate([paired(zs.at[0], i, 0, 32), ymid[i], paired(zs.at[1], i, 0, 32)], axis=0)
                    for i in (2 * b, 2 * b + 1)
                ],
                axis=1,
            )
        )
        hl = pltpu.roll(halo_lo, (128 - 32 * b) % 128, 1) if b else halo_lo
        hh = pltpu.roll(halo_hi, (96 - 32 * b) % 128, 1) if b != 3 else halo_hi
        halo = jnp.where(lane < 32, hl, hh)
        g = gcp[rows, :] + cb[rows, :] * halo
        g = jnp.where(lax.axis_index("tm") == 0, 0.0, g)
        gc[rows, :] = g
        jp[8 + 128 * b : 136 + 128 * b, :] = t - g
    jp[0:8, :] = jp[CX : CX + 8, :]
    jp[CX + 8 : CX + 24, :] = jp[8:24, :]


def finish(messages, fin, edge, velocity, diffusivity, gcp, cb, ymid):
    return pl.pallas_call(
        finish_kernel,
        out_shape=[
            jax.ShapeDtypeStruct((4, NY, NX), F32),
            jax.ShapeDtypeStruct((CX + 24, CL), F32),
            jax.ShapeDtypeStruct((CX, CL), F32),
        ],
        in_specs=[whole()] * 15,
        out_specs=[whole()] * 3,
        scratch_shapes=[
            pltpu.VMEM((2, NY, NX), F32),
            pltpu.VMEM((2, 8, NY, 128), F32),
        ],
        compiler_params=params(16),
        name="finish",
    )(*messages, fin, edge, velocity, diffusivity, gcp, cb, ymid)


def spread_kernel(jp, w0, w1, w2, w3, msg, quad):
    for i in range(BLOCKS):
        msg[i] = jp[XB * i : XB * i + WIN, :]
    mine = quad_rank()
    for i, window in enumerate((w0, w1, w2, w3)):
        quad[mine ^ i] = window[...]


def spread(sources, windows):
    return pl.pallas_call(
        spread_kernel,
        out_shape=[
            jax.ShapeDtypeStruct((BLOCKS, WIN, CL), F32),
            jax.ShapeDtypeStruct((QUAD, 4, WIN, CL), F32),
        ],
        in_specs=[whole()] * 5,
        out_specs=[whole()] * 2,
        compiler_params=params(16),
        name="spread",
    )(sources, *windows)


HALO_ROWS = (32, 32, 24, 24, 24, 24, 24, 32, 32, 32, 32, 24, 24)
HALO_AT = tuple(sum(HALO_ROWS[:i]) for i in range(len(HALO_ROWS) + 1))
SHARED = ((0, 6, 96), (1, 5, 64), (2, 4, 32))


def pick_kernel(got, quad, even, odd):
    lane = lax.broadcasted_iota(jnp.int32, (24, CL), 1)
    inner = slice(4, 28)
    for parity, out in enumerate((even, odd)):
        up = lax.rem(lax.axis_index("px"), 2) == parity
        near, far = jnp.where(up, 3, 0), jnp.where(up, 2, 1)

        def put(i, value):
            out[HALO_AT[i] : HALO_AT[i + 1], :] = value

        def shared(main, other, width):
            return jnp.where(
                up,
                jnp.where(lane >= CL - width, main, pltpu.roll(other, CL - width, 1)),
                jnp.where(lane < width, main, pltpu.roll(other, width, 1)),
            )

        for j in range(4):
            put(j, got[QUAD * j + near] if HALO_ROWS[j] == WIN else got[QUAD * j + near, inner, :])
            put(7 + j, quad[near, j])
        for j, other, width in SHARED:
            put(4 + j, shared(got[QUAD * j + far, inner, :], got[QUAD * other + near, inner, :], width))
        for j in range(2):
            put(11 + j, shared(quad[far, 2 * j, inner, :], quad[far, 2 * j + 1, inner, :], 64))


def pick(got, quad):
    halo = jax.ShapeDtypeStruct((HALO_AT[-1], CL), F32)
    return pl.pallas_call(
        pick_kernel,
        out_shape=[halo, halo],
        in_specs=[whole()] * 2,
        out_specs=[whole(), whole()],
        compiler_params=params(16),
        name="pick",
    )(got, quad)


def chain_kernel(got, quad, even, odd, out, cf, e):
    place = lax.axis_index("px")
    first = lax.rem(place, 2) == 0

    def block_of(ref, i):
        value = ref[HALO_AT[i] : HALO_AT[i + 1], :]
        if HALO_ROWS[i] == WIN:
            return value
        rest = jnp.zeros((4, CL), F32)
        return jnp.concatenate([rest, value, rest], axis=0)

    def below(i):
        return jnp.where(place == 0, 0.0, jnp.where(first, block_of(odd, i), block_of(even, i)))

    def above(i):
        return jnp.where(place == 3, 0.0, jnp.where(first, block_of(even, i), block_of(odd, i)))

    def source(j, block):
        if 2 <= block < 6:
            return got[QUAD * j + block - 2]
        halo = below if block < 2 else above
        if block in (0, 7):
            return halo(4 + j) if j < 3 else None
        if j < 4:
            return halo(j)
        _, other, width = SHARED[6 - j]
        return pltpu.roll(halo(10 - j), width if block == 1 else CL - width, 1)

    for block in range(8):
        halo = below if block < 2 else above
        if 2 <= block < 6:
            values = [quad[block - 2, i] for i in range(4)]
        elif block in (1, 6):
            values = [halo(7 + i) for i in range(4)]
        else:
            values = []
            for i in (11, 12):
                values += [halo(i), pltpu.roll(halo(i), 64, 1)]
        for i, value in enumerate(coarse_coefs(*values)):
            cf[i, block] = value
        e[0, block] = source(0, block)
    for q in range(QUAD):
        out[q] = jnp.zeros((XB, CL), F32)
    lane = lax.broadcasted_iota(jnp.int32, (WIN, CL), 1)
    for k in range(1, GROUPS):
        now, later = (k - 1) % 2, k % 2
        low = 0 if k < 3 else 1 if k < 7 else 2
        reach = range(max(0, low - 1), min(8, 9 - low))
        near = {b: lane_neighbours(e[now, b]) for b in reach}
        for block in range(low, 8 - low):
            c = e[now, block]
            b, t, s, n = near[block]
            if block > 0:
                b = jnp.where(lane < 32, near[block - 1][0], b)
            if block < 7:
                t = jnp.where(lane >= 96, near[block + 1][1], t)
            w, x = pltpu.roll(c, 1, 0), pltpu.roll(c, WIN - 1, 0)
            y = c + (
                (cf[0, block] * (w - c) + cf[1, block] * (x - c))
                + (cf[2, block] * (s - c) + cf[3, block] * (n - c))
                + (cf[4, block] * (b - c) + cf[5, block] * (t - c))
            )
            if 2 <= block < 6:
                out[QUAD * k + block - 2] = y[8 : 8 + XB, :]
            if k < GROUPS - 1:
                more = source(k, block)
                e[later, block] = y if more is None else y + more


def chain(got, quad, even, odd):
    return pl.pallas_call(
        chain_kernel,
        out_shape=jax.ShapeDtypeStruct((BLOCKS, XB, CL), F32),
        in_specs=[whole()] * 4,
        out_specs=whole(),
        scratch_shapes=[
            pltpu.VMEM((6, 8, WIN, CL), F32),
            pltpu.VMEM((2, 8, WIN, CL), F32),
        ],
        compiler_params=params(24),
        name="chain",
    )(got, quad, even, odd)


def result_kernel(y, gc, fin, ub, out, copied, buf, sems):
    copy_y = table((256, CL), lambda r, c: r // 2 == c)
    copy_x = table((128, 256), lambda r, c: r == c // 2)
    for b in range(4):
        rows = slice(128 * b, 128 * b + 128)
        for i, part in enumerate(split3(y[rows, :] - gc[rows, :])):
            copied[i, :, rows] = dot(copy_y, part, 1, 1).astype(BF16)
    copies = []
    for zc in range(4):
        rows = slice(zc * NY, zc * NY + NY)
        for b in range(4):
            cols = slice(256 * b, 256 * b + 256)
            fine = sum(dot(copied[i, rows, 128 * b : 128 * b + 128], copy_x, 1, 0) for i in range(3))
            for z in (2 * zc, 2 * zc + 1):
                base = fin[z - 1, :, cols] if 2 <= z < 6 else ub[z if z < 2 else z - 4, :, cols]
                buf[z, :, cols] = base + fine
        layers = slice(2 * zc, 2 * zc + 2)
        copies.append(pltpu.make_async_copy(buf.at[layers], out.at[layers], sems.at[zc]))
        copies[zc].start()
    for copy in copies:
        copy.wait()


def result(y, gc, fin, ub):
    return pl.pallas_call(
        result_kernel,
        out_shape=jax.ShapeDtypeStruct((LZ, NY, NX), F32),
        in_specs=[whole()] * 4,
        out_specs=remains(),
        scratch_shapes=[
            pltpu.VMEM((3, 4 * NY, CX), BF16),
            pltpu.VMEM((LZ, NY, NX), F32),
            pltpu.SemaphoreType.DMA((4,)),
        ],
        compiler_params=params(16),
        name="result",
    )(y, gc, fin, ub)


def swap(value, axes, partner):
    return lax.ppermute(value, axes, [(i, partner(i)) for i in range(lax.axis_size(axes))])


def off_chip(i):
    return (i + 1 if i % 2 else i - 1) % 16


def off_chip_copy(i):
    return (i // 16 ^ 1) * 16 + off_chip(i % 16)


def quad_beside(i):
    return (i + 1 if i % 2 else i - 1) % 4


def shards(state_old, velocity, diffusivity):
    state = state_old[0]
    ofar, ofac = edge_message(1, state, velocity, diffusivity)
    rfar = swap(ofar, SPACE, off_chip)
    rfac = swap(ofac, ("tm",) + SPACE, off_chip_copy)
    onear, otail = edge_message(0, state, velocity, diffusivity, ofac)
    rnear = swap(onear, SPACE, lambda i: i ^ 1)
    rtail = swap(otail, SPACE, lambda i: i ^ 1)
    ct, w0, w1, w2, w3 = coefs(velocity, diffusivity, rtail)
    windows = (
        w0,
        swap(w1, SPACE, lambda i: i ^ 1),
        swap(w2, ("tm",) + SPACE, lambda i: i ^ 18),
        swap(w3, ("tm",) + SPACE, lambda i: i ^ 19),
    )
    fin, edge, gcp, cb, ymid = interior(state, velocity, diffusivity, ct, windows[1])
    messages = (rnear, rtail, rfar, rfac, onear, otail, ofar, ofac)
    ub, sources, gc = finish(messages, fin, edge, velocity, diffusivity, gcp, cb, ymid)
    msg, quad = spread(sources, windows)
    got = lax.all_to_all(msg, GROUP, 0, 0)
    even, odd = pick(got, quad)
    even = swap(even, "px", lambda i: i ^ 1)
    odd = swap(odd, "px", quad_beside)
    back = lax.all_to_all(chain(got, quad, even, odd), GROUP, 0, 0)
    return result(back.reshape(CX, CL), gc, fin, ub)[None]


def solution(mesh):
    fine_mesh = Mesh(mesh.devices.reshape(GROUPS, 4, 2, 2), ("tm",) + SPACE)
    return jax.shard_map(
        shards,
        mesh=fine_mesh,
        in_specs=(
            P("tm", SPACE, None, None),
            P(None, SPACE, None, None),
            P(SPACE, None, None),
        ),
        out_specs=P("tm", SPACE, None, None),
        check_vma=False,
    )
```

```python
import functools

import jax
import jax.numpy as jnp
from jax import lax
from jax.experimental import pallas as pl
from jax.experimental.pallas import tpu as pltpu
from jax.sharding import Mesh
from jax.sharding import PartitionSpec as P

F32 = jnp.float32
BF16 = jnp.bfloat16
NY, NX = 64, 1024
LZ = 8
CX, CL = 512, 128
GROUPS = 8
QUAD = 4
BLOCKS = GROUPS * QUAD
XB = CX // BLOCKS
WIN = XB + 16
SPACE = ("px", "pz", "core")
GROUP = ("tm", "pz", "core")


def params(mib):
    return pltpu.CompilerParams(vmem_limit_bytes=mib * 1024 * 1024)


def split3(x):
    hi = x.astype(BF16)
    rest = x - hi.astype(F32)
    mid = rest.astype(BF16)
    return hi, mid, (rest - mid.astype(F32)).astype(BF16)


def dot(a, b, ca, cb):
    return lax.dot_general(a, b, (((ca,), (cb,)), ((), ())), preferred_element_type=F32)


def table(shape, test):
    rows = lax.broadcasted_iota(jnp.int32, shape, 0)
    cols = lax.broadcasted_iota(jnp.int32, shape, 1)
    return test(rows, cols).astype(F32).astype(BF16)


def halved_x(part):
    halve = table((128, 256), lambda r, c: r == c // 2)
    return sum(dot(halve, p, 1, 1) for p in split3(part)) * 0.125


def put_columns(ref, at, value):
    for i in range(NX // 128):
        ref[i, at, :] = value[:, 128 * i : 128 * i + 128]


def paired(ref, column, first, rows):
    return ref[column, pl.ds(first, rows, 2), :] + ref[column, pl.ds(first + 1, rows, 2), :]


def advanced(c, w, e, s, n, b, t, ax, ay, az, k):
    lap = ((w + e) + (s + n)) + ((b + t) - 6.0 * c)
    dx = jnp.abs(ax) * (jnp.where(ax > 0, w, e) - c)
    dy = jnp.abs(ay) * (jnp.where(ay > 0, s, n) - c)
    dz = jnp.abs(az) * (jnp.where(az > 0, b, t) - c)
    return (c + k * lap) + ((dx + dy) + dz)


def planes(ref, z):
    row = lax.broadcasted_iota(jnp.int32, (8, NX), 0)
    c = ref[z, 0:8, :]
    before = pltpu.roll(ref[z, NY - 8 : NY, :], 1, 0)
    for r in range(0, NY, 8):
        after = ref[z, (r + 8) % NY : (r + 8) % NY + 8, :]
        down = pltpu.roll(c, 1, 0)
        s = jnp.where(row == 0, before, down)
        n = jnp.where(row == 7, pltpu.roll(after, 7, 0), pltpu.roll(c, 7, 0))
        yield r, slice(r, r + 8), (c, pltpu.roll(c, 1, 1), pltpu.roll(c, NX - 1, 1), s, n)
        c, before = after, down


def coarse_coefs(vx, vy, vz, k):
    half = 0.5 * k
    out = []
    for a in (vx, vy, vz):
        out += [half + jnp.maximum(a, 0.0), half - jnp.minimum(a, 0.0)]
    return out


def lane_neighbours(c):
    y = lax.rem(lax.broadcasted_iota(jnp.int32, c.shape, 1), 32)
    below, above = pltpu.roll(c, 32, 1), pltpu.roll(c, CL - 32, 1)
    s = jnp.where(y == 0, pltpu.roll(c, CL - 31, 1), pltpu.roll(c, 1, 1))
    n = jnp.where(y == 31, pltpu.roll(c, 31, 1), pltpu.roll(c, CL - 1, 1))
    return below, above, s, n


FAR = 2 * NY + 16
TAIL = 16 + NY
CROWS = CX + 32


def edge_is_top(kind):
    return lax.axis_index("core") == kind


def edge_kernel(kind, st, vel, dif, *rest):
    if kind == 0:
        _, out, tail, u, v, d, zs, sems = rest
        coarse_out, coarse_at, factor, factor_at = tail, 0, tail, 16
    else:
        out, factor, u, v, d, zs, sems = rest
        coarse_out, coarse_at, factor_at = out, 2 * NY, 0
    top = edge_is_top(kind)
    z, beside = jnp.where(top, LZ - 1, 0), jnp.where(top, LZ - 2, 1)
    pairs = ((st.at[z], u.at[0]), (vel.at[:, z], v), (dif.at[z], d), (st.at[beside], u.at[1]))
    copies = [pltpu.make_async_copy(a, b, sems.at[i]) for i, (a, b) in enumerate(pairs)]
    for copy in copies:
        copy.start()
    for copy in copies:
        copy.wait()
    for r, rows, (c, w, e, s, n) in planes(u, 0):
        inside = u[1, rows, :]
        ax, ay, k = v[0, rows, :], v[1, rows, :], d[rows, :]
        up = jnp.where(top, v[2, rows, :], -v[2, rows, :])
        out[r : r + 8, :] = c
        out[NY + r : NY + r + 8, :] = advanced(c, w, e, s, n, inside, jnp.zeros_like(c), ax, ay, up, k)
        factor[factor_at + r : factor_at + r + 8, :] = k - jnp.minimum(up, 0.0)
        put_columns(zs, rows, c + inside)
    coarse = jnp.zeros((128, 128), F32)
    for b in range(4):
        part = jnp.concatenate([paired(zs, 2 * b + i, 0, 32) for i in range(2)], axis=1)
        t = halved_x(jnp.concatenate([part, jnp.zeros((96, 256), F32)], axis=0))
        coarse += pltpu.roll(t, 32 * b, 1) if b else t
    for i in range(8):
        coarse_out[coarse_at : coarse_at + 16, 128 * i : 128 * i + 128] = coarse[16 * i : 16 * i + 16, :]


def whole():
    return pl.BlockSpec(memory_space=pltpu.VMEM)


def remains():
    return pl.BlockSpec(memory_space=pltpu.HBM)


def edge_message(kind, state, velocity, diffusivity, *after):
    shapes = [((2 * NY, NX), (TAIL, NX)), ((FAR, NX), (NY, NX))][kind]
    return pl.pallas_call(
        functools.partial(edge_kernel, kind),
        out_shape=[jax.ShapeDtypeStruct(shape, F32) for shape in shapes],
        in_specs=[remains()] * 3 + [whole()] * len(after),
        out_specs=[whole()] * len(shapes),
        scratch_shapes=[
            pltpu.VMEM((2, NY, NX), F32),
            pltpu.VMEM((3, NY, NX), F32),
            pltpu.VMEM((NY, NX), F32),
            pltpu.VMEM((8, NY, 128), F32),
            pltpu.SemaphoreType.DMA((4,)),
        ],
        compiler_params=params([8, 52][kind]),
        cost_estimate=pl.CostEstimate(flops=15_000_000, bytes_accessed=[12_000_000, 3_000_000][kind], transcendentals=0),
        name=["near_message", "far_message"][kind],
    )(state, velocity, diffusivity, *after)


def quad_rank():
    return lax.axis_index("pz") * 2 + lax.axis_index("core")


def coefs_kernel(vel, dif, after, ct, w0, w1, w2, w3, zs):
    for comp in range(4):
        for zc in range(4):
            for r in range(0, NY, 8):
                rows = slice(r, r + 8)
                two = [dif[z, rows, :] if comp == 3 else vel[comp, z, rows, :] for z in (2 * zc, 2 * zc + 1)]
                put_columns(zs.at[comp], slice(zc * NY + r, zc * NY + r + 8), two[0] + two[1])
        for b in range(4):
            ct[comp, 8 + 128 * b : 136 + 128 * b, :] = halved_x(
                jnp.concatenate([paired(zs.at[comp], 2 * b + i, 0, 128) for i in range(2)], axis=1)
            )
        ct[comp, 0:8, :] = ct[comp, CX : CX + 8, :]
        ct[comp, CX + 8 : CX + 32, :] = ct[comp, 8:32, :]
    mine = quad_rank()
    slice_index = lax.axis_index("tm")
    for i, out in enumerate((w0, w1, w2, w3)):
        block = (slice_index if i < 2 else slice_index ^ 1) * QUAD + (mine ^ i)
        for comp in range(4):
            out[comp] = ct[comp, pl.ds(pl.multiple_of(block * XB, XB), WIN), :]


def coefs(velocity, diffusivity, after):
    window = jax.ShapeDtypeStruct((4, WIN, CL), F32)
    return pl.pallas_call(
        coefs_kernel,
        out_shape=[jax.ShapeDtypeStruct((4, CROWS, CL), F32)] + [window] * 4,
        in_specs=[whole()] * 3,
        out_specs=[whole()] * 5,
        scratch_shapes=[pltpu.VMEM((4, 8, 4 * NY, 128), F32)],
        compiler_params=params(12),
        cost_estimate=pl.CostEstimate(flops=20_000_000, bytes_accessed=9_000_000, transcendentals=0),
        name="coefs",
    )(velocity, diffusivity, after)


def interior_kernel(u, v, d, ct, after, fin, edge, gcp, cb, ymid, u1, zs, zf, ct0):
    def first(z, _):
        for _, rows, (c, w, e, s, n) in planes(u, z):
            u1[z, rows, :] = advanced(
                c, w, e, s, n, u[z - 1, rows, :], u[z + 1, rows, :],
                v[0, z, rows, :], v[1, z, rows, :], v[2, z, rows, :], d[z, rows, :],
            )
        return 0

    lax.fori_loop(1, LZ - 1, first, 0)
    u1[0] = jnp.zeros((NY, NX), F32)
    u1[LZ - 1] = jnp.zeros((NY, NX), F32)
    edge[0] = u1[1]
    edge[1] = u1[LZ - 2]

    def second(z, _):
        for _, rows, (c, w, e, s, n) in planes(u1, z):
            fin[z - 1, rows, :] = advanced(
                c, w, e, s, n, u1[z - 1, rows, :], u1[z + 1, rows, :],
                v[0, z, rows, :], v[1, z, rows, :], v[2, z, rows, :], d[z, rows, :],
            )
        return 0

    lax.fori_loop(1, LZ - 1, second, 0)
    edge[2] = d[1] + jnp.maximum(v[2, 1], 0.0)
    edge[3] = d[LZ - 2] - jnp.minimum(v[2, LZ - 2], 0.0)
    for zc in (1, 2):
        for r in range(0, NY, 8):
            rows = slice(r, r + 8)
            put_columns(zf, slice((zc - 1) * NY + r, (zc - 1) * NY + r + 8), fin[2 * zc - 1, rows, :] + fin[2 * zc, rows, :])
    for i in range(8):
        ymid[i] = paired(zf, i, 0, 64)

    for zc in range(4):
        for r in range(0, NY, 8):
            rows = slice(r, r + 8)
            put_columns(zs, slice(zc * NY + r, zc * NY + r + 8), u[2 * zc, rows, :] + u[2 * zc + 1, rows, :])
    for b in range(4):
        ct0[8 + 128 * b : 136 + 128 * b, :] = halved_x(
            jnp.concatenate([paired(zs, 2 * b + i, 0, 128) for i in range(2)], axis=1)
        )
    ct0[0:8, :] = ct0[CX : CX + 8, :]
    ct0[CX + 8 : CX + 16, :] = ct0[8:16, :]
    lane = lax.broadcasted_iota(jnp.int32, (64, CL), 1)
    for r in range(0, CX, 64):
        c = ct0[8 + r : 72 + r, :]
        xl, xh, yl, yh, zl, zh = coarse_coefs(*(ct[i, 8 + r : 72 + r, :] for i in range(4)))
        b, t, s, n = lane_neighbours(c)
        b = jnp.where(lane < 32, 0.0, b)
        t = jnp.where(lane >= 96, 0.0, t)
        w = ct0[7 + r : 71 + r, :]
        e = ct0[9 + r : 73 + r, :]
        gcp[r : r + 64, :] = c + (
            (xl * (w - c) + xh * (e - c)) + (yl * (s - c) + yh * (n - c)) + (zl * (b - c) + zh * (t - c))
        )
        cb[r : r + 64, :] = jnp.where(lane < 32, zl, jnp.where(lane >= 96, zh, 0.0))


def interior(state, velocity, diffusivity, ct, after):
    small = jax.ShapeDtypeStruct((CX, CL), F32)
    return pl.pallas_call(
        interior_kernel,
        out_shape=[
            jax.ShapeDtypeStruct((LZ - 2, NY, NX), F32),
            jax.ShapeDtypeStruct((4, NY, NX), F32),
            small,
            small,
            jax.ShapeDtypeStruct((8, 64, 128), F32),
        ],
        in_specs=[whole()] * 5,
        out_specs=[whole()] * 5,
        scratch_shapes=[
            pltpu.VMEM((LZ, NY, NX), F32),
            pltpu.VMEM((8, 4 * NY, 128), F32),
            pltpu.VMEM((8, 2 * NY, 128), F32),
            pltpu.VMEM((CX + 16, CL), F32),
        ],
        compiler_params=params(16),
        cost_estimate=pl.CostEstimate(flops=60_000_000, bytes_accessed=20_000_000, transcendentals=0),
        name="interior",
    )(state, velocity, diffusivity, ct, after)


def at_end():
    slab = lax.axis_index("px") * QUAD + quad_rank()
    return (slab == 0) | (slab == 15)


def dropped(beyond, value):
    return value if beyond is False else jnp.where(beyond, 0.0, value)


def edge_layers(kind, rec, own, recb, ownb, at, fin, edge, v, d, ub, zs, u1):
    top = edge_is_top(kind)
    side = jnp.where(top, 1, 0)
    beyond = kind == 1 and at_end()
    for r in range(0, NY, 8):
        u1[0, r : r + 8, :] = (
            own[NY + r : NY + r + 8, :] + ownb[at + r : at + r + 8, :] * dropped(beyond, rec[r : r + 8, :])
        )
    z = side * (LZ - 1)
    for r, rows, (c, w, e, s, n) in planes(u1, 0):
        outside = rec[NY + r : NY + r + 8, :] + recb[at + r : at + r + 8, :] * own[r : r + 8, :]
        outside = dropped(beyond, outside)
        inside = edge[side, rows, :]
        ax, ay, az, k = v[0, z, rows, :], v[1, z, rows, :], v[2, z, rows, :], d[z, rows, :]
        last = advanced(c, w, e, s, n, inside, outside, ax, ay, jnp.where(top, az, -az), k)
        near = fin[5 * side, rows, :] + edge[2 + side, rows, :] * c
        ub[0, rows, :] = last
        ub[1, rows, :] = near
        put_columns(zs, rows, last + near)


def finish_near_kernel(rnear, rtail, onear, otail, fin, edge, v, d, ub, zs, u1):
    edge_layers(0, rnear, onear, rtail, otail, 16, fin, edge, v, d, ub, zs, u1)


def finish_near(messages, fin, edge, velocity, diffusivity):
    return pl.pallas_call(
        finish_near_kernel,
        out_shape=[jax.ShapeDtypeStruct((2, NY, NX), F32), jax.ShapeDtypeStruct((8, NY, 128), F32)],
        in_specs=[whole()] * 8,
        out_specs=[whole()] * 2,
        scratch_shapes=[pltpu.VMEM((1, NY, NX), F32)],
        compiler_params=params(16),
        name="finish_near",
    )(*messages, fin, edge, velocity, diffusivity)


def finish_kernel(rtail, rfar, rfac, ofar, ofac, fin, edge, v, d, gcp, cb, ymid, zs_near, ub, jp, gc, u1, zs):
    edge_layers(1, rfar, ofar, rfac, ofac, 0, fin, edge, v, d, ub, zs, u1)
    lane = lax.broadcasted_iota(jnp.int32, (128, 128), 1)
    hnear = jnp.concatenate([rtail[0:16, 128 * i : 128 * i + 128] for i in range(8)], axis=0)
    hfar = jnp.concatenate([rfar[2 * NY : FAR, 128 * i : 128 * i + 128] for i in range(8)], axis=0)
    hfar = dropped(at_end(), hfar)
    first_core = lax.axis_index("core") == 0
    halo_lo, halo_hi = jnp.where(first_core, hfar, hnear), jnp.where(first_core, hnear, hfar)

    def sides(i):
        a, b = paired(zs, i, 0, 32), paired(zs_near, i, 0, 32)
        return [jnp.where(first_core, a, b), ymid[i], jnp.where(first_core, b, a)]

    for b in range(4):
        rows = slice(128 * b, 128 * b + 128)
        t = halved_x(
            jnp.concatenate(
                [
                    jnp.concatenate(sides(i), axis=0)
                    for i in (2 * b, 2 * b + 1)
                ],
                axis=1,
            )
        )
        hl = pltpu.roll(halo_lo, (128 - 32 * b) % 128, 1) if b else halo_lo
        hh = pltpu.roll(halo_hi, (96 - 32 * b) % 128, 1) if b != 3 else halo_hi
        halo = jnp.where(lane < 32, hl, hh)
        g = gcp[rows, :] + cb[rows, :] * halo
        g = jnp.where(lax.axis_index("tm") == 0, 0.0, g)
        gc[rows, :] = g
        jp[8 + 128 * b : 136 + 128 * b, :] = t - g
    jp[0:8, :] = jp[CX : CX + 8, :]
    jp[CX + 8 : CX + 24, :] = jp[8:24, :]


def finish(messages, fin, edge, velocity, diffusivity, gcp, cb, ymid, zs_near):
    return pl.pallas_call(
        finish_kernel,
        out_shape=[
            jax.ShapeDtypeStruct((2, NY, NX), F32),
            jax.ShapeDtypeStruct((CX + 24, CL), F32),
            jax.ShapeDtypeStruct((CX, CL), F32),
        ],
        in_specs=[whole()] * 13,
        out_specs=[whole()] * 3,
        scratch_shapes=[pltpu.VMEM((1, NY, NX), F32), pltpu.VMEM((8, NY, 128), F32)],
        compiler_params=params(16),
        name="finish",
    )(*messages, fin, edge, velocity, diffusivity, gcp, cb, ymid, zs_near)


def spread_kernel(jp, w0, w1, w2, w3, msg, quad):
    for i in range(BLOCKS):
        msg[i] = jp[XB * i : XB * i + WIN, :]
    mine = quad_rank()
    for i, window in enumerate((w0, w1, w2, w3)):
        quad[mine ^ i] = window[...]


def spread(sources, windows):
    return pl.pallas_call(
        spread_kernel,
        out_shape=[
            jax.ShapeDtypeStruct((BLOCKS, WIN, CL), F32),
            jax.ShapeDtypeStruct((QUAD, 4, WIN, CL), F32),
        ],
        in_specs=[whole()] * 5,
        out_specs=[whole()] * 2,
        compiler_params=params(16),
        name="spread",
    )(sources, *windows)


HALO_ROWS = (32, 32, 24, 24, 24, 24, 24, 32, 32, 32, 32, 24, 24)
HALO_AT = tuple(sum(HALO_ROWS[:i]) for i in range(len(HALO_ROWS) + 1))
SHARED = ((0, 6, 96), (1, 5, 64), (2, 4, 32))


def pick_kernel(got, quad, even, odd):
    lane = lax.broadcasted_iota(jnp.int32, (24, CL), 1)
    inner = slice(4, 28)
    for parity, out in enumerate((even, odd)):
        up = lax.rem(lax.axis_index("px"), 2) == parity
        near, far = jnp.where(up, 3, 0), jnp.where(up, 2, 1)

        def put(i, value):
            out[HALO_AT[i] : HALO_AT[i + 1], :] = value

        def shared(main, other, width):
            return jnp.where(
                up,
                jnp.where(lane >= CL - width, main, pltpu.roll(other, CL - width, 1)),
                jnp.where(lane < width, main, pltpu.roll(other, width, 1)),
            )

        for j in range(4):
            put(j, got[QUAD * j + near] if HALO_ROWS[j] == WIN else got[QUAD * j + near, inner, :])
            put(7 + j, quad[near, j])
        for j, other, width in SHARED:
            put(4 + j, shared(got[QUAD * j + far, inner, :], got[QUAD * other + near, inner, :], width))
        for j in range(2):
            put(11 + j, shared(quad[far, 2 * j, inner, :], quad[far, 2 * j + 1, inner, :], 64))


def pick(got, quad):
    halo = jax.ShapeDtypeStruct((HALO_AT[-1], CL), F32)
    return pl.pallas_call(
        pick_kernel,
        out_shape=[halo, halo],
        in_specs=[whole()] * 2,
        out_specs=[whole(), whole()],
        compiler_params=params(16),
        name="pick",
    )(got, quad)


def chain_kernel(got, quad, even, odd, out, cf, e):
    place = lax.axis_index("px")
    first = lax.rem(place, 2) == 0

    def block_of(ref, i):
        value = ref[HALO_AT[i] : HALO_AT[i + 1], :]
        if HALO_ROWS[i] == WIN:
            return value
        rest = jnp.zeros((4, CL), F32)
        return jnp.concatenate([rest, value, rest], axis=0)

    def below(i):
        return jnp.where(place == 0, 0.0, jnp.where(first, block_of(odd, i), block_of(even, i)))

    def above(i):
        return jnp.where(place == 3, 0.0, jnp.where(first, block_of(even, i), block_of(odd, i)))

    def source(j, block):
        if 2 <= block < 6:
            return got[QUAD * j + block - 2]
        halo = below if block < 2 else above
        if block in (0, 7):
            return halo(4 + j) if j < 3 else None
        if j < 4:
            return halo(j)
        _, other, width = SHARED[6 - j]
        return pltpu.roll(halo(10 - j), width if block == 1 else CL - width, 1)

    for block in range(8):
        halo = below if block < 2 else above
        if 2 <= block < 6:
            values = [quad[block - 2, i] for i in range(4)]
        elif block in (1, 6):
            values = [halo(7 + i) for i in range(4)]
        else:
            values = []
            for i in (11, 12):
                values += [halo(i), pltpu.roll(halo(i), 64, 1)]
        for i, value in enumerate(coarse_coefs(*values)):
            cf[i, block] = value
        e[0, block] = source(0, block)
    for q in range(QUAD):
        out[q] = jnp.zeros((XB, CL), F32)
    lane = lax.broadcasted_iota(jnp.int32, (WIN, CL), 1)
    for k in range(1, GROUPS):
        now, later = (k - 1) % 2, k % 2
        low = 0 if k < 3 else 1 if k < 7 else 2
        reach = range(max(0, low - 1), min(8, 9 - low))
        near = {b: lane_neighbours(e[now, b]) for b in reach}
        for block in range(low, 8 - low):
            c = e[now, block]
            b, t, s, n = near[block]
            if block > 0:
                b = jnp.where(lane < 32, near[block - 1][0], b)
            if block < 7:
                t = jnp.where(lane >= 96, near[block + 1][1], t)
            w, x = pltpu.roll(c, 1, 0), pltpu.roll(c, WIN - 1, 0)
            y = c + (
                (cf[0, block] * (w - c) + cf[1, block] * (x - c))
                + (cf[2, block] * (s - c) + cf[3, block] * (n - c))
                + (cf[4, block] * (b - c) + cf[5, block] * (t - c))
            )
            if 2 <= block < 6:
                out[QUAD * k + block - 2] = y[8 : 8 + XB, :]
            if k < GROUPS - 1:
                more = source(k, block)
                e[later, block] = y if more is None else y + more


def chain(got, quad, even, odd):
    return pl.pallas_call(
        chain_kernel,
        out_shape=jax.ShapeDtypeStruct((BLOCKS, XB, CL), F32),
        in_specs=[whole()] * 4,
        out_specs=whole(),
        scratch_shapes=[
            pltpu.VMEM((6, 8, WIN, CL), F32),
            pltpu.VMEM((2, 8, WIN, CL), F32),
        ],
        compiler_params=params(24),
        name="chain",
    )(got, quad, even, odd)


def result_kernel(y, gc, fin, near, far, out, copied, buf, sems):
    first_core = lax.axis_index("core") == 0
    copy_y = table((256, CL), lambda r, c: r // 2 == c)
    copy_x = table((128, 256), lambda r, c: r == c // 2)
    for b in range(4):
        rows = slice(128 * b, 128 * b + 128)
        for i, part in enumerate(split3(y[rows, :] - gc[rows, :])):
            copied[i, :, rows] = dot(copy_y, part, 1, 1).astype(BF16)
    copies = []
    for zc in range(4):
        rows = slice(zc * NY, zc * NY + NY)
        for b in range(4):
            cols = slice(256 * b, 256 * b + 256)
            fine = sum(dot(copied[i, rows, 128 * b : 128 * b + 128], copy_x, 1, 0) for i in range(3))
            for z in (2 * zc, 2 * zc + 1):
                if 2 <= z < 6:
                    base = fin[z - 1, :, cols]
                else:
                    here, there = (far, near) if z < 2 else (near, far)
                    i = min(z, LZ - 1 - z)
                    base = jnp.where(first_core, here[i, :, cols], there[i, :, cols])
                buf[z, :, cols] = base + fine
        layers = slice(2 * zc, 2 * zc + 2)
        copies.append(pltpu.make_async_copy(buf.at[layers], out.at[layers], sems.at[zc]))
        copies[zc].start()
    for copy in copies:
        copy.wait()


def result(y, gc, fin, near, far):
    return pl.pallas_call(
        result_kernel,
        out_shape=jax.ShapeDtypeStruct((LZ, NY, NX), F32),
        in_specs=[whole()] * 5,
        out_specs=remains(),
        scratch_shapes=[
            pltpu.VMEM((3, 4 * NY, CX), BF16),
            pltpu.VMEM((LZ, NY, NX), F32),
            pltpu.SemaphoreType.DMA((4,)),
        ],
        compiler_params=params(16),
        name="result",
    )(y, gc, fin, near, far)


def swap(value, axes, partner):
    return lax.ppermute(value, axes, [(i, partner(i)) for i in range(lax.axis_size(axes))])


def off_chip(i):
    return (i + 1 if i % 2 else i - 1) % 16


def off_chip_copy(i):
    return (i // 16 ^ 1) * 16 + off_chip(i % 16)


def quad_beside(i):
    return (i + 1 if i % 2 else i - 1) % 4


def shards(state_old, velocity, diffusivity):
    state = state_old[0]
    ofar, ofac = edge_message(1, state, velocity, diffusivity)
    rfar = swap(ofar, SPACE, off_chip)
    rfac = swap(ofac, ("tm",) + SPACE, off_chip_copy)
    onear, otail = edge_message(0, state, velocity, diffusivity, ofac)
    rnear = swap(onear, SPACE, lambda i: i ^ 1)
    rtail = swap(otail, SPACE, lambda i: i ^ 1)
    ct, w0, w1, w2, w3 = coefs(velocity, diffusivity, rtail)
    windows = (
        w0,
        swap(w1, SPACE, lambda i: i ^ 1),
        swap(w2, ("tm",) + SPACE, lambda i: i ^ 18),
        swap(w3, ("tm",) + SPACE, lambda i: i ^ 19),
    )
    fin, edge, gcp, cb, ymid = interior(state, velocity, diffusivity, ct, windows[1])
    near, zs_near = finish_near((rnear, rtail, onear, otail), fin, edge, velocity, diffusivity)
    messages = (rtail, rfar, rfac, ofar, ofac)
    far, sources, gc = finish(messages, fin, edge, velocity, diffusivity, gcp, cb, ymid, zs_near)
    msg, quad = spread(sources, windows)
    got = lax.all_to_all(msg, GROUP, 0, 0)
    even, odd = pick(got, quad)
    even = swap(even, "px", lambda i: i ^ 1)
    odd = swap(odd, "px", quad_beside)
    back = lax.all_to_all(chain(got, quad, even, odd), GROUP, 0, 0)
    return result(back.reshape(CX, CL), gc, fin, near, far)[None]


def solution(mesh):
    fine_mesh = Mesh(mesh.devices.reshape(GROUPS, 4, 2, 2), ("tm",) + SPACE)
    return jax.shard_map(
        shards,
        mesh=fine_mesh,
        in_specs=(
            P("tm", SPACE, None, None),
            P(None, SPACE, None, None),
            P(SPACE, None, None),
        ),
        out_specs=P("tm", SPACE, None, None),
        check_vma=False,
    )
```

```python
import functools

import jax
import jax.numpy as jnp
from jax import lax
from jax.experimental import pallas as pl
from jax.experimental.pallas import tpu as pltpu
from jax.sharding import Mesh
from jax.sharding import PartitionSpec as P

F32 = jnp.float32
BF16 = jnp.bfloat16
NY, NX = 64, 1024
LZ = 8
CX, CL = 512, 128
GROUPS = 8
QUAD = 4
BLOCKS = GROUPS * QUAD
XB = CX // BLOCKS
WIN = XB + 16
SPACE = ("px", "pz", "core")
GROUP = ("tm", "pz", "core")


def params(mib):
    return pltpu.CompilerParams(vmem_limit_bytes=mib * 1024 * 1024)


def split3(x):
    hi = x.astype(BF16)
    rest = x - hi.astype(F32)
    mid = rest.astype(BF16)
    return hi, mid, (rest - mid.astype(F32)).astype(BF16)


def dot(a, b, ca, cb):
    return lax.dot_general(a, b, (((ca,), (cb,)), ((), ())), preferred_element_type=F32)


def table(shape, test):
    rows = lax.broadcasted_iota(jnp.int32, shape, 0)
    cols = lax.broadcasted_iota(jnp.int32, shape, 1)
    return test(rows, cols).astype(F32).astype(BF16)


def halved_x(part):
    halve = table((128, 256), lambda r, c: r == c // 2)
    return sum(dot(halve, p, 1, 1) for p in split3(part)) * 0.125


def put_columns(ref, at, value):
    for i in range(NX // 128):
        ref[i, at, :] = value[:, 128 * i : 128 * i + 128]


def paired(ref, column, first, rows):
    return ref[column, pl.ds(first, rows, 2), :] + ref[column, pl.ds(first + 1, rows, 2), :]


def advanced(c, w, e, s, n, b, t, ax, ay, az, k):
    lap = ((w + e) + (s + n)) + ((b + t) - 6.0 * c)
    dx = jnp.abs(ax) * (jnp.where(ax > 0, w, e) - c)
    dy = jnp.abs(ay) * (jnp.where(ay > 0, s, n) - c)
    dz = jnp.abs(az) * (jnp.where(az > 0, b, t) - c)
    return (c + k * lap) + ((dx + dy) + dz)


def planes(ref, z):
    row = lax.broadcasted_iota(jnp.int32, (8, NX), 0)
    c = ref[z, 0:8, :]
    before = pltpu.roll(ref[z, NY - 8 : NY, :], 1, 0)
    for r in range(0, NY, 8):
        after = ref[z, (r + 8) % NY : (r + 8) % NY + 8, :]
        down = pltpu.roll(c, 1, 0)
        s = jnp.where(row == 0, before, down)
        n = jnp.where(row == 7, pltpu.roll(after, 7, 0), pltpu.roll(c, 7, 0))
        yield r, slice(r, r + 8), (c, pltpu.roll(c, 1, 1), pltpu.roll(c, NX - 1, 1), s, n)
        c, before = after, down


def coarse_coefs(vx, vy, vz, k):
    half = 0.5 * k
    out = []
    for a in (vx, vy, vz):
        out += [half + jnp.maximum(a, 0.0), half - jnp.minimum(a, 0.0)]
    return out


def lane_neighbours(c):
    y = lax.rem(lax.broadcasted_iota(jnp.int32, c.shape, 1), 32)
    below, above = pltpu.roll(c, 32, 1), pltpu.roll(c, CL - 32, 1)
    s = jnp.where(y == 0, pltpu.roll(c, CL - 31, 1), pltpu.roll(c, 1, 1))
    n = jnp.where(y == 31, pltpu.roll(c, 31, 1), pltpu.roll(c, CL - 1, 1))
    return below, above, s, n


FAR = 2 * NY + 16
TAIL = 16 + NY
CROWS = CX + 32


def edge_is_top(kind):
    return lax.axis_index("core") == kind


def edge_kernel(kind, st, vel, dif, *rest):
    if kind == 0:
        _, out, tail, u, v, d, zs, sems = rest
        coarse_out, coarse_at, factor, factor_at = tail, 0, tail, 16
    else:
        out, factor, u, v, d, zs, sems = rest
        coarse_out, coarse_at, factor_at = out, 2 * NY, 0
    top = edge_is_top(kind)
    z, beside = jnp.where(top, LZ - 1, 0), jnp.where(top, LZ - 2, 1)
    pairs = ((st.at[z], u.at[0]), (vel.at[:, z], v), (dif.at[z], d), (st.at[beside], u.at[1]))
    copies = [pltpu.make_async_copy(a, b, sems.at[i]) for i, (a, b) in enumerate(pairs)]
    for copy in copies:
        copy.start()
    for copy in copies:
        copy.wait()
    for r, rows, (c, w, e, s, n) in planes(u, 0):
        inside = u[1, rows, :]
        ax, ay, k = v[0, rows, :], v[1, rows, :], d[rows, :]
        up = jnp.where(top, v[2, rows, :], -v[2, rows, :])
        out[r : r + 8, :] = c
        out[NY + r : NY + r + 8, :] = advanced(c, w, e, s, n, inside, jnp.zeros_like(c), ax, ay, up, k)
        factor[factor_at + r : factor_at + r + 8, :] = k - jnp.minimum(up, 0.0)
        put_columns(zs, rows, c + inside)
    coarse = jnp.zeros((128, 128), F32)
    for b in range(4):
        part = jnp.concatenate([paired(zs, 2 * b + i, 0, 32) for i in range(2)], axis=1)
        t = halved_x(jnp.concatenate([part, jnp.zeros((96, 256), F32)], axis=0))
        coarse += pltpu.roll(t, 32 * b, 1) if b else t
    for i in range(8):
        coarse_out[coarse_at : coarse_at + 16, 128 * i : 128 * i + 128] = coarse[16 * i : 16 * i + 16, :]


def whole():
    return pl.BlockSpec(memory_space=pltpu.VMEM)


def remains():
    return pl.BlockSpec(memory_space=pltpu.HBM)


def edge_message(kind, state, velocity, diffusivity, *after):
    shapes = [((2 * NY, NX), (TAIL, NX)), ((FAR, NX), (NY, NX))][kind]
    return pl.pallas_call(
        functools.partial(edge_kernel, kind),
        out_shape=[jax.ShapeDtypeStruct(shape, F32) for shape in shapes],
        in_specs=[remains()] * 3 + [whole()] * len(after),
        out_specs=[whole()] * len(shapes),
        scratch_shapes=[
            pltpu.VMEM((2, NY, NX), F32),
            pltpu.VMEM((3, NY, NX), F32),
            pltpu.VMEM((NY, NX), F32),
            pltpu.VMEM((8, NY, 128), F32),
            pltpu.SemaphoreType.DMA((4,)),
        ],
        compiler_params=params([8, 52][kind]),
        cost_estimate=pl.CostEstimate(flops=15_000_000, bytes_accessed=[12_000_000, 3_000_000][kind], transcendentals=0),
        name=["near_message", "far_message"][kind],
    )(state, velocity, diffusivity, *after)


def quad_rank():
    return lax.axis_index("pz") * 2 + lax.axis_index("core")


def coefs_kernel(vel, dif, ct, zs):
    for comp in range(4):
        for zc in range(4):
            for r in range(0, NY, 8):
                rows = slice(r, r + 8)
                two = [dif[z, rows, :] if comp == 3 else vel[comp, z, rows, :] for z in (2 * zc, 2 * zc + 1)]
                put_columns(zs.at[comp], slice(zc * NY + r, zc * NY + r + 8), two[0] + two[1])
        for b in range(4):
            ct[comp, 8 + 128 * b : 136 + 128 * b, :] = halved_x(
                jnp.concatenate([paired(zs.at[comp], 2 * b + i, 0, 128) for i in range(2)], axis=1)
            )
        ct[comp, 0:8, :] = ct[comp, CX : CX + 8, :]
        ct[comp, CX + 8 : CX + 32, :] = ct[comp, 8:32, :]


def coefs(velocity, diffusivity):
    return pl.pallas_call(
        coefs_kernel,
        out_shape=jax.ShapeDtypeStruct((4, CROWS, CL), F32),
        in_specs=[whole()] * 2,
        out_specs=whole(),
        scratch_shapes=[pltpu.VMEM((4, 8, 4 * NY, 128), F32)],
        compiler_params=params(12),
        cost_estimate=pl.CostEstimate(flops=20_000_000, bytes_accessed=9_000_000, transcendentals=0),
        name="coefs",
    )(velocity, diffusivity)


def cut_kernel(ct, after, w0, w1, w2, w3):
    mine = quad_rank()
    slice_index = lax.axis_index("tm")
    for i, out in enumerate((w0, w1, w2, w3)):
        block = (slice_index if i < 2 else slice_index ^ 1) * QUAD + (mine ^ i)
        for comp in range(4):
            out[comp] = ct[comp, pl.ds(pl.multiple_of(block * XB, XB), WIN), :]


def cut(ct, after):
    window = jax.ShapeDtypeStruct((4, WIN, CL), F32)
    return pl.pallas_call(
        cut_kernel,
        out_shape=[window] * 4,
        in_specs=[whole()] * 2,
        out_specs=[whole()] * 4,
        compiler_params=params(12),
        name="cut",
    )(ct, after)


def interior_kernel(u, v, d, ct, after, fin, edge, gcp, cb, ymid, u1, zs, zf, ct0):
    def first(z, _):
        for _, rows, (c, w, e, s, n) in planes(u, z):
            u1[z, rows, :] = advanced(
                c, w, e, s, n, u[z - 1, rows, :], u[z + 1, rows, :],
                v[0, z, rows, :], v[1, z, rows, :], v[2, z, rows, :], d[z, rows, :],
            )
        return 0

    lax.fori_loop(1, LZ - 1, first, 0)
    u1[0] = jnp.zeros((NY, NX), F32)
    u1[LZ - 1] = jnp.zeros((NY, NX), F32)
    edge[0] = u1[1]
    edge[1] = u1[LZ - 2]

    def second(z, _):
        for _, rows, (c, w, e, s, n) in planes(u1, z):
            fin[z - 1, rows, :] = advanced(
                c, w, e, s, n, u1[z - 1, rows, :], u1[z + 1, rows, :],
                v[0, z, rows, :], v[1, z, rows, :], v[2, z, rows, :], d[z, rows, :],
            )
        return 0

    lax.fori_loop(1, LZ - 1, second, 0)
    edge[2] = d[1] + jnp.maximum(v[2, 1], 0.0)
    edge[3] = d[LZ - 2] - jnp.minimum(v[2, LZ - 2], 0.0)
    for zc in (1, 2):
        for r in range(0, NY, 8):
            rows = slice(r, r + 8)
            put_columns(zf, slice((zc - 1) * NY + r, (zc - 1) * NY + r + 8), fin[2 * zc - 1, rows, :] + fin[2 * zc, rows, :])
    for i in range(8):
        ymid[i] = paired(zf, i, 0, 64)

    for zc in range(4):
        for r in range(0, NY, 8):
            rows = slice(r, r + 8)
            put_columns(zs, slice(zc * NY + r, zc * NY + r + 8), u[2 * zc, rows, :] + u[2 * zc + 1, rows, :])
    for b in range(4):
        ct0[8 + 128 * b : 136 + 128 * b, :] = halved_x(
            jnp.concatenate([paired(zs, 2 * b + i, 0, 128) for i in range(2)], axis=1)
        )
    ct0[0:8, :] = ct0[CX : CX + 8, :]
    ct0[CX + 8 : CX + 16, :] = ct0[8:16, :]
    lane = lax.broadcasted_iota(jnp.int32, (64, CL), 1)
    for r in range(0, CX, 64):
        c = ct0[8 + r : 72 + r, :]
        xl, xh, yl, yh, zl, zh = coarse_coefs(*(ct[i, 8 + r : 72 + r, :] for i in range(4)))
        b, t, s, n = lane_neighbours(c)
        b = jnp.where(lane < 32, 0.0, b)
        t = jnp.where(lane >= 96, 0.0, t)
        w = ct0[7 + r : 71 + r, :]
        e = ct0[9 + r : 73 + r, :]
        gcp[r : r + 64, :] = c + (
            (xl * (w - c) + xh * (e - c)) + (yl * (s - c) + yh * (n - c)) + (zl * (b - c) + zh * (t - c))
        )
        cb[r : r + 64, :] = jnp.where(lane < 32, zl, jnp.where(lane >= 96, zh, 0.0))


def interior(state, velocity, diffusivity, ct, after):
    small = jax.ShapeDtypeStruct((CX, CL), F32)
    return pl.pallas_call(
        interior_kernel,
        out_shape=[
            jax.ShapeDtypeStruct((LZ - 2, NY, NX), F32),
            jax.ShapeDtypeStruct((4, NY, NX), F32),
            small,
            small,
            jax.ShapeDtypeStruct((8, 64, 128), F32),
        ],
        in_specs=[whole()] * 5,
        out_specs=[whole()] * 5,
        scratch_shapes=[
            pltpu.VMEM((LZ, NY, NX), F32),
            pltpu.VMEM((8, 4 * NY, 128), F32),
            pltpu.VMEM((8, 2 * NY, 128), F32),
            pltpu.VMEM((CX + 16, CL), F32),
        ],
        compiler_params=params(16),
        cost_estimate=pl.CostEstimate(flops=60_000_000, bytes_accessed=20_000_000, transcendentals=0),
        name="interior",
    )(state, velocity, diffusivity, ct, after)


def at_end():
    slab = lax.axis_index("px") * QUAD + quad_rank()
    return (slab == 0) | (slab == 15)


def dropped(beyond, value):
    return value if beyond is False else jnp.where(beyond, 0.0, value)


def edge_layers(kind, rec, own, recb, ownb, at, fin, edge, v, d, ub, zs, u1):
    top = edge_is_top(kind)
    side = jnp.where(top, 1, 0)
    beyond = kind == 1 and at_end()
    for r in range(0, NY, 8):
        u1[0, r : r + 8, :] = (
            own[NY + r : NY + r + 8, :] + ownb[at + r : at + r + 8, :] * dropped(beyond, rec[r : r + 8, :])
        )
    z = side * (LZ - 1)
    for r, rows, (c, w, e, s, n) in planes(u1, 0):
        outside = rec[NY + r : NY + r + 8, :] + recb[at + r : at + r + 8, :] * own[r : r + 8, :]
        outside = dropped(beyond, outside)
        inside = edge[side, rows, :]
        ax, ay, az, k = v[0, z, rows, :], v[1, z, rows, :], v[2, z, rows, :], d[z, rows, :]
        last = advanced(c, w, e, s, n, inside, outside, ax, ay, jnp.where(top, az, -az), k)
        near = fin[5 * side, rows, :] + edge[2 + side, rows, :] * c
        ub[0, rows, :] = last
        ub[1, rows, :] = near
        put_columns(zs, rows, last + near)


def finish_near_kernel(rnear, rtail, onear, otail, fin, edge, v, d, ub, zs, u1):
    edge_layers(0, rnear, onear, rtail, otail, 16, fin, edge, v, d, ub, zs, u1)


def finish_near(messages, fin, edge, velocity, diffusivity):
    return pl.pallas_call(
        finish_near_kernel,
        out_shape=[jax.ShapeDtypeStruct((2, NY, NX), F32), jax.ShapeDtypeStruct((8, NY, 128), F32)],
        in_specs=[whole()] * 8,
        out_specs=[whole()] * 2,
        scratch_shapes=[pltpu.VMEM((1, NY, NX), F32)],
        compiler_params=params(16),
        name="finish_near",
    )(*messages, fin, edge, velocity, diffusivity)


def finish_kernel(rtail, rfar, rfac, ofar, ofac, fin, edge, v, d, gcp, cb, ymid, zs_near, ub, jp, gc, u1, zs):
    edge_layers(1, rfar, ofar, rfac, ofac, 0, fin, edge, v, d, ub, zs, u1)
    lane = lax.broadcasted_iota(jnp.int32, (128, 128), 1)
    hnear = jnp.concatenate([rtail[0:16, 128 * i : 128 * i + 128] for i in range(8)], axis=0)
    hfar = jnp.concatenate([rfar[2 * NY : FAR, 128 * i : 128 * i + 128] for i in range(8)], axis=0)
    hfar = dropped(at_end(), hfar)
    first_core = lax.axis_index("core") == 0
    halo_lo, halo_hi = jnp.where(first_core, hfar, hnear), jnp.where(first_core, hnear, hfar)

    def sides(i):
        a, b = paired(zs, i, 0, 32), paired(zs_near, i, 0, 32)
        return [jnp.where(first_core, a, b), ymid[i], jnp.where(first_core, b, a)]

    for b in range(4):
        rows = slice(128 * b, 128 * b + 128)
        t = halved_x(
            jnp.concatenate(
                [
                    jnp.concatenate(sides(i), axis=0)
                    for i in (2 * b, 2 * b + 1)
                ],
                axis=1,
            )
        )
        hl = pltpu.roll(halo_lo, (128 - 32 * b) % 128, 1) if b else halo_lo
        hh = pltpu.roll(halo_hi, (96 - 32 * b) % 128, 1) if b != 3 else halo_hi
        halo = jnp.where(lane < 32, hl, hh)
        g = gcp[rows, :] + cb[rows, :] * halo
        g = jnp.where(lax.axis_index("tm") == 0, 0.0, g)
        gc[rows, :] = g
        jp[8 + 128 * b : 136 + 128 * b, :] = t - g
    jp[0:8, :] = jp[CX : CX + 8, :]
    jp[CX + 8 : CX + 24, :] = jp[8:24, :]


def finish(messages, fin, edge, velocity, diffusivity, gcp, cb, ymid, zs_near):
    return pl.pallas_call(
        finish_kernel,
        out_shape=[
            jax.ShapeDtypeStruct((2, NY, NX), F32),
            jax.ShapeDtypeStruct((CX + 24, CL), F32),
            jax.ShapeDtypeStruct((CX, CL), F32),
        ],
        in_specs=[whole()] * 13,
        out_specs=[whole()] * 3,
        scratch_shapes=[pltpu.VMEM((1, NY, NX), F32), pltpu.VMEM((8, NY, 128), F32)],
        compiler_params=params(16),
        name="finish",
    )(*messages, fin, edge, velocity, diffusivity, gcp, cb, ymid, zs_near)


def spread_kernel(jp, w0, w1, w2, w3, msg, quad):
    for i in range(BLOCKS):
        msg[i] = jp[XB * i : XB * i + WIN, :]
    mine = quad_rank()
    for i, window in enumerate((w0, w1, w2, w3)):
        quad[mine ^ i] = window[...]


def spread(sources, windows):
    return pl.pallas_call(
        spread_kernel,
        out_shape=[
            jax.ShapeDtypeStruct((BLOCKS, WIN, CL), F32),
            jax.ShapeDtypeStruct((QUAD, 4, WIN, CL), F32),
        ],
        in_specs=[whole()] * 5,
        out_specs=[whole()] * 2,
        compiler_params=params(16),
        name="spread",
    )(sources, *windows)


HALO_ROWS = (32, 32, 24, 24, 24, 24, 24, 32, 32, 32, 32, 24, 24)
HALO_AT = tuple(sum(HALO_ROWS[:i]) for i in range(len(HALO_ROWS) + 1))
SHARED = ((0, 6, 96), (1, 5, 64), (2, 4, 32))


def pick_kernel(got, quad, even, odd):
    lane = lax.broadcasted_iota(jnp.int32, (24, CL), 1)
    inner = slice(4, 28)
    for parity, out in enumerate((even, odd)):
        up = lax.rem(lax.axis_index("px"), 2) == parity
        near, far = jnp.where(up, 3, 0), jnp.where(up, 2, 1)

        def put(i, value):
            out[HALO_AT[i] : HALO_AT[i + 1], :] = value

        def shared(main, other, width):
            return jnp.where(
                up,
                jnp.where(lane >= CL - width, main, pltpu.roll(other, CL - width, 1)),
                jnp.where(lane < width, main, pltpu.roll(other, width, 1)),
            )

        for j in range(4):
            put(j, got[QUAD * j + near] if HALO_ROWS[j] == WIN else got[QUAD * j + near, inner, :])
            put(7 + j, quad[near, j])
        for j, other, width in SHARED:
            put(4 + j, shared(got[QUAD * j + far, inner, :], got[QUAD * other + near, inner, :], width))
        for j in range(2):
            put(11 + j, shared(quad[far, 2 * j, inner, :], quad[far, 2 * j + 1, inner, :], 64))


def pick(got, quad):
    halo = jax.ShapeDtypeStruct((HALO_AT[-1], CL), F32)
    return pl.pallas_call(
        pick_kernel,
        out_shape=[halo, halo],
        in_specs=[whole()] * 2,
        out_specs=[whole(), whole()],
        compiler_params=params(16),
        name="pick",
    )(got, quad)


def prepare_kernel(quad, after, own):
    for q in range(QUAD):
        for i, value in enumerate(coarse_coefs(*(quad[q, j] for j in range(4)))):
            own[i, q] = value


def prepare(quad, after):
    return pl.pallas_call(
        prepare_kernel,
        out_shape=jax.ShapeDtypeStruct((6, QUAD, WIN, CL), F32),
        in_specs=[whole()] * 2,
        out_specs=whole(),
        compiler_params=params(16),
        name="prepare",
    )(quad, after)


def chain_kernel(got, own, even, odd, out, halo_cf, e):
    place = lax.axis_index("px")
    first = lax.rem(place, 2) == 0

    def block_of(ref, i):
        value = ref[HALO_AT[i] : HALO_AT[i + 1], :]
        if HALO_ROWS[i] == WIN:
            return value
        rest = jnp.zeros((4, CL), F32)
        return jnp.concatenate([rest, value, rest], axis=0)

    def below(i):
        return jnp.where(place == 0, 0.0, jnp.where(first, block_of(odd, i), block_of(even, i)))

    def above(i):
        return jnp.where(place == 3, 0.0, jnp.where(first, block_of(even, i), block_of(odd, i)))

    def source(j, block):
        if 2 <= block < 6:
            return got[QUAD * j + block - 2]
        halo = below if block < 2 else above
        if block in (0, 7):
            return halo(4 + j) if j < 3 else None
        if j < 4:
            return halo(j)
        _, other, width = SHARED[6 - j]
        return pltpu.roll(halo(10 - j), width if block == 1 else CL - width, 1)

    for block in range(8):
        halo = below if block < 2 else above
        values = []
        if block in (1, 6):
            values = [halo(7 + i) for i in range(4)]
        elif block in (0, 7):
            for i in (11, 12):
                values += [halo(i), pltpu.roll(halo(i), 64, 1)]
        if values:
            for i, value in enumerate(coarse_coefs(*values)):
                halo_cf[i, block % 4] = value
        e[0, block] = source(0, block)
    for q in range(QUAD):
        out[q] = jnp.zeros((XB, CL), F32)
    lane = lax.broadcasted_iota(jnp.int32, (WIN, CL), 1)
    for k in range(1, GROUPS):
        now, later = (k - 1) % 2, k % 2
        low = 0 if k < 3 else 1 if k < 7 else 2
        reach = range(max(0, low - 1), min(8, 9 - low))
        near = {b: lane_neighbours(e[now, b]) for b in reach}
        for block in range(low, 8 - low):
            c = e[now, block]
            cf, at = (own, block - 2) if 2 <= block < 6 else (halo_cf, block % 4)
            b, t, s, n = near[block]
            if block > 0:
                b = jnp.where(lane < 32, near[block - 1][0], b)
            if block < 7:
                t = jnp.where(lane >= 96, near[block + 1][1], t)
            w, x = pltpu.roll(c, 1, 0), pltpu.roll(c, WIN - 1, 0)
            y = c + (
                (cf[0, at] * (w - c) + cf[1, at] * (x - c))
                + (cf[2, at] * (s - c) + cf[3, at] * (n - c))
                + (cf[4, at] * (b - c) + cf[5, at] * (t - c))
            )
            if 2 <= block < 6:
                out[QUAD * k + block - 2] = y[8 : 8 + XB, :]
            if k < GROUPS - 1:
                more = source(k, block)
                e[later, block] = y if more is None else y + more


def chain(got, own, even, odd):
    return pl.pallas_call(
        chain_kernel,
        out_shape=jax.ShapeDtypeStruct((BLOCKS, XB, CL), F32),
        in_specs=[whole()] * 4,
        out_specs=whole(),
        scratch_shapes=[
            pltpu.VMEM((6, 4, WIN, CL), F32),
            pltpu.VMEM((2, 8, WIN, CL), F32),
        ],
        compiler_params=params(24),
        name="chain",
    )(got, own, even, odd)


def result_kernel(y, gc, fin, near, far, out, copied, buf, sems):
    first_core = lax.axis_index("core") == 0
    copy_y = table((256, CL), lambda r, c: r // 2 == c)
    copy_x = table((128, 256), lambda r, c: r == c // 2)
    for b in range(4):
        rows = slice(128 * b, 128 * b + 128)
        for i, part in enumerate(split3(y[rows, :] - gc[rows, :])):
            copied[i, :, rows] = dot(copy_y, part, 1, 1).astype(BF16)
    copies = []
    for zc in range(4):
        rows = slice(zc * NY, zc * NY + NY)
        for b in range(4):
            cols = slice(256 * b, 256 * b + 256)
            fine = sum(dot(copied[i, rows, 128 * b : 128 * b + 128], copy_x, 1, 0) for i in range(3))
            for z in (2 * zc, 2 * zc + 1):
                if 2 <= z < 6:
                    base = fin[z - 1, :, cols]
                else:
                    here, there = (far, near) if z < 2 else (near, far)
                    i = min(z, LZ - 1 - z)
                    base = jnp.where(first_core, here[i, :, cols], there[i, :, cols])
                buf[z, :, cols] = base + fine
        layers = slice(2 * zc, 2 * zc + 2)
        copies.append(pltpu.make_async_copy(buf.at[layers], out.at[layers], sems.at[zc]))
        copies[zc].start()
    for copy in copies:
        copy.wait()


def result(y, gc, fin, near, far):
    return pl.pallas_call(
        result_kernel,
        out_shape=jax.ShapeDtypeStruct((LZ, NY, NX), F32),
        in_specs=[whole()] * 5,
        out_specs=remains(),
        scratch_shapes=[
            pltpu.VMEM((3, 4 * NY, CX), BF16),
            pltpu.VMEM((LZ, NY, NX), F32),
            pltpu.SemaphoreType.DMA((4,)),
        ],
        compiler_params=params(16),
        name="result",
    )(y, gc, fin, near, far)


def swap(value, axes, partner):
    return lax.ppermute(value, axes, [(i, partner(i)) for i in range(lax.axis_size(axes))])


def off_chip(i):
    return (i + 1 if i % 2 else i - 1) % 16


def off_chip_copy(i):
    return (i // 16 ^ 1) * 16 + off_chip(i % 16)


def quad_beside(i):
    return (i + 1 if i % 2 else i - 1) % 4


def shards(state_old, velocity, diffusivity):
    state = state_old[0]
    ofar, ofac = edge_message(1, state, velocity, diffusivity)
    rfar = swap(ofar, SPACE, off_chip)
    rfac = swap(ofac, ("tm",) + SPACE, off_chip_copy)
    onear, otail = edge_message(0, state, velocity, diffusivity, ofac)
    rnear = swap(onear, SPACE, lambda i: i ^ 1)
    rtail = swap(otail, SPACE, lambda i: i ^ 1)
    ct = coefs(velocity, diffusivity)
    w0, w1, w2, w3 = cut(ct, rtail)
    windows = (
        w0,
        swap(w1, SPACE, lambda i: i ^ 1),
        swap(w2, ("tm",) + SPACE, lambda i: i ^ 18),
        swap(w3, ("tm",) + SPACE, lambda i: i ^ 19),
    )
    fin, edge, gcp, cb, ymid = interior(state, velocity, diffusivity, ct, windows[1])
    near, zs_near = finish_near((rnear, rtail, onear, otail), fin, edge, velocity, diffusivity)
    messages = (rtail, rfar, rfac, ofar, ofac)
    far, sources, gc = finish(messages, fin, edge, velocity, diffusivity, gcp, cb, ymid, zs_near)
    msg, quad = spread(sources, windows)
    got = lax.all_to_all(msg, GROUP, 0, 0)
    even, odd = pick(got, quad)
    own = prepare(quad, even)
    even = swap(even, "px", lambda i: i ^ 1)
    odd = swap(odd, "px", quad_beside)
    back = lax.all_to_all(chain(got, own, even, odd), GROUP, 0, 0)
    return result(back.reshape(CX, CL), gc, fin, near, far)[None]


def solution(mesh):
    fine_mesh = Mesh(mesh.devices.reshape(GROUPS, 4, 2, 2), ("tm",) + SPACE)
    return jax.shard_map(
        shards,
        mesh=fine_mesh,
        in_specs=(
            P("tm", SPACE, None, None),
            P(None, SPACE, None, None),
            P(SPACE, None, None),
        ),
        out_specs=P("tm", SPACE, None, None),
        check_vma=False,
    )
```
